512 devices in a mesh: gx: 8 (over z), gy: 16 (over x, y_lo), gz: 4 (over y_hi, core).
Axes of the slice: x: 4, y: 8 (y_hi: 2, y_lo: 4; y = y_hi * 4 + y_lo), z: 8, core: 2. Of those that a mesh axis runs over, the one named last changes fastest.
Arguments:
- density: float32 [128, 512, 1024], P('gz', 'gy', 'gx'), may hold values from -10 to 10
Outputs:
- potential: float32 [128, 512, 1024], P('gz', 'gy', 'gx')
The draws below stay inside these ranges and needn't reach their ends.
All inputs are finite; a program needn't handle non-finite values.
Results may differ from the reference program's by a relative error of at most 0.0003.
Values sent between devices are 32-bit elements; how exact they have to be, the bound alone decides.
No kernel may reach another device: no remote copies, remote signals or barrier semaphores. Data moves between devices by JAX's collectives and lax.ppermute only.
A program may use at most 64 MiB of HBM per device.

```python
import math
import jax
import jax.numpy as jnp
from jax import lax

PATCH = 32
HALO = 8
COARSEN = 4
NX = 1024
NY = 512
NZ = 128


def draw_density(key, part):
    key = jax.random.fold_in(key, 11)
    key_rough, key_factor = jax.random.split(key)
    full_shape = (NZ, NY, NX)
    factor = jnp.exp(jax.random.uniform(key_factor, full_shape, jnp.float32, -0.9, 0.9))
    return jnp.clip(jax.random.normal(key_rough, full_shape, jnp.float32), -4.0, 4.0) * factor


def setup_inputs(seed: int = 0) -> dict:
    keys = jax.random.split(jax.random.key(seed), 2)
    return {
        "density": draw_density(jax.random.fold_in(keys[1], 71), 0),
    }


screen = 6.0
soften = 0.25

def kernel_value(shift_z, shift_y, shift_x):
    squared = (shift_z * shift_z + shift_y * shift_y + shift_x * shift_x).astype(jnp.float32)
    return jax.scipy.special.erfc(jnp.sqrt(squared) / screen) / (4.0 * math.pi * jnp.sqrt(squared + soften))

def window_kernel(length):
    offset = (jnp.arange(length, dtype=jnp.int32) + length // 2) % length - length // 2
    within = (jnp.abs(offset) <= HALO).astype(jnp.float32)
    values = kernel_value(offset[:, None, None], offset[None, :, None], offset[None, None, :])
    return values * within[:, None, None] * within[None, :, None] * within[None, None, :]

def axis_terms(index_list, points):
    signed = (index_list + points // 2) % points - points // 2
    laplace = 2.0 - 2.0 * jnp.cos(2.0 * math.pi / points * index_list.astype(jnp.float32))
    wave = 2.0 * math.pi / (points * COARSEN) * signed.astype(jnp.float32)
    return (laplace, wave * wave, index_list == 0)

def multiplier(index_z, index_y, index_x, points_z, points_y, points_x):
    laplace_z, wave_z, anchor_z = axis_terms(index_z, points_z)
    laplace_y, wave_y, anchor_y = axis_terms(index_y, points_y)
    laplace_x, wave_x, anchor_x = axis_terms(index_x, points_x)
    laplace = laplace_z[:, None, None] + laplace_y[None, :, None] + laplace_x[None, None, :]
    wave_sq = wave_z[:, None, None] + wave_y[None, :, None] + wave_x[None, None, :]
    at_anchor = (anchor_z[:, None, None] & anchor_y[None, :, None] & anchor_x[None, None, :]).astype(jnp.float32)
    return (1.0 - at_anchor) * jnp.exp(-(screen * screen / 4.0) * wave_sq) / (COARSEN * (laplace + at_anchor))

def refine(coarse, axis_number):
    lower_side = jnp.roll(coarse, 1, axis_number)
    upper_side = jnp.roll(coarse, -1, axis_number)
    pieces = []
    for residue in range(COARSEN):
        offset = (residue + 0.5) / COARSEN - 0.5
        if offset < 0.0:
            pieces.append((1.0 + offset) * coarse - offset * lower_side)
        else:
            pieces.append((1.0 - offset) * coarse + offset * upper_side)
    stacked = jnp.stack(pieces, axis=axis_number + 1)
    new_shape = list(coarse.shape)
    new_shape[axis_number] = new_shape[axis_number] * COARSEN
    return stacked.reshape(new_shape)

def short_range(density):
    size_z, size_y, size_x = density.shape
    length = PATCH + 2 * HALO
    spectral_kernel = jnp.fft.rfftn(window_kernel(length))
    padded = jnp.pad(density, HALO, mode='wrap')
    count_z, count_y, count_x = (size_z // PATCH, size_y // PATCH, size_x // PATCH)

    def solve_row(flat):
        start_z = flat // count_y * PATCH
        start_y = flat % count_y * PATCH
        slab = lax.dynamic_slice(padded, (start_z, start_y, jnp.int32(0)), (length, length, size_x + 2 * HALO))
        blocks = jnp.stack([slab[:, :, column * PATCH:column * PATCH + length] for column in range(count_x)], axis=0)
        result = jnp.fft.irfftn(jnp.fft.rfftn(blocks, axes=(1, 2, 3)) * spectral_kernel, s=(length, length, length), axes=(1, 2, 3))
        inner = result[:, HALO:HALO + PATCH, HALO:HALO + PATCH, HALO:HALO + PATCH].astype(jnp.float32)
        return inner.transpose(1, 2, 0, 3).reshape(PATCH, PATCH, size_x)
    solved = lax.map(solve_row, jnp.arange(count_z * count_y, dtype=jnp.int32))
    solved = solved.reshape(count_z, count_y, PATCH, PATCH, size_x).transpose(0, 2, 1, 3, 4)
    return solved.reshape(size_z, size_y, size_x)

def reference(density):
    size_z, size_y, size_x = density.shape
    charges = density.reshape(size_z // COARSEN, COARSEN, size_y // COARSEN, COARSEN, size_x // COARSEN, COARSEN).sum(axis=(1, 3, 5))
    points_z, points_y, points_x = charges.shape
    weights = multiplier(jnp.arange(points_z, dtype=jnp.int32), jnp.arange(points_y, dtype=jnp.int32), jnp.arange(points_x, dtype=jnp.int32), points_z, points_y, points_x)
    coarse_field = jnp.real(jnp.fft.ifftn(jnp.fft.fftn(charges) * weights)).astype(jnp.float32)
    far_field = refine(refine(refine(coarse_field, 2), 1), 0)
    near_field = short_range(density)
    return far_field + near_field
```

```python
import math

import jax
import jax.numpy as jnp
import ml_dtypes
import numpy as np
from jax import lax
from jax.experimental import pallas as pl
from jax.experimental.pallas import tpu as pltpu
from jax.sharding import PartitionSpec as P

HALO = 8
COARSEN = 4
SCREEN = 6.0
SOFTEN = 0.25

NZ, NY, NX = 128, 512, 1024
GZ, GY, GX = 4, 16, 8
CZ, CY, CX = NZ // GZ, NY // GY, NX // GX
MZ, MY, MX = NZ // COARSEN, NY // COARSEN, NX // COARSEN
BZ, BY, BX = MZ // GZ, MY // GY, MX // GX
PZ, PY, PX = CZ + 2 * HALO, CY + 2 * HALO, CX + 2 * HALO
LANES = 256
GROUP = 3 * PY
BORDER_X = BX + 2

f32 = jnp.float32
bf16 = jnp.bfloat16
HIGHEST = lax.Precision.HIGHEST


def cas(a, b, points):
    angles = 2.0 * np.pi / points * (np.outer(a, b) % points)
    return np.cos(angles) + np.sin(angles)


def split(table):
    high = table.astype(np.float32).astype(ml_dtypes.bfloat16)
    low = (table - high.astype(np.float64)).astype(np.float32).astype(ml_dtypes.bfloat16)
    return high, low


def near_tables():
    reach = np.arange(HALO + 1)
    both = np.arange(-HALO, HALO + 1)
    squared = (
        reach[:, None, None] ** 2 + both[None, :, None] ** 2 + both[None, None, :] ** 2
    ).astype(np.float64)
    erfc = np.vectorize(math.erfc)
    kernel = erfc(np.sqrt(squared) / SCREEN) / (4.0 * math.pi * np.sqrt(squared + SOFTEN))
    cos_y = np.cos(2.0 * np.pi / PY * np.outer(np.arange(PY), both))
    cos_x = np.cos(2.0 * np.pi / PX * np.outer(np.arange(PX), both))
    spectral = np.einsum("dab,ka,lb->dkl", kernel, cos_y, cos_x) / (PY * PX)
    gains = np.zeros((HALO + 1, PY, LANES))
    gains[:, :, :PX] = spectral

    every_x, every_y = np.arange(PX), np.arange(PY)
    forward_x = np.zeros((PX, LANES))
    forward_x[:, :PX] = cas(every_x, every_x, PX)
    high, low = split(forward_x)
    own = slice(HALO, HALO + CX)
    ends = np.r_[0:HALO, HALO + CX : PX]
    into_x = np.zeros((512, LANES), ml_dtypes.bfloat16)
    into_x[0:128], into_x[128:256], into_x[256:384] = high[own], low[own], high[own]
    into_x[384:400], into_x[400:416], into_x[416:432] = high[ends], low[ends], high[ends]

    high, low = split(cas(every_y, every_y, PY))
    into_y = np.concatenate([high, low, high], axis=1)
    out_y = into_y[HALO : HALO + CY]

    back_x = np.zeros((LANES, CX))
    back_x[:PX] = cas(every_x, every_x[own], PX)
    high, low = split(back_x)
    out_x = np.concatenate([high, low, high], axis=0)
    return gains.astype(np.float32), into_x, into_y, out_y, out_x


def far_tables():
    every_y = cas(np.arange(MY), np.arange(MY), MY).reshape(GY, BY, GY, BY)
    first_y = np.einsum("gkbc,hi->ghkbic", every_y, np.eye(2)).reshape(GY, 2 * BY, GY * 2 * BY)

    full_x = cas(np.arange(MX), np.arange(MX), MX)
    full_z = cas(np.arange(MZ), np.arange(MZ), MZ)
    order = full_z.reshape(MZ, GZ, 2, 4).transpose(0, 3, 1, 2).reshape(MZ, MZ)
    into_z = np.kron(order, np.eye(BY))

    def waves(points):
        index = np.arange(points)
        signed = (index + points // 2) % points - points // 2
        laplace = 2.0 - 2.0 * np.cos(2.0 * np.pi / points * index)
        return laplace, (2.0 * np.pi / (points * COARSEN) * signed) ** 2

    (lap_z, wave_z), (lap_y, wave_y), (lap_x, wave_x) = waves(MZ), waves(MY), waves(MX)
    laplace = lap_z[:, None, None] + lap_y[None, :, None] + lap_x[None, None, :]
    wave = wave_z[:, None, None] + wave_y[None, :, None] + wave_x[None, None, :]
    laplace[0, 0, 0] = 1.0
    gain = np.exp(-(SCREEN * SCREEN / 4.0) * wave) / (COARSEN * laplace)
    gain[0, 0, 0] = 0.0
    gain = gain / (MZ * MY * MX)
    gain = gain.reshape(MZ, GY, BY, MX).transpose(1, 0, 2, 3).reshape(GY, MZ * BY, MX)

    out_z = np.zeros((GZ, 3, 4, BY, MZ, BY))
    for g in range(GZ):
        for plane in range(BZ + 2):
            z = (g * BZ - 1 + plane) % MZ
            for k in range(BY):
                out_z[g, plane % 3, plane // 3, k, :, k] = full_z[:, z]
    out_z = out_z.reshape(GZ, 3 * 4 * BY, MZ * BY)

    out_x = np.zeros((GX, MX, 128))
    for g in range(GX):
        out_x[g, :, :BORDER_X] = full_x[:, (g * BX - 1 + np.arange(BORDER_X)) % MX]

    def refine(coarse):
        matrix = np.zeros((COARSEN * coarse, coarse + 2))
        for fine in range(COARSEN * coarse):
            below, t = fine // COARSEN, (fine % COARSEN + 0.5) / COARSEN - 0.5
            matrix[fine, below + 1] = 1.0 - abs(t)
            matrix[fine, below if t < 0 else below + 2] = abs(t)
        return matrix

    last_y = np.zeros((GY, CY, MY))
    for g in range(GY):
        rows = (g * BY - 1 + np.arange(BY + 2)) % MY
        last_y[g] = refine(BY) @ cas(rows, np.arange(MY), MY)

    last_x = np.zeros((128, 3, CX))
    for low in range(3):
        last_x[low * BORDER_X : (low + 1) * BORDER_X, low] = refine(BX).T
    last_x = last_x.reshape(128, 3 * CX)
    tables = first_y, full_x, into_z, gain, out_z, out_x, last_y, last_x
    return tuple(table.astype(np.float32) for table in tables)


def dot(a, b):
    return jnp.dot(a, b, preferred_element_type=f32)


def exact_dot(a, b):
    return jnp.dot(a, b, preferred_element_type=f32, precision=HIGHEST)


def halves(x):
    high = x.astype(bf16)
    return high, (x - high.astype(f32)).astype(bf16)


def lane(shape):
    return lax.broadcasted_iota(jnp.int32, shape, len(shape) - 1)


def charge_kernel(density, out):
    parts = []
    for high in range(2):
        planes = []
        for low in range(4):
            z = (high * 4 + low) * COARSEN
            planes.append((density[z] + density[z + 1]) + (density[z + 2] + density[z + 3]))
        parts.append(jnp.concatenate(planes, axis=1))
    rows = jnp.concatenate(parts, axis=0)

    def pool(shape, fine, coarse):
        a = lax.broadcasted_iota(jnp.int32, shape, fine)
        b = lax.broadcasted_iota(jnp.int32, shape, coarse)
        return (a // COARSEN == b).astype(f32)

    rows = exact_dot(rows, pool((4 * CX, 128), 0, 1))
    rows = exact_dot(pool((2 * BY, 2 * CY), 1, 0), rows)
    for peer in range(GY):
        out[peer] = rows


def first_kernel(table, charges, out, held, sem):
    copy = pltpu.make_async_copy(table.at[lax.axis_index("gy")], held, sem)
    copy.start()
    rows = charges[...].reshape(GY * 2 * BY, 128)
    copy.wait()
    rows = exact_dot(held[...], rows)
    for peer in range(GX * GZ):
        out[peer] = rows


def filter_kernel(
    full_x, into_z, gain, out_z, out_x, spectrum, out, held_x, held_z, held_g, held_iz, held_ix, sems
):
    sources = (
        (full_x, held_x),
        (into_z, held_z),
        (gain.at[lax.axis_index("gy")], held_g),
        (out_z.at[lax.axis_index("gz")], held_iz),
        (out_x.at[lax.axis_index("gx")], held_ix),
    )
    copies = [
        pltpu.make_async_copy(source, held, sems.at[i]) for i, (source, held) in enumerate(sources)
    ]
    for copy in copies:
        copy.start()
    place = lane((GZ * 16, 128)) // BX
    blocks = []
    for low in range(4):
        sides = []
        for side in range(2):
            total = None
            for q in range(4):
                peer = spectrum[pl.ds((side * 4 + q) * GZ, GZ)].reshape(GZ * 16, 128)
                shift = (q - low) * BX % 128
                moved = pltpu.roll(peer, shift, 1) if shift else peer
                total = moved if q == 0 else jnp.where(place == q, moved, total)
            sides.append(total)
        blocks.append(jnp.concatenate(sides, axis=1))
    rows = jnp.concatenate(blocks, axis=0)
    copies[0].wait()
    rows = exact_dot(rows, held_x[...])
    copies[1].wait()
    rows = exact_dot(held_z[...], rows)
    copies[2].wait()
    rows = rows * held_g[...]
    copies[3].wait()
    rows = exact_dot(held_iz[...], rows)
    copies[4].wait()
    rows = exact_dot(rows, held_ix[...])
    total = rows[0:32] + pltpu.roll(rows[32:64], BORDER_X, 1) + pltpu.roll(rows[64:96], 2 * BORDER_X, 1)
    for peer in range(GY):
        out[peer] = total


def last_kernel(last_y, last_x, spectrum, near, out, held_y, held_x, sems):
    copies = [
        pltpu.make_async_copy(last_y.at[lax.axis_index("gy")], held_y, sems.at[0]),
        pltpu.make_async_copy(last_x, held_x, sems.at[1]),
    ]
    for copy in copies:
        copy.start()
    copies[0].wait()
    rows = []
    for high in range(4):
        rows.append(exact_dot(held_y[...], spectrum[:, pl.ds(high * BY, BY), :].reshape(MY, 128)))
    copies[1].wait()
    field = exact_dot(jnp.concatenate(rows, axis=0), held_x[...])

    def plane(z):
        high, low = z // 3, z % 3
        return field[high * CY : (high + 1) * CY, low * CX : (low + 1) * CX]

    for block in range(BZ):
        before, here, after = plane(block), plane(block + 1), plane(block + 2)
        for residue in range(COARSEN):
            t = (residue + 0.5) / COARSEN - 0.5
            value = (1.0 - abs(t)) * here + abs(t) * (before if t < 0 else after)
            z = block * COARSEN + residue
            out[z] = near[z] + value


def plane_rows(z, density, below, above, before, after):
    if z < HALO:
        middle = below[z]
    elif z < HALO + CZ:
        middle = density[z - HALO]
    else:
        middle = above[z - HALO - CZ]
    return jnp.concatenate([before[z], middle, after[z]], axis=0)


def edge_kernel(density, below, above, before, after, first, last):
    place = lane((GROUP, 128)) // HALO
    left = right = jnp.zeros((GROUP, 128), f32)
    for j in range(16):
        rows = jnp.concatenate(
            [plane_rows(3 * j + i, density, below, above, before, after) for i in range(3)], axis=0
        )
        shift = j * HALO
        left = jnp.where(place == j, pltpu.roll(rows, shift, 1) if shift else rows, left)
        shift = (j * HALO - (CX - HALO)) % 128
        right = jnp.where(place == j, pltpu.roll(rows, shift, 1) if shift else rows, right)
    first[...] = left
    last[...] = right


def near_kernel(
    density, below, above, before, after, left, right, gains, into_x, into_y, out_y, out_x, out, wave_x, wave_y, wave_z
):
    lanes = lane((GROUP, 128))
    for j in range(16):
        rows = jnp.concatenate(
            [plane_rows(3 * j + i, density, below, above, before, after) for i in range(3)], axis=0
        )
        ends = jnp.where(
            lanes < HALO,
            pltpu.roll(left[...], (-HALO * j) % 128, 1) if j else left[...],
            jnp.where(lanes < 2 * HALO, pltpu.roll(right[...], (HALO - HALO * j) % 128, 1), 0.0)
            if j != 1
            else jnp.where(lanes < 2 * HALO, right[...], 0.0),
        )
        high = ends.astype(bf16).astype(f32)
        low = ends - high
        ends = (high + pltpu.roll(high, 2 * HALO, 1) + pltpu.roll(low, 4 * HALO, 1)).astype(bf16)
        high, low = halves(rows)
        wave = dot(jnp.concatenate([high, high, low, ends], axis=1), into_x[...])
        for i in range(3):
            wave_x[3 * j + i] = wave[i * PY : (i + 1) * PY]

    @pl.loop(0, PZ, unroll=8)
    def _(z):
        high, low = halves(wave_x[z])
        wave_y[z] = dot(into_y[...], jnp.concatenate([high, high, low], axis=0))

    @pl.loop(0, PY // 8)
    def _(c):
        row = pl.ds(pl.multiple_of(c * 8, 8), 8)
        for side in range(LANES // 128):
            column = pl.ds(side * 128, 128)
            gain = [gains[d, row, column] for d in range(HALO + 1)]
            window = [wave_y[z, row, column] for z in range(2 * HALO)]
            for z in range(CZ):
                window.append(wave_y[z + 2 * HALO, row, column])
                total = gain[0] * window[HALO]
                for d in range(1, HALO + 1):
                    total = total + gain[d] * (window[HALO - d] + window[HALO + d])
                wave_z[z, row, column] = total
                window.pop(0)

    @pl.loop(0, CZ // 4, unroll=2)
    def _(step):
        rows = []
        for i in range(4):
            high, low = halves(wave_z[step * 4 + i])
            rows.append(dot(out_y[...], jnp.concatenate([high, high, low], axis=0)))
        high, low = halves(jnp.concatenate(rows, axis=0))
        field = dot(jnp.concatenate([high, high, low], axis=1), out_x[...])
        for i in range(4):
            out[step * 4 + i] = field[i * CY : (i + 1) * CY]


def call(kernel, outs, scratch=(), specs=None, name=None):
    vmem = pl.BlockSpec(memory_space=pltpu.VMEM)
    many = isinstance(outs, list)
    return pl.pallas_call(
        kernel,
        out_shape=[jax.ShapeDtypeStruct(s, f32) for s in outs] if many else jax.ShapeDtypeStruct(outs, f32),
        in_specs=specs,
        out_specs=[vmem] * len(outs) if many else vmem,
        scratch_shapes=list(scratch),
        compiler_params=pltpu.CompilerParams(vmem_limit_bytes=40 * 1024 * 1024),
        name=name,
    )


def both_ways(low_edge, high_edge, axis):
    peers = lax.axis_size(axis)
    up = [(i, (i + 1) % peers) for i in range(peers)]
    down = [(j, i) for i, j in up]
    return lax.ppermute(high_edge, axis, up), lax.ppermute(low_edge, axis, down)


def body(density):
    vmem, far = pl.BlockSpec(memory_space=pltpu.VMEM), pl.BlockSpec(memory_space=pl.ANY)
    dma = pltpu.SemaphoreType.DMA
    first_y, full_x, into_z, gain, out_z, out_x, last_y, last_x = (jnp.asarray(t) for t in far_tables())
    near_consts = [jnp.asarray(t) for t in near_tables()]

    charges = call(charge_kernel, (GY, 16, 128), specs=[vmem], name="charges")(density)
    charges = lax.all_to_all(charges, "gy", 0, 0, tiled=True)

    below, above = both_ways(density[:HALO], density[CZ - HALO :], "gz")

    def edge(start):
        rows = slice(start, start + HALO)
        return jnp.concatenate([below[:, rows], density[:, rows], above[:, rows]], axis=0)

    before, after = both_ways(edge(0), edge(CY - HALO), "gy")
    ends = call(edge_kernel, [(GROUP, 128)] * 2, specs=[vmem] * 5, name="edges")(
        density, below, above, before, after
    )
    left, right = both_ways(ends[0], ends[1], "gx")

    spectrum = call(
        first_kernel,
        (GX * GZ, 16, 128),
        [pltpu.VMEM((16, 256), f32), dma],
        [far, vmem],
        name="first_y",
    )(first_y, charges)
    spectrum = lax.all_to_all(spectrum, ("gx", "gz"), 0, 0, tiled=True)
    spectrum = call(
        filter_kernel,
        (GY, 32, 128),
        [
            pltpu.VMEM((MX, MX), f32),
            pltpu.VMEM((256, 256), f32),
            pltpu.VMEM((256, MX), f32),
            pltpu.VMEM((96, 256), f32),
            pltpu.VMEM((MX, 128), f32),
            dma((5,)),
        ],
        [far] * 5 + [vmem],
        name="filter",
    )(full_x, into_z, gain, out_z, out_x, spectrum)
    spectrum = lax.all_to_all(spectrum, "gy", 0, 0, tiled=True)

    near = call(
        near_kernel,
        (CZ, CY, CX),
        [
            pltpu.VMEM((PZ, PY, LANES), f32),
            pltpu.VMEM((PZ, PY, LANES), f32),
            pltpu.VMEM((CZ, PY, LANES), f32),
        ],
        [vmem] * 12,
        name="near",
    )(density, below, above, before, after, left, right, *near_consts)

    return call(
        last_kernel,
        (CZ, CY, CX),
        [pltpu.VMEM((CY, MY), f32), pltpu.VMEM((128, 3 * CX), f32), dma((2,))],
        [far, far, vmem, vmem],
        name="last",
    )(last_y, last_x, spectrum, near)


def solution(mesh):
    placed = P("gz", "gy", "gx")
    return jax.shard_map(body, mesh=mesh, in_specs=(placed,), out_specs=placed, check_vma=False)
```

```python
import math

import jax
import jax.numpy as jnp
import ml_dtypes
import numpy as np
from jax import lax
from jax.experimental import pallas as pl
from jax.experimental.pallas import tpu as pltpu
from jax.sharding import PartitionSpec as P

HALO = 8
COARSEN = 4
SCREEN = 6.0
SOFTEN = 0.25

NZ, NY, NX = 128, 512, 1024
GZ, GY, GX = 4, 16, 8
CZ, CY, CX = NZ // GZ, NY // GY, NX // GX
MZ, MY, MX = NZ // COARSEN, NY // COARSEN, NX // COARSEN
BZ, BY, BX = MZ // GZ, MY // GY, MX // GX
PZ, PY, PX = CZ + 2 * HALO, CY + 2 * HALO, CX + 2 * HALO
LANES = 256
GROUP = 3 * PY
BORDER = BY + 2
SHARE = 2 * GX
KX = MX // SHARE

f32 = jnp.float32
bf16 = jnp.bfloat16
HIGHEST = lax.Precision.HIGHEST


def cas(a, b, points):
    angles = 2.0 * np.pi / points * (np.outer(a, b) % points)
    return np.cos(angles) + np.sin(angles)


def split(table):
    high = table.astype(np.float32).astype(ml_dtypes.bfloat16)
    low = (table - high.astype(np.float64)).astype(np.float32).astype(ml_dtypes.bfloat16)
    return high, low


def near_tables():
    reach = np.arange(HALO + 1)
    both = np.arange(-HALO, HALO + 1)
    squared = (
        reach[:, None, None] ** 2 + both[None, :, None] ** 2 + both[None, None, :] ** 2
    ).astype(np.float64)
    erfc = np.vectorize(math.erfc)
    kernel = erfc(np.sqrt(squared) / SCREEN) / (4.0 * math.pi * np.sqrt(squared + SOFTEN))
    cos_y = np.cos(2.0 * np.pi / PY * np.outer(np.arange(PY), both))
    cos_x = np.cos(2.0 * np.pi / PX * np.outer(np.arange(PX), both))
    spectral = np.einsum("dab,ka,lb->dkl", kernel, cos_y, cos_x) / (PY * PX)
    gains = np.zeros((HALO + 1, PY, LANES))
    gains[:, :, :PX] = spectral

    every_x, every_y = np.arange(PX), np.arange(PY)
    forward_x = np.zeros((PX, LANES))
    forward_x[:, :PX] = cas(every_x, every_x, PX)
    high, low = split(forward_x)
    own = slice(HALO, HALO + CX)
    ends = np.r_[0:HALO, HALO + CX : PX]
    into_x = np.zeros((512, LANES), ml_dtypes.bfloat16)
    into_x[0:128], into_x[128:256], into_x[256:384] = high[own], low[own], high[own]
    into_x[384:400], into_x[400:416], into_x[416:432] = high[ends], low[ends], high[ends]

    high, low = split(cas(every_y, every_y, PY))
    into_y = np.concatenate([high, low, high], axis=1)
    out_y = into_y[HALO : HALO + CY]

    back_x = np.zeros((LANES, CX))
    back_x[:PX] = cas(every_x, every_x[own], PX)
    high, low = split(back_x)
    out_x = np.concatenate([high, low, high], axis=0)
    return gains.astype(np.float32), into_x, into_y, out_y, out_x


def far_tables():
    full_x = cas(np.arange(MX), np.arange(MX), MX)
    full_y = cas(np.arange(MY), np.arange(MY), MY)
    full_z = cas(np.arange(MZ), np.arange(MZ), MZ)

    first_x = np.tile(full_x.reshape(MX, SHARE, KX).transpose(1, 0, 2), (1, 1, 8))
    into_z = np.kron(full_z, np.eye(8))

    def waves(points):
        index = np.arange(points)
        signed = (index + points // 2) % points - points // 2
        laplace = 2.0 - 2.0 * np.cos(2.0 * np.pi / points * index)
        return laplace, (2.0 * np.pi / (points * COARSEN) * signed) ** 2

    (lap_z, wave_z), (lap_y, wave_y), (lap_x, wave_x) = waves(MZ), waves(MY), waves(MX)
    laplace = lap_z[:, None, None] + lap_y[None, :, None] + lap_x[None, None, :]
    wave = wave_z[:, None, None] + wave_y[None, :, None] + wave_x[None, None, :]
    laplace[0, 0, 0] = 1.0
    gain = np.exp(-(SCREEN * SCREEN / 4.0) * wave) / (COARSEN * laplace)
    gain[0, 0, 0] = 0.0
    gain = gain / (MZ * MY * MX)
    gain = gain.reshape(MZ, MY, SHARE, 2, 8).transpose(2, 0, 4, 3, 1).reshape(SHARE, MZ * 8, 2 * MY)

    out_z = np.zeros((2, 2 * BORDER * 8, MZ * 8))
    for g in range(2):
        z = np.concatenate([(2 * g + c) * BZ - 1 + np.arange(BORDER) for c in range(2)]) % MZ
        out_z[g] = np.kron(full_z[z], np.eye(8))

    out_y = np.zeros((GY, MY, 128))
    for g in range(GY):
        out_y[g, :, :BORDER] = full_y[:, (g * BY - 1 + np.arange(BORDER)) % MY]

    def refine(coarse):
        matrix = np.zeros((COARSEN * coarse, coarse + 2))
        for fine in range(COARSEN * coarse):
            below, t = fine // COARSEN, (fine % COARSEN + 0.5) / COARSEN - 0.5
            matrix[fine, below + 1] = 1.0 - abs(t)
            matrix[fine, below if t < 0 else below + 2] = abs(t)
        return matrix

    last_x = np.zeros((GX, MX, CX))
    for g in range(GX):
        last_x[g] = full_x[:, (g * BX - 1 + np.arange(BX + 2)) % MX] @ refine(BX).T
    last_y = np.zeros((BORDER * CY, 128))
    last_y[:, : BORDER * BORDER] = np.kron(np.eye(BORDER), refine(BY))
    tables = first_x, full_y, into_z, gain, out_z, out_y, last_x, last_y
    return tuple(table.astype(np.float32) for table in tables)


def dot(a, b):
    return jnp.dot(a, b, preferred_element_type=f32)


def exact_dot(a, b):
    return jnp.dot(a, b, preferred_element_type=f32, precision=HIGHEST)


def halves(x):
    high = x.astype(bf16)
    return high, (x - high.astype(f32)).astype(bf16)


def lane(shape):
    return lax.broadcasted_iota(jnp.int32, shape, len(shape) - 1)


def transposed_dot(a, b):
    return lax.dot_general(a, b, (((0,), (0,)), ((), ())), preferred_element_type=f32, precision=HIGHEST)


def share():
    return lax.axis_index("gx") * 2 + lax.axis_index("core")


def is_even(axis):
    return lax.rem(lax.axis_index(axis), 2) == 0


def charge_kernel(density, out, even, odd):
    parts = []
    for high in range(2):
        planes = []
        for low in range(4):
            z = (high * 4 + low) * COARSEN
            planes.append((density[z] + density[z + 1]) + (density[z + 2] + density[z + 3]))
        parts.append(jnp.concatenate(planes, axis=1))
    rows = jnp.concatenate(parts, axis=0)

    def pool(shape, fine, coarse):
        a = lax.broadcasted_iota(jnp.int32, shape, fine)
        b = lax.broadcasted_iota(jnp.int32, shape, coarse)
        return (a // COARSEN == b).astype(f32)

    rows = exact_dot(rows, pool((4 * CX, 128), 0, 1))
    rows = exact_dot(pool((2 * BY, 2 * CY), 1, 0), rows)
    for peer in range(SHARE):
        out[peer] = rows
    start = jnp.where(is_even("core"), CZ - HALO, 0)
    even[...] = density[pl.ds(start, HALO)]
    odd[...] = density[pl.ds(CZ - HALO - start, HALO)]


def first_kernel(table, charges, out, held, sem):
    copy = pltpu.make_async_copy(table.at[share()], held, sem)
    copy.start()
    peers = charges[...].reshape(GX, 32, 128)
    place = lane((32, 128)) // BX
    blocks = []
    for low in range(4):
        sides = []
        for side in range(2):
            total = None
            for q in range(4):
                shift = (q - low) * BX % 128
                peer = peers[side * 4 + q]
                moved = pltpu.roll(peer, shift, 1) if shift else peer
                total = moved if q == 0 else jnp.where(place == q, moved, total)
            sides.append(total)
        blocks.append(jnp.concatenate(sides, axis=1))
    rows = jnp.concatenate(blocks, axis=0)
    copy.wait()
    rows = exact_dot(rows, held[...])
    place = lane((BY, 128)) // KX
    for core in range(2):
        total = None
        for z in range(BZ):
            start = (z % 4) * 32 + core * 16 + (z // 4) * 8
            piece = rows[start : start + 8]
            total = piece if z == 0 else jnp.where(place == z, piece, total)
        for peer in range(2 * GY):
            out[peer, core] = total


def filter_kernel(
    full_y, into_z, gain, out_z, out_y, spectrum, out, held_y, held_z, held_g, held_iz, held_iy, sems
):
    sources = (
        (full_y, held_y),
        (into_z, held_z),
        (gain.at[share()], held_g),
        (out_z.at[lax.axis_index("yh")], held_iz),
        (out_y.at[lax.axis_index("gy")], held_iy),
    )
    copies = [
        pltpu.make_async_copy(source, held, sems.at[i]) for i, (source, held) in enumerate(sources)
    ]
    for copy in copies:
        copy.start()
    blocks = spectrum[...].reshape(GY, 4, BY, 128)
    copies[0].wait()
    waves = [transposed_dot(blocks[:, b].reshape(MY, 128), held_y[...]) for b in range(4)]
    rows = jnp.concatenate(waves, axis=0).reshape(MZ, 2, 8, MY)
    rows = jnp.concatenate([rows[:, half].reshape(MZ * 8, MY) for half in range(2)], axis=1)
    copies[1].wait()
    rows = exact_dot(held_z[...], rows)
    copies[2].wait()
    rows = rows * held_g[...]
    copies[3].wait()
    rows = exact_dot(held_iz[...], rows)
    copies[4].wait()
    rows = jnp.concatenate([rows[:, :MY], rows[:, MY:]], axis=0)
    rows = exact_dot(rows, held_iy[...])
    for core in range(2):
        sides = []
        for half in range(2):
            total = None
            for z in range(BORDER):
                start = ((half * 2 + core) * BORDER + z) * 8
                piece = rows[start : start + 8]
                total = piece if z == 0 else total + pltpu.roll(piece, z * BORDER, 1)
            sides.append(total)
        message = jnp.concatenate(sides, axis=0)
        for peer in range(GX):
            out[peer * 2 + core] = message


def last_kernel(last_x, last_y, spectrum, near, out, held_x, held_y, sems):
    copies = [
        pltpu.make_async_copy(last_x.at[lax.axis_index("gx")], held_x, sems.at[0]),
        pltpu.make_async_copy(last_y, held_y, sems.at[1]),
    ]
    for copy in copies:
        copy.start()
    rows = spectrum[...].reshape(MX, 128)
    copies[0].wait()
    field = transposed_dot(rows, held_x[...])
    copies[1].wait()
    field = exact_dot(held_y[...], field)

    def plane(z):
        return field[z * CY : (z + 1) * CY]

    for block in range(BZ):
        before, here, after = plane(block), plane(block + 1), plane(block + 2)
        for residue in range(COARSEN):
            t = (residue + 0.5) / COARSEN - 0.5
            value = (1.0 - abs(t)) * here + abs(t) * (before if t < 0 else after)
            z = block * COARSEN + residue
            out[z] = near[z] + value


def edge_y_kernel(density, z_even, z_odd, even, odd):
    lower = is_even("core")
    start = jnp.where(is_even("gy"), CY - HALO, 0)
    for target, first in ((even, start), (odd, CY - HALO - start)):
        rows = pl.ds(pl.multiple_of(first, 8), HALO)
        one, two = z_even[:, rows], z_odd[:, rows]
        target[0:HALO] = jnp.where(lower, two, one)
        target[HALO : HALO + CZ] = density[:, rows]
        target[HALO + CZ : PZ] = jnp.where(lower, one, two)


def edge_x_kernel(density, z_even, z_odd, y_even, y_odd, padded, even, odd):
    lower = is_even("core")
    one, two = z_even[...], z_odd[...]
    middle = slice(HALO, HALO + CY)
    padded[0:HALO, middle] = jnp.where(lower, two, one)
    padded[HALO : HALO + CZ, middle] = density[...]
    padded[HALO + CZ : PZ, middle] = jnp.where(lower, one, two)
    lower = is_even("gy")
    one, two = y_even[...], y_odd[...]
    padded[:, 0:HALO] = jnp.where(lower, two, one)
    padded[:, HALO + CY : PY] = jnp.where(lower, one, two)

    place = lane((GROUP, 128)) // HALO
    left = right = jnp.zeros((GROUP, 128), f32)
    for j in range(16):
        rows = padded[3 * j : 3 * j + 3].reshape(GROUP, 128)
        shift = j * HALO
        left = jnp.where(place == j, pltpu.roll(rows, shift, 1) if shift else rows, left)
        shift = (j * HALO - (CX - HALO)) % 128
        right = jnp.where(place == j, pltpu.roll(rows, shift, 1) if shift else rows, right)
    lower = is_even("gx")
    even[...] = jnp.where(lower, right, left)
    odd[...] = jnp.where(lower, left, right)


def near_kernel(
    padded, x_even, x_odd, gains, into_x, into_y, out_y, out_x, out, wave_x, wave_y, wave_z
):
    lanes = lane((GROUP, 128))
    lower = is_even("gx")
    one, two = x_even[...], x_odd[...]
    left, right = jnp.where(lower, two, one), jnp.where(lower, one, two)
    for j in range(16):
        rows = padded[3 * j : 3 * j + 3].reshape(GROUP, 128)
        to_left, to_right = (-HALO * j) % 128, (HALO - HALO * j) % 128
        ends = jnp.where(
            lanes < HALO,
            pltpu.roll(left, to_left, 1) if to_left else left,
            pltpu.roll(right, to_right, 1) if to_right else right,
        )
        ends = jnp.where(lanes < 2 * HALO, ends, 0.0)
        high = ends.astype(bf16).astype(f32)
        low = ends - high
        ends = (high + pltpu.roll(high, 2 * HALO, 1) + pltpu.roll(low, 4 * HALO, 1)).astype(bf16)
        high, low = halves(rows)
        wave = dot(jnp.concatenate([high, high, low, ends], axis=1), into_x[...])
        for i in range(3):
            wave_x[3 * j + i] = wave[i * PY : (i + 1) * PY]

    @pl.loop(0, PZ, unroll=8)
    def _(z):
        high, low = halves(wave_x[z])
        wave_y[z] = dot(into_y[...], jnp.concatenate([high, high, low], axis=0))

    @pl.loop(0, PY // 8)
    def _(c):
        row = pl.ds(pl.multiple_of(c * 8, 8), 8)
        for side in range(LANES // 128):
            column = pl.ds(side * 128, 128)
            gain = [gains[d, row, column] for d in range(HALO + 1)]
            window = [wave_y[z, row, column] for z in range(2 * HALO)]
            for z in range(CZ):
                window.append(wave_y[z + 2 * HALO, row, column])
                total = gain[0] * window[HALO]
                for d in range(1, HALO + 1):
                    total = total + gain[d] * (window[HALO - d] + window[HALO + d])
                wave_z[z, row, column] = total
                window.pop(0)

    @pl.loop(0, CZ // 4, unroll=2)
    def _(step):
        rows = []
        for i in range(4):
            high, low = halves(wave_z[step * 4 + i])
            rows.append(dot(out_y[...], jnp.concatenate([high, high, low], axis=0)))
        high, low = halves(jnp.concatenate(rows, axis=0))
        field = dot(jnp.concatenate([high, high, low], axis=1), out_x[...])
        for i in range(4):
            out[step * 4 + i] = field[i * CY : (i + 1) * CY]


def call(kernel, outs, scratch=(), specs=None, name=None):
    vmem = pl.BlockSpec(memory_space=pltpu.VMEM)
    many = isinstance(outs, list)
    return pl.pallas_call(
        kernel,
        out_shape=[jax.ShapeDtypeStruct(s, f32) for s in outs] if many else jax.ShapeDtypeStruct(outs, f32),
        in_specs=specs,
        out_specs=[vmem] * len(outs) if many else vmem,
        scratch_shapes=list(scratch),
        compiler_params=pltpu.CompilerParams(vmem_limit_bytes=40 * 1024 * 1024),
        name=name,
    )


def exchange(even, odd, axis):
    peers = lax.axis_size(axis)
    low_first = [(i, i + 1 if i % 2 == 0 else i - 1) for i in range(peers)]
    high_first = [(i, (i + 1 if i % 2 else i - 1) % peers) for i in range(peers)]
    odd = lax.ppermute(odd, axis, high_first)
    return lax.ppermute(even, axis, low_first), odd


def body(density):
    vmem, far = pl.BlockSpec(memory_space=pltpu.VMEM), pl.BlockSpec(memory_space=pltpu.HBM)
    dma = pltpu.SemaphoreType.DMA
    first_x, full_y, into_z, gain, out_z, out_y, last_x, last_y = (jnp.asarray(t) for t in far_tables())
    near_consts = [jnp.asarray(t) for t in near_tables()]

    charges, even, odd = call(
        charge_kernel, [(SHARE, 16, 128), (HALO, CY, CX), (HALO, CY, CX)], specs=[vmem], name="charges"
    )(density)
    charges = lax.all_to_all(charges, ("gx", "core"), 0, 0, tiled=True)
    z_ends = exchange(even, odd, ("yh", "core"))
    spectrum = call(
        first_kernel,
        (2 * GY, 2, 8, 128),
        [pltpu.VMEM((MX, 128), f32), dma],
        [far, vmem],
        name="first_x",
    )(first_x, charges)
    spectrum = lax.all_to_all(spectrum, ("gy", "yh"), 0, 0, tiled=True)

    y_ends = call(edge_y_kernel, [(PZ, HALO, CX)] * 2, specs=[vmem] * 3, name="edges_y")(density, *z_ends)
    y_ends = exchange(*y_ends, "gy")
    padded, even, odd = call(
        edge_x_kernel, [(PZ, PY, CX), (GROUP, 128), (GROUP, 128)], specs=[vmem] * 5, name="edges_x"
    )(density, *z_ends, *y_ends)
    x_ends = exchange(even, odd, "gx")

    spectrum, x_ends = lax.optimization_barrier((spectrum, x_ends))
    spectrum = call(
        filter_kernel,
        (SHARE, KX, 128),
        [
            pltpu.VMEM((MY, MY), f32),
            pltpu.VMEM((256, 256), f32),
            pltpu.VMEM((256, 256), f32),
            pltpu.VMEM((2 * BORDER * 8, 256), f32),
            pltpu.VMEM((MY, 128), f32),
            dma((5,)),
        ],
        [far] * 5 + [vmem],
        name="filter",
    )(full_y, into_z, gain, out_z, out_y, spectrum)
    spectrum = lax.all_to_all(spectrum, ("gx", "core"), 0, 0, tiled=True)

    near = call(
        near_kernel,
        (CZ, CY, CX),
        [
            pltpu.VMEM((PZ, PY, LANES), f32),
            pltpu.VMEM((PZ, PY, LANES), f32),
            pltpu.VMEM((CZ, PY, LANES), f32),
        ],
        [vmem] * 8,
        name="near",
    )(padded, *x_ends, *near_consts)

    return call(
        last_kernel,
        (CZ, CY, CX),
        [pltpu.VMEM((MX, CX), f32), pltpu.VMEM((BORDER * CY, 128), f32), dma((2,))],
        [far, far, vmem, vmem],
        name="last",
    )(last_x, last_y, spectrum, near)


def solution(mesh):
    devices = mesh.devices.reshape(GX, GY, 2, 2)
    parts = jax.sharding.Mesh(devices, ("gx", "gy", "yh", "core"))
    placed = P(("yh", "core"), "gy", "gx")
    return jax.shard_map(body, mesh=parts, in_specs=(placed,), out_specs=placed, check_vma=False)
```

```python
import math

import jax
import jax.numpy as jnp
import ml_dtypes
import numpy as np
from jax import lax
from jax.experimental import pallas as pl
from jax.experimental.pallas import tpu as pltpu
from jax.sharding import PartitionSpec as P

HALO = 8
COARSEN = 4
SCREEN = 6.0
SOFTEN = 0.25

NZ, NY, NX = 128, 512, 1024
GZ, GY, GX = 4, 16, 8
CZ, CY, CX = NZ // GZ, NY // GY, NX // GX
MZ, MY, MX = NZ // COARSEN, NY // COARSEN, NX // COARSEN
BZ, BY, BX = MZ // GZ, MY // GY, MX // GX
PZ, PY, PX = CZ + 2 * HALO, CY + 2 * HALO, CX + 2 * HALO
LANES = 256
GROUP = 3 * PY
BORDER = BY + 2
SHARE = 2 * GX
KX = MX // SHARE
VMEM_MIB = 44
TABLE_ROWS = 24 * 2048

f32 = jnp.float32
bf16 = jnp.bfloat16
HIGHEST = lax.Precision.HIGHEST


def cas(a, b, points):
    angles = 2.0 * np.pi / points * (np.outer(a, b) % points)
    return np.cos(angles) + np.sin(angles)


def split(table):
    high = table.astype(np.float32).astype(ml_dtypes.bfloat16)
    low = (table - high.astype(np.float64)).astype(np.float32).astype(ml_dtypes.bfloat16)
    return high, low


def near_tables():
    reach = np.arange(HALO + 1)
    both = np.arange(-HALO, HALO + 1)
    squared = (
        reach[:, None, None] ** 2 + both[None, :, None] ** 2 + both[None, None, :] ** 2
    ).astype(np.float64)
    erfc = np.vectorize(math.erfc)
    kernel = erfc(np.sqrt(squared) / SCREEN) / (4.0 * math.pi * np.sqrt(squared + SOFTEN))
    cos_y = np.cos(2.0 * np.pi / PY * np.outer(np.arange(PY), both))
    cos_x = np.cos(2.0 * np.pi / PX * np.outer(np.arange(PX), both))
    spectral = np.einsum("dab,ka,lb->dkl", kernel, cos_y, cos_x) / (PY * PX)
    gains = np.zeros(((HALO + 1) * PY, LANES))
    gains[:, :PX] = spectral.reshape(-1, PX)

    every_x, every_y = np.arange(PX), np.arange(PY)
    forward_x = np.zeros((PX, LANES))
    forward_x[:, :PX] = cas(every_x, every_x, PX)
    high, low = split(forward_x)
    own = slice(HALO, HALO + CX)
    ends = np.r_[0:HALO, HALO + CX : PX]
    into_x = np.zeros((512, LANES))
    into_x[0:128], into_x[128:256], into_x[256:384] = high[own], low[own], high[own]
    into_x[384:400], into_x[400:416], into_x[416:432] = high[ends], low[ends], high[ends]

    high, low = split(cas(every_y, every_y, PY))
    into_y = np.zeros((PY, LANES))
    into_y[:, : 3 * PY] = np.concatenate([high, low, high], axis=1)

    back_x = np.zeros((LANES, CX))
    back_x[:PX] = cas(every_x, every_x[own], PX)
    high, low = split(back_x)
    out_x = np.concatenate([high, low, high], axis=0)
    return {"gains": gains, "into_x": into_x, "into_y": into_y, "out_x": out_x}


def far_tables():
    full_x = cas(np.arange(MX), np.arange(MX), MX)
    full_y = cas(np.arange(MY), np.arange(MY), MY)
    full_z = cas(np.arange(MZ), np.arange(MZ), MZ)

    first_x = np.tile(full_x.reshape(MX, SHARE, KX).transpose(1, 0, 2), (1, 1, 8))
    into_z = np.kron(full_z, np.eye(8))

    def waves(points):
        index = np.arange(points)
        signed = (index + points // 2) % points - points // 2
        laplace = 2.0 - 2.0 * np.cos(2.0 * np.pi / points * index)
        return laplace, (2.0 * np.pi / (points * COARSEN) * signed) ** 2

    (lap_z, wave_z), (lap_y, wave_y), (lap_x, wave_x) = waves(MZ), waves(MY), waves(MX)
    laplace = lap_z[:, None, None] + lap_y[None, :, None] + lap_x[None, None, :]
    wave = wave_z[:, None, None] + wave_y[None, :, None] + wave_x[None, None, :]
    laplace[0, 0, 0] = 1.0
    gain = np.exp(-(SCREEN * SCREEN / 4.0) * wave) / (COARSEN * laplace)
    gain[0, 0, 0] = 0.0
    gain = gain / (MZ * MY * MX)
    gain = gain.reshape(MZ, MY, SHARE, 2, 8).transpose(2, 0, 4, 3, 1).reshape(SHARE, MZ * 8, 2 * MY)

    out_z = np.zeros((2, 2 * BORDER * 8, MZ * 8))
    for g in range(2):
        z = np.concatenate([(2 * g + c) * BZ - 1 + np.arange(BORDER) for c in range(2)]) % MZ
        out_z[g] = np.kron(full_z[z], np.eye(8))

    out_y = np.zeros((GY, MY, 128))
    for g in range(GY):
        out_y[g, :, :BORDER] = full_y[:, (g * BY - 1 + np.arange(BORDER)) % MY]

    def refine(coarse):
        matrix = np.zeros((COARSEN * coarse, coarse + 2))
        for fine in range(COARSEN * coarse):
            below, t = fine // COARSEN, (fine % COARSEN + 0.5) / COARSEN - 0.5
            matrix[fine, below + 1] = 1.0 - abs(t)
            matrix[fine, below if t < 0 else below + 2] = abs(t)
        return matrix

    last_x = np.zeros((GX, MX, CX))
    for g in range(GX):
        last_x[g] = full_x[:, (g * BX - 1 + np.arange(BX + 2)) % MX] @ refine(BX).T
    last_y = np.zeros((BORDER * CY, 128))
    last_y[:, : BORDER * BORDER] = np.kron(np.eye(BORDER), refine(BY))
    return {
        "first_x": first_x,
        "full_y": full_y,
        "into_z": into_z,
        "gain": gain,
        "out_z": out_z,
        "out_y": out_y,
        "last_x": last_x,
        "last_y": last_y,
    }


class Tables:
    def __init__(self):
        self.place, rows, pieces = {}, 0, []
        for name, table in (near_tables() | far_tables()).items():
            count, lanes = table.shape[-2:]
            halves = lanes // 128
            flat = table.reshape(-1, count, halves, 128).swapaxes(1, 2).reshape(-1, 128)
            self.place[name] = rows, count, halves
            rows += flat.shape[0]
            pieces.append(flat)
        self.array = np.zeros((TABLE_ROWS, 128), np.float32)
        self.array[:rows] = np.concatenate(pieces)

    def shape(self, name):
        _, count, halves = self.place[name]
        return pltpu.VMEM((halves, count, 128), f32)

    def copies(self, ref, held, sems, index):
        made = []
        for i, (name, target) in enumerate(held.items()):
            first, count, halves = self.place[name]
            rows = halves * count
            start = first + index.get(name, 0) * rows
            if name in index:
                start = pl.multiple_of(start, 8)
            for half in range(halves):
                source = ref.at[pl.ds(start + half * count, count)]
                made.append(pltpu.make_async_copy(source, target.at[half], sems.at[i]))
        for copy in made:
            copy.start()
        pairs, at = {}, 0
        for name in held:
            halves = self.place[name][2]
            pairs[name] = made[at : at + halves]
            at += halves

        def wait(name):
            for copy in pairs[name]:
                copy.wait()
            target = held[name]
            if len(pairs[name]) == 1:
                return target[0]
            return jnp.concatenate([target[0], target[1]], axis=1)

        return wait


TABLES = Tables()


def dot(a, b):
    return jnp.dot(a, b, preferred_element_type=f32)


def exact_dot(a, b):
    return jnp.dot(a, b, preferred_element_type=f32, precision=HIGHEST)


def halves(x):
    high = x.astype(bf16)
    return high, (x - high.astype(f32)).astype(bf16)


def lane(shape):
    return lax.broadcasted_iota(jnp.int32, shape, len(shape) - 1)


def transposed_dot(a, b):
    return lax.dot_general(a, b, (((0,), (0,)), ((), ())), preferred_element_type=f32, precision=HIGHEST)


def share():
    return lax.axis_index("gx") * 2 + lax.axis_index("core")


def is_even(axis):
    return lax.rem(lax.axis_index(axis), 2) == 0


def charge_kernel(density, out, even, odd):
    parts = []
    for high in range(2):
        planes = []
        for low in range(4):
            z = (high * 4 + low) * COARSEN
            planes.append((density[z] + density[z + 1]) + (density[z + 2] + density[z + 3]))
        parts.append(jnp.concatenate(planes, axis=1))
    rows = jnp.concatenate(parts, axis=0)

    def pool(shape, fine, coarse):
        a = lax.broadcasted_iota(jnp.int32, shape, fine)
        b = lax.broadcasted_iota(jnp.int32, shape, coarse)
        return (a // COARSEN == b).astype(f32)

    rows = exact_dot(rows, pool((4 * CX, 128), 0, 1))
    rows = exact_dot(pool((2 * BY, 2 * CY), 1, 0), rows)
    for peer in range(SHARE):
        out[peer] = rows
    start = jnp.where(is_even("core"), CZ - HALO, 0)
    even[...] = density[pl.ds(start, HALO)]
    odd[...] = density[pl.ds(CZ - HALO - start, HALO)]


def first_kernel(table, charges, out, held, sems):
    wait = TABLES.copies(table, {"first_x": held}, sems, {"first_x": share()})
    peers = charges[...].reshape(GX, 32, 128)
    place = lane((32, 128)) // BX
    blocks = []
    for low in range(4):
        sides = []
        for side in range(2):
            total = None
            for q in range(4):
                shift = (q - low) * BX % 128
                peer = peers[side * 4 + q]
                moved = pltpu.roll(peer, shift, 1) if shift else peer
                total = moved if q == 0 else jnp.where(place == q, moved, total)
            sides.append(total)
        blocks.append(jnp.concatenate(sides, axis=1))
    rows = jnp.concatenate(blocks, axis=0)
    rows = exact_dot(rows, wait("first_x"))
    place = lane((BY, 128)) // KX
    for core in range(2):
        total = None
        for z in range(BZ):
            start = (z % 4) * 32 + core * 16 + (z // 4) * 8
            piece = rows[start : start + 8]
            total = piece if z == 0 else jnp.where(place == z, piece, total)
        for peer in range(2 * GY):
            out[peer, core] = total


def filter_kernel(table, spectrum, out, held_y, held_z, held_g, held_iz, held_iy, sems):
    held = {"full_y": held_y, "into_z": held_z, "gain": held_g, "out_z": held_iz, "out_y": held_iy}
    index = {"gain": share(), "out_z": lax.axis_index("yh"), "out_y": lax.axis_index("gy")}
    wait = TABLES.copies(table, held, sems, index)
    blocks = spectrum[...].reshape(GY, 4, BY, 128)
    full_y = wait("full_y")
    waves = [transposed_dot(blocks[:, b].reshape(MY, 128), full_y) for b in range(4)]
    rows = jnp.concatenate(waves, axis=0).reshape(MZ, 2, 8, MY)
    rows = jnp.concatenate([rows[:, half].reshape(MZ * 8, MY) for half in range(2)], axis=1)
    rows = exact_dot(wait("into_z"), rows)
    rows = rows * wait("gain")
    rows = exact_dot(wait("out_z"), rows)
    rows = jnp.concatenate([rows[:, :MY], rows[:, MY:]], axis=0)
    rows = exact_dot(rows, wait("out_y"))
    for core in range(2):
        sides = []
        for half in range(2):
            total = None
            for z in range(BORDER):
                start = ((half * 2 + core) * BORDER + z) * 8
                piece = rows[start : start + 8]
                total = piece if z == 0 else total + pltpu.roll(piece, z * BORDER, 1)
            sides.append(total)
        message = jnp.concatenate(sides, axis=0)
        for peer in range(GX):
            out[peer * 2 + core] = message


def last_kernel(table, spectrum, near, out, held_x, held_y, sems):
    held = {"last_x": held_x, "last_y": held_y}
    wait = TABLES.copies(table, held, sems, {"last_x": lax.axis_index("gx")})
    rows = spectrum[...].reshape(MX, 128)
    field = transposed_dot(rows, wait("last_x"))
    field = exact_dot(wait("last_y"), field)

    def plane(z):
        return field[z * CY : (z + 1) * CY]

    for block in range(BZ):
        before, here, after = plane(block), plane(block + 1), plane(block + 2)
        for residue in range(COARSEN):
            t = (residue + 0.5) / COARSEN - 0.5
            value = (1.0 - abs(t)) * here + abs(t) * (before if t < 0 else after)
            z = block * COARSEN + residue
            out[z] = near[z] + value


def edge_y_kernel(density, z_even, z_odd, even, odd):
    lower = is_even("core")
    start = jnp.where(is_even("gy"), CY - HALO, 0)
    for target, first in ((even, start), (odd, CY - HALO - start)):
        rows = pl.ds(pl.multiple_of(first, 8), HALO)
        one, two = z_even[:, rows], z_odd[:, rows]
        target[0:HALO] = jnp.where(lower, two, one)
        target[HALO : HALO + CZ] = density[:, rows]
        target[HALO + CZ : PZ] = jnp.where(lower, one, two)


def edge_x_kernel(table, density, z_even, z_odd, y_even, y_odd, waves, even, odd, padded, held, sems):
    wait = TABLES.copies(table, {"into_y": held}, sems, {})
    lower = is_even("core")
    one, two = z_even[...], z_odd[...]
    middle = slice(HALO, HALO + CY)
    padded[0:HALO, middle] = jnp.where(lower, two, one)
    padded[HALO : HALO + CZ, middle] = density[...]
    padded[HALO + CZ : PZ, middle] = jnp.where(lower, one, two)
    lower = is_even("gy")
    one, two = y_even[...], y_odd[...]
    padded[:, 0:HALO] = jnp.where(lower, two, one)
    padded[:, HALO + CY : PY] = jnp.where(lower, one, two)

    into_y = wait("into_y")[:, : 3 * PY].astype(bf16)
    place = lane((GROUP, 128)) // HALO
    left = right = jnp.zeros((GROUP, 128), f32)
    for j in range(8):
        rows = []
        for pair in range(3):
            z = 6 * j + 2 * pair
            high, low = halves(jnp.concatenate([padded[z], padded[z + 1]], axis=1))
            wave = dot(into_y, jnp.concatenate([high, high, low], axis=0))
            waves[z], waves[z + 1] = wave[:, :128], wave[:, 128:]
            rows += [wave[:, :128], wave[:, 128:]]
        for i in range(2):
            group = jnp.concatenate(rows[3 * i : 3 * i + 3], axis=0)
            shift = (2 * j + i) * HALO
            left = jnp.where(place == 2 * j + i, pltpu.roll(group, shift, 1) if shift else group, left)
            shift = (shift - (CX - HALO)) % 128
            right = jnp.where(place == 2 * j + i, pltpu.roll(group, shift, 1) if shift else group, right)
    lower = is_even("gx")
    even[...] = jnp.where(lower, right, left)
    odd[...] = jnp.where(lower, left, right)


def near_kernel(
    table, waves, x_even, x_odd, out, wave_x, wave_z, held_g, held_ix, held_y, held_ox, sems
):
    held = {"into_x": held_ix, "gains": held_g, "into_y": held_y, "out_x": held_ox}
    wait = TABLES.copies(table, held, sems, {})
    lanes = lane((GROUP, 128))
    lower = is_even("gx")
    one, two = x_even[...], x_odd[...]
    left, right = jnp.where(lower, two, one), jnp.where(lower, one, two)
    into_x = wait("into_x").astype(bf16)
    for j in range(16):
        rows = waves[3 * j : 3 * j + 3].reshape(GROUP, 128)
        to_left, to_right = (-HALO * j) % 128, (HALO - HALO * j) % 128
        ends = jnp.where(
            lanes < HALO,
            pltpu.roll(left, to_left, 1) if to_left else left,
            pltpu.roll(right, to_right, 1) if to_right else right,
        )
        ends = jnp.where(lanes < 2 * HALO, ends, 0.0)
        high = ends.astype(bf16).astype(f32)
        low = ends - high
        ends = (high + pltpu.roll(high, 2 * HALO, 1) + pltpu.roll(low, 4 * HALO, 1)).astype(bf16)
        high, low = halves(rows)
        wave = dot(jnp.concatenate([high, high, low, ends], axis=1), into_x)
        for i in range(3):
            wave_x[3 * j + i] = wave[i * PY : (i + 1) * PY]

    wait("gains")

    @pl.loop(0, PY // 8)
    def _(c):
        for side in range(LANES // 128):
            gain = [
                held_g[side, pl.ds(pl.multiple_of(d * PY + c * 8, 8), 8)] for d in range(HALO + 1)
            ]
            row, column = pl.ds(pl.multiple_of(c * 8, 8), 8), pl.ds(side * 128, 128)
            window = [wave_x[z, row, column] for z in range(2 * HALO)]
            for z in range(CZ):
                window.append(wave_x[z + 2 * HALO, row, column])
                total = gain[0] * window[HALO]
                for d in range(1, HALO + 1):
                    total = total + gain[d] * (window[HALO - d] + window[HALO + d])
                wave_z[z, row, column] = total
                window.pop(0)

    out_y = wait("into_y")[HALO : HALO + CY, : 3 * PY].astype(bf16)
    out_x = wait("out_x").astype(bf16)

    for step in range(CZ // 4):
        rows = []
        for i in range(4):
            high, low = halves(wave_z[step * 4 + i])
            rows.append(dot(out_y, jnp.concatenate([high, high, low], axis=0)))
        high, low = halves(jnp.concatenate(rows, axis=0))
        field = dot(jnp.concatenate([high, high, low], axis=1), out_x)
        for i in range(4):
            out[step * 4 + i] = field[i * CY : (i + 1) * CY]


def call(kernel, outs, arrays=0, tables=(), scratch=(), us=1.0):
    vmem = pl.BlockSpec(memory_space=pltpu.VMEM)
    many = isinstance(outs, list)
    specs = [vmem] * arrays
    scratch = list(scratch)
    if tables:
        specs = [pl.BlockSpec(memory_space=pltpu.HBM)] + specs
        scratch += [TABLES.shape(name) for name in tables]
        scratch.append(pltpu.SemaphoreType.DMA((len(tables),)))
    return pl.pallas_call(
        kernel,
        out_shape=[jax.ShapeDtypeStruct(s, f32) for s in outs] if many else jax.ShapeDtypeStruct(outs, f32),
        in_specs=specs,
        out_specs=[vmem] * len(outs) if many else vmem,
        scratch_shapes=scratch,
        compiler_params=pltpu.CompilerParams(vmem_limit_bytes=VMEM_MIB * 1024 * 1024),
        cost_estimate=pl.CostEstimate(flops=int(us * 1e9), bytes_accessed=int(us * 3e6), transcendentals=0),
        name=kernel.__name__,
    )


def exchange(even, odd, axis):
    peers = lax.axis_size(axis)
    low_first = [(i, i + 1 if i % 2 == 0 else i - 1) for i in range(peers)]
    high_first = [(i, (i + 1 if i % 2 else i - 1) % peers) for i in range(peers)]
    odd = lax.ppermute(odd, axis, high_first)
    return lax.ppermute(even, axis, low_first), odd


def body(density):
    table = jnp.asarray(TABLES.array)
    charges, even, odd = call(charge_kernel, [(SHARE, 16, 128), (HALO, CY, CX), (HALO, CY, CX)], 1, us=0.5)(density)
    charges = lax.all_to_all(charges, ("gx", "core"), 0, 0, tiled=True)
    z_ends = exchange(even, odd, ("yh", "core"))
    charges, z_ends = lax.optimization_barrier((charges, z_ends))
    spectrum = call(first_kernel, (2 * GY, 2, 8, 128), 1, ["first_x"], us=1.3)(table, charges)
    spectrum = lax.all_to_all(spectrum, ("gy", "yh"), 0, 0, tiled=True)

    y_ends = call(edge_y_kernel, [(PZ, HALO, CX)] * 2, 3, us=0.2)(density, *z_ends)
    spectrum, _ = lax.optimization_barrier((spectrum, y_ends))
    y_ends = exchange(*y_ends, "gy")
    spectrum = call(filter_kernel, (SHARE, KX, 128), 1, ["full_y", "into_z", "gain", "out_z", "out_y"], us=3.0)(
        table, spectrum
    )
    y_ends, _ = lax.optimization_barrier((y_ends, spectrum))
    spectrum = lax.all_to_all(spectrum, ("gx", "core"), 0, 0, tiled=True)
    waves, even, odd = call(
        edge_x_kernel,
        [(PZ, PY, CX), (GROUP, 128), (GROUP, 128)],
        5,
        ["into_y"],
        [pltpu.VMEM((PZ, PY, CX), f32)],
        us=2.0,
    )(table, density, *z_ends, *y_ends)
    x_ends = exchange(even, odd, "gx")
    near = call(
        near_kernel,
        (CZ, CY, CX),
        3,
        ["gains", "into_x", "into_y", "out_x"],
        [pltpu.VMEM((PZ, PY, LANES), f32), pltpu.VMEM((CZ, PY, LANES), f32)],
        us=6.0,
    )(table, waves, *x_ends)
    return call(last_kernel, (CZ, CY, CX), 2, ["last_x", "last_y"], us=1.8)(table, spectrum, near)


def solution(mesh):
    devices = mesh.devices.reshape(GX, GY, 2, 2)
    parts = jax.sharding.Mesh(devices, ("gx", "gy", "yh", "core"))
    placed = P(("yh", "core"), "gy", "gx")
    return jax.shard_map(body, mesh=parts, in_specs=(placed,), out_specs=placed, check_vma=False)
```

```python
import math

import jax
import jax.numpy as jnp
import ml_dtypes
import numpy as np
from jax import lax
from jax.experimental import pallas as pl
from jax.experimental.pallas import tpu as pltpu
from jax.sharding import PartitionSpec as P

HALO = 8
COARSEN = 4
SCREEN = 6.0
SOFTEN = 0.25

NZ, NY, NX = 128, 512, 1024
GZ, GY, GX = 4, 16, 8
CZ, CY, CX = NZ // GZ, NY // GY, NX // GX
MZ, MY, MX = NZ // COARSEN, NY // COARSEN, NX // COARSEN
BZ, BY, BX = MZ // GZ, MY // GY, MX // GX
PZ, PY, PX = CZ + 2 * HALO, CY + 2 * HALO, CX + 2 * HALO
LANES = 256
EDGE = 2 * CY
TAIL = PX - CX
BORDER = BY + 2
SHARE = 2 * GX
KX = MX // SHARE
VMEM_MIB = 44
TABLE_ROWS = 24 * 2048

f32 = jnp.float32
bf16 = jnp.bfloat16
HIGHEST = lax.Precision.HIGHEST


def cas(a, b, points):
    angles = 2.0 * np.pi / points * (np.outer(a, b) % points)
    return np.cos(angles) + np.sin(angles)


def split(table):
    high = table.astype(np.float32).astype(ml_dtypes.bfloat16)
    low = (table - high.astype(np.float64)).astype(np.float32).astype(ml_dtypes.bfloat16)
    return high, low


def near_tables():
    reach = np.arange(HALO + 1)
    both = np.arange(-HALO, HALO + 1)
    squared = (
        reach[:, None, None] ** 2 + both[None, :, None] ** 2 + both[None, None, :] ** 2
    ).astype(np.float64)
    erfc = np.vectorize(math.erfc)
    kernel = erfc(np.sqrt(squared) / SCREEN) / (4.0 * math.pi * np.sqrt(squared + SOFTEN))
    cos_y = np.cos(2.0 * np.pi / PY * np.outer(np.arange(PY), both))
    cos_x = np.cos(2.0 * np.pi / PX * np.outer(np.arange(PX), both))
    spectral = np.einsum("dab,ka,lb->dkl", kernel, cos_y, cos_x) / (PY * PX)
    gains = np.zeros(((HALO + 1) * PY, LANES))
    gains[:, :PX] = spectral.reshape(-1, PX)

    every_x, every_y = np.arange(PX), np.arange(PY)
    forward_x = np.zeros((PX, LANES))
    forward_x[:, :PX] = cas(every_x, every_x, PX)
    high, low = split(forward_x)
    own = slice(HALO, HALO + CX)
    ends = np.r_[0:HALO, HALO + CX : PX]
    into_x = np.zeros((512, LANES))
    into_x[0:128], into_x[128:256], into_x[256:384] = high[own], low[own], high[own]
    into_x[384:400], into_x[400:416], into_x[416:432] = high[ends], low[ends], high[ends]

    high, low = split(cas(every_y, every_y, PY))
    into_y = np.zeros((PY, LANES))
    into_y[:, : 3 * PY] = np.concatenate([high, low, high], axis=1)

    back_x = np.zeros((LANES, CX))
    back_x[:PX] = cas(every_x, every_x[own], PX)
    high, low = split(back_x)
    out_x = np.concatenate([high, low, high], axis=0)
    return {"gains": gains, "into_x": into_x, "into_y": into_y, "out_x": out_x}


def far_tables():
    full_x = cas(np.arange(MX), np.arange(MX), MX)
    full_y = cas(np.arange(MY), np.arange(MY), MY)
    full_z = cas(np.arange(MZ), np.arange(MZ), MZ)

    first_x = np.tile(full_x.reshape(MX, SHARE, KX).transpose(1, 0, 2), (1, 1, 8))
    into_z = np.kron(full_z, np.eye(8))

    def waves(points):
        index = np.arange(points)
        signed = (index + points // 2) % points - points // 2
        laplace = 2.0 - 2.0 * np.cos(2.0 * np.pi / points * index)
        return laplace, (2.0 * np.pi / (points * COARSEN) * signed) ** 2

    (lap_z, wave_z), (lap_y, wave_y), (lap_x, wave_x) = waves(MZ), waves(MY), waves(MX)
    laplace = lap_z[:, None, None] + lap_y[None, :, None] + lap_x[None, None, :]
    wave = wave_z[:, None, None] + wave_y[None, :, None] + wave_x[None, None, :]
    laplace[0, 0, 0] = 1.0
    gain = np.exp(-(SCREEN * SCREEN / 4.0) * wave) / (COARSEN * laplace)
    gain[0, 0, 0] = 0.0
    gain = gain / (MZ * MY * MX)
    gain = gain.reshape(MZ, MY, SHARE, 2, 8).transpose(2, 0, 4, 3, 1).reshape(SHARE, MZ * 8, 2 * MY)

    out_z = np.zeros((2, 2 * BORDER * 8, MZ * 8))
    for g in range(2):
        z = np.concatenate([(2 * g + c) * BZ - 1 + np.arange(BORDER) for c in range(2)]) % MZ
        out_z[g] = np.kron(full_z[z], np.eye(8))

    out_y = np.zeros((GY, MY, 128))
    for g in range(GY):
        out_y[g, :, :BORDER] = full_y[:, (g * BY - 1 + np.arange(BORDER)) % MY]

    def refine(coarse):
        matrix = np.zeros((COARSEN * coarse, coarse + 2))
        for fine in range(COARSEN * coarse):
            below, t = fine // COARSEN, (fine % COARSEN + 0.5) / COARSEN - 0.5
            matrix[fine, below + 1] = 1.0 - abs(t)
            matrix[fine, below if t < 0 else below + 2] = abs(t)
        return matrix

    last_x = np.zeros((GX, MX, CX))
    for g in range(GX):
        last_x[g] = full_x[:, (g * BX - 1 + np.arange(BX + 2)) % MX] @ refine(BX).T
    last_y = np.zeros((BORDER * CY, 128))
    last_y[:, : BORDER * BORDER] = np.kron(np.eye(BORDER), refine(BY))
    return {
        "first_x": first_x,
        "full_y": full_y,
        "into_z": into_z,
        "gain": gain,
        "out_z": out_z,
        "out_y": out_y,
        "last_x": last_x,
        "last_y": last_y,
    }


class Tables:
    def __init__(self):
        self.place, rows, pieces = {}, 0, []
        for name, table in (near_tables() | far_tables()).items():
            count, lanes = table.shape[-2:]
            halves = lanes // 128
            flat = table.reshape(-1, count, halves, 128).swapaxes(1, 2).reshape(-1, 128)
            self.place[name] = rows, count, halves
            rows += flat.shape[0]
            pieces.append(flat)
        self.array = np.zeros((TABLE_ROWS, 128), np.float32)
        self.array[:rows] = np.concatenate(pieces)

    def shape(self, name):
        _, count, halves = self.place[name]
        return pltpu.VMEM((halves, count, 128), f32)

    def copies(self, ref, held, sems, index):
        made = []
        for i, (name, target) in enumerate(held.items()):
            first, count, halves = self.place[name]
            rows = halves * count
            start = first + index.get(name, 0) * rows
            if name in index:
                start = pl.multiple_of(start, 8)
            for half in range(halves):
                source = ref.at[pl.ds(start + half * count, count)]
                made.append(pltpu.make_async_copy(source, target.at[half], sems.at[i]))
        for copy in made:
            copy.start()
        pairs, at = {}, 0
        for name in held:
            halves = self.place[name][2]
            pairs[name] = made[at : at + halves]
            at += halves

        def wait(name):
            for copy in pairs[name]:
                copy.wait()
            target = held[name]
            if len(pairs[name]) == 1:
                return target[0]
            return jnp.concatenate([target[0], target[1]], axis=1)

        return wait


TABLES = Tables()


def dot(a, b):
    return jnp.dot(a, b, preferred_element_type=f32)


def exact_dot(a, b):
    return jnp.dot(a, b, preferred_element_type=f32, precision=HIGHEST)


def halves(x):
    high = x.astype(bf16)
    return high, (x - high.astype(f32)).astype(bf16)


def lane(shape):
    return lax.broadcasted_iota(jnp.int32, shape, len(shape) - 1)


def transposed_dot(a, b):
    return lax.dot_general(a, b, (((0,), (0,)), ((), ())), preferred_element_type=f32, precision=HIGHEST)


def share():
    return lax.axis_index("gx") * 2 + lax.axis_index("core")


def is_even(axis):
    return lax.rem(lax.axis_index(axis), 2) == 0


def charge_kernel(density, out):
    parts = []
    for high in range(2):
        planes = []
        for low in range(4):
            z = (high * 4 + low) * COARSEN
            planes.append((density[z] + density[z + 1]) + (density[z + 2] + density[z + 3]))
        parts.append(jnp.concatenate(planes, axis=1))
    rows = jnp.concatenate(parts, axis=0)

    def pool(shape, fine, coarse):
        a = lax.broadcasted_iota(jnp.int32, shape, fine)
        b = lax.broadcasted_iota(jnp.int32, shape, coarse)
        return (a // COARSEN == b).astype(f32)

    rows = exact_dot(rows, pool((4 * CX, 128), 0, 1))
    rows = exact_dot(pool((2 * BY, 2 * CY), 1, 0), rows)
    for peer in range(SHARE):
        out[peer] = rows


def first_kernel(table, charges, out, held, sems):
    wait = TABLES.copies(table, {"first_x": held}, sems, {"first_x": share()})
    peers = charges[...].reshape(GX, 32, 128)
    place = lane((32, 128)) // BX
    blocks = []
    for low in range(4):
        sides = []
        for side in range(2):
            total = None
            for q in range(4):
                shift = (q - low) * BX % 128
                peer = peers[side * 4 + q]
                moved = pltpu.roll(peer, shift, 1) if shift else peer
                total = moved if q == 0 else jnp.where(place == q, moved, total)
            sides.append(total)
        blocks.append(jnp.concatenate(sides, axis=1))
    rows = jnp.concatenate(blocks, axis=0)
    rows = exact_dot(rows, wait("first_x"))
    place = lane((BY, 128)) // KX
    for core in range(2):
        total = None
        for z in range(BZ):
            start = (z % 4) * 32 + core * 16 + (z // 4) * 8
            piece = rows[start : start + 8]
            total = piece if z == 0 else jnp.where(place == z, piece, total)
        for peer in range(2 * GY):
            out[peer, core] = total


def filter_kernel(table, spectrum, out, held_y, held_z, held_g, held_iz, held_iy, sems):
    held = {"full_y": held_y, "into_z": held_z, "gain": held_g, "out_z": held_iz, "out_y": held_iy}
    index = {"gain": share(), "out_z": lax.axis_index("yh"), "out_y": lax.axis_index("gy")}
    wait = TABLES.copies(table, held, sems, index)
    blocks = spectrum[...].reshape(GY, 4, BY, 128)
    full_y = wait("full_y")
    waves = [transposed_dot(blocks[:, b].reshape(MY, 128), full_y) for b in range(4)]
    rows = jnp.concatenate(waves, axis=0).reshape(MZ, 2, 8, MY)
    rows = jnp.concatenate([rows[:, half].reshape(MZ * 8, MY) for half in range(2)], axis=1)
    rows = exact_dot(wait("into_z"), rows)
    rows = rows * wait("gain")
    rows = exact_dot(wait("out_z"), rows)
    rows = jnp.concatenate([rows[:, :MY], rows[:, MY:]], axis=0)
    rows = exact_dot(rows, wait("out_y"))
    for core in range(2):
        sides = []
        for half in range(2):
            total = None
            for z in range(BORDER):
                start = ((half * 2 + core) * BORDER + z) * 8
                piece = rows[start : start + 8]
                total = piece if z == 0 else total + pltpu.roll(piece, z * BORDER, 1)
            sides.append(total)
        message = jnp.concatenate(sides, axis=0)
        for peer in range(GX):
            out[peer * 2 + core] = message


def edge_x_kernel(density, even, odd):
    place = lane((EDGE, 128)) // HALO
    left = right = jnp.zeros((EDGE, 128), f32)
    for j in range(16):
        rows = density[2 * j : 2 * j + 2].reshape(EDGE, 128)
        shift = j * HALO
        left = jnp.where(place == j, pltpu.roll(rows, shift, 1) if shift else rows, left)
        shift = (shift - (CX - HALO)) % 128
        right = jnp.where(place == j, pltpu.roll(rows, shift, 1) if shift else rows, right)
    lower = is_even("gx")
    even[...] = jnp.where(lower, right, left)
    odd[...] = jnp.where(lower, left, right)


def near_x_kernel(table, density, x_even, x_odd, waves, even, odd, held, sems):
    wait = TABLES.copies(table, {"into_x": held}, sems, {})
    lanes = lane((EDGE, 128))
    lower = is_even("gx")
    one, two = x_even[...], x_odd[...]
    left, right = jnp.where(lower, two, one), jnp.where(lower, one, two)
    groups = []
    for j in range(16):
        rows = density[2 * j : 2 * j + 2].reshape(EDGE, 128)
        to_left, to_right = (-HALO * j) % 128, (HALO - HALO * j) % 128
        ends = jnp.where(
            lanes < HALO,
            pltpu.roll(left, to_left, 1) if to_left else left,
            pltpu.roll(right, to_right, 1) if to_right else right,
        )
        ends = jnp.where(lanes < 2 * HALO, ends, 0.0)
        high = ends.astype(bf16).astype(f32)
        low = ends - high
        ends = (high + pltpu.roll(high, 2 * HALO, 1) + pltpu.roll(low, 4 * HALO, 1)).astype(bf16)
        high, low = halves(rows)
        groups.append(jnp.concatenate([high, high, low, ends], axis=1))
    into_x = wait("into_x").astype(bf16)
    for j in range(4):
        wave = dot(jnp.concatenate(groups[4 * j : 4 * j + 4], axis=0), into_x)
        waves[8 * j : 8 * j + 8] = wave.reshape(8, CY, LANES)

    place = lane((4 * HALO, 128)) // TAIL
    start = jnp.where(is_even("gy"), CY - HALO, 0)
    for target, first in ((even, start), (odd, CY - HALO - start)):
        rows = pl.ds(pl.multiple_of(first, 8), HALO)
        target[0:CZ] = waves[:, rows, pl.ds(0, 128)]
        total = None
        for j in range(8):
            tail = waves[4 * j : 4 * j + 4, rows, pl.ds(128, 128)].reshape(4 * HALO, 128)
            total = tail if j == 0 else jnp.where(place == j, pltpu.roll(tail, j * TAIL, 1), total)
        target[CZ : CZ + 4] = total.reshape(4, HALO, 128)


def near_y_kernel(table, waves_x, y_even, y_odd, waves, even, odd, held, sems):
    wait = TABLES.copies(table, {"into_y": held}, sems, {})
    lower = is_even("gy")
    one, two = y_even[...], y_odd[...]
    before, after = jnp.where(lower, two, one), jnp.where(lower, one, two)
    into_y = wait("into_y")[:, : 3 * PY].astype(bf16)
    tails = [ends[CZ : CZ + 4].reshape(4 * HALO, 128) for ends in (before, after)]
    for j in range(8):
        ends = [pltpu.roll(tail, -j * TAIL % 128, 1) if j else tail for tail in tails]
        for i in range(4):
            z, rows = 4 * j + i, slice(i * HALO, (i + 1) * HALO)
            high, low = halves(
                jnp.concatenate(
                    [
                        jnp.concatenate([before[z], ends[0][rows]], axis=1),
                        waves_x[z],
                        jnp.concatenate([after[z], ends[1][rows]], axis=1),
                    ],
                    axis=0,
                )
            )
            waves[z] = dot(into_y, jnp.concatenate([high, high, low], axis=0))

    place = lane((PY, 128)) // TAIL
    start = jnp.where(is_even("core"), CZ - HALO, 0)
    for target, first in ((even, start), (odd, CZ - HALO - start)):
        target[0:HALO] = waves[pl.ds(first, HALO), :, pl.ds(0, 128)]
        total = None
        for j in range(HALO):
            tail = waves[first + j, :, pl.ds(128, 128)]
            total = tail if j == 0 else jnp.where(place == j, pltpu.roll(tail, j * TAIL, 1), total)
        target[HALO] = total


def sum_planes(gains, count, load, store):
    window = [load(z) for z in range(2 * HALO)]
    for z in range(count):
        window.append(load(z + 2 * HALO))
        total = gains[0] * window[HALO]
        for d in range(1, HALO + 1):
            total = total + gains[d] * (window[HALO - d] + window[HALO + d])
        store(z, total)
        window.pop(0)


def back(planes, out_y, out_x):
    rows = []
    for plane in planes:
        high, low = halves(plane)
        rows.append(dot(out_y, jnp.concatenate([high, high, low], axis=0)))
    high, low = halves(jnp.concatenate(rows, axis=0))
    field = dot(jnp.concatenate([high, high, low], axis=1), out_x)
    return [field[i * CY : (i + 1) * CY] for i in range(len(planes))]


def inner_kernel(
    table, waves, spectrum, out, sums, held_g, held_y, held_ox, held_lx, held_ly, sems
):
    held = {"gains": held_g, "into_y": held_y, "out_x": held_ox, "last_x": held_lx, "last_y": held_ly}
    wait = TABLES.copies(table, held, sems, {"last_x": lax.axis_index("gx")})
    wait("gains")

    @pl.loop(0, PY // 8)
    def _(c):
        row = pl.ds(pl.multiple_of(c * 8, 8), 8)
        for side in range(2):
            column = pl.ds(side * 128, 128)
            gains = [held_g[side, pl.ds(pl.multiple_of(d * PY + c * 8, 8), 8)] for d in range(HALO + 1)]

            def store(i, value):
                sums[i, row, column] = value

            sum_planes(gains, CZ - 2 * HALO, lambda z: waves[z, row, column], store)

    rows = spectrum[...].reshape(MX, 128)
    field = transposed_dot(rows, wait("last_x"))
    field = exact_dot(wait("last_y"), field)

    def plane(z):
        return field[z * CY : (z + 1) * CY]

    out_y = wait("into_y")[HALO : HALO + CY, : 3 * PY].astype(bf16)
    out_x = wait("out_x").astype(bf16)
    for block in range(BZ):
        before, here, after = plane(block), plane(block + 1), plane(block + 2)
        inner = 2 <= block < 6
        near = back([sums[4 * (block - 2) + i] for i in range(4)], out_y, out_x) if inner else None
        for residue in range(COARSEN):
            t = (residue + 0.5) / COARSEN - 0.5
            value = (1.0 - abs(t)) * here + abs(t) * (before if t < 0 else after)
            out[block * COARSEN + residue] = near[residue] + value if inner else value


def outer_kernel(
    table, waves, z_even, z_odd, inner, out, ends, sums, held_g, held_y, held_ox, sems
):
    held = {"gains": held_g, "into_y": held_y, "out_x": held_ox}
    wait = TABLES.copies(table, held, sems, {})
    out[HALO : CZ - HALO] = inner[HALO : CZ - HALO]
    lower = is_even("core")
    one, two = z_even[...], z_odd[...]
    for i, end in enumerate((jnp.where(lower, two, one), jnp.where(lower, one, two))):
        for j in range(HALO):
            ends[i, j, :, 0:128] = end[j]
            ends[i, j, :, 128:256] = pltpu.roll(end[HALO], -j * TAIL % 128, 1) if j else end[HALO]
    wait("gains")

    @pl.loop(0, PY // 8)
    def _(c):
        row = pl.ds(pl.multiple_of(c * 8, 8), 8)
        for side in range(2):
            column = pl.ds(side * 128, 128)
            gains = [held_g[side, pl.ds(pl.multiple_of(d * PY + c * 8, 8), 8)] for d in range(HALO + 1)]

            def low(z):
                return ends[0, z, row, column] if z < HALO else waves[z - HALO, row, column]

            def high(z):
                z += CZ - 2 * HALO
                return waves[z, row, column] if z < CZ else ends[1, z - CZ, row, column]

            def store(first):
                def put(i, value):
                    sums[first + i, row, column] = value

                return put

            sum_planes(gains, HALO, low, store(0))
            sum_planes(gains, HALO, high, store(HALO))

    out_y = wait("into_y")[HALO : HALO + CY, : 3 * PY].astype(bf16)
    out_x = wait("out_x").astype(bf16)
    for step in range(4):
        near = back([sums[4 * step + i] for i in range(4)], out_y, out_x)
        first = 4 * step + (CZ - 2 * HALO if step >= 2 else 0)
        for i in range(4):
            out[first + i] = inner[first + i] + near[i]


def call(kernel, outs, arrays=0, tables=(), scratch=(), us=1.0):
    vmem = pl.BlockSpec(memory_space=pltpu.VMEM)
    many = isinstance(outs, list)
    specs = [vmem] * arrays
    scratch = list(scratch)
    if tables:
        specs = [pl.BlockSpec(memory_space=pltpu.HBM)] + specs
        scratch += [TABLES.shape(name) for name in tables]
        scratch.append(pltpu.SemaphoreType.DMA((len(tables),)))
    return pl.pallas_call(
        kernel,
        out_shape=[jax.ShapeDtypeStruct(s, f32) for s in outs] if many else jax.ShapeDtypeStruct(outs, f32),
        in_specs=specs,
        out_specs=[vmem] * len(outs) if many else vmem,
        scratch_shapes=scratch,
        compiler_params=pltpu.CompilerParams(vmem_limit_bytes=VMEM_MIB * 1024 * 1024),
        cost_estimate=pl.CostEstimate(flops=int(us * 1e9), bytes_accessed=int(us * 3e6), transcendentals=0),
        name=kernel.__name__,
    )


def exchange(even, odd, axis):
    peers = lax.axis_size(axis)
    low_first = [(i, i + 1 if i % 2 == 0 else i - 1) for i in range(peers)]
    high_first = [(i, (i + 1 if i % 2 else i - 1) % peers) for i in range(peers)]
    even = lax.ppermute(even, axis, low_first)
    return even, lax.ppermute(odd, axis, high_first)


def body(density):
    table = jnp.asarray(TABLES.array)
    charges = call(charge_kernel, (SHARE, 16, 128), 1, us=1.0)(density)
    charges = lax.all_to_all(charges, ("gx", "core"), 0, 0, tiled=True)

    x_ends = call(edge_x_kernel, [(EDGE, 128)] * 2, 1, us=0.2)(density)
    x_ends = exchange(*x_ends, "gx")
    charges, x_ends = lax.optimization_barrier((charges, x_ends))

    spectrum = call(first_kernel, (2 * GY, 2, 8, 128), 1, ["first_x"], us=1.5)(table, charges)
    spectrum = lax.all_to_all(spectrum, ("gy", "yh"), 0, 0, tiled=True)

    waves_x, *y_ends = call(
        near_x_kernel, [(CZ, CY, LANES), (CZ + 4, HALO, 128), (CZ + 4, HALO, 128)], 3, ["into_x"], us=1.0
    )(table, density, *x_ends)
    spectrum, _ = lax.optimization_barrier((spectrum, y_ends))
    y_ends = exchange(*y_ends, "gy")

    spectrum = call(
        filter_kernel, (SHARE, KX, 128), 1, ["full_y", "into_z", "gain", "out_z", "out_y"], us=3.0
    )(table, spectrum)
    y_ends, _ = lax.optimization_barrier((y_ends, spectrum))
    spectrum = lax.all_to_all(spectrum, ("gx", "core"), 0, 0, tiled=True)

    waves, *z_ends = call(
        near_y_kernel, [(CZ, PY, LANES), (HALO + 1, PY, 128), (HALO + 1, PY, 128)], 3, ["into_y"], us=1.5
    )(table, waves_x, *y_ends)
    z_ends = exchange(*z_ends, ("yh", "core"))

    inner = call(
        inner_kernel,
        (CZ, CY, CX),
        2,
        ["gains", "into_y", "out_x", "last_x", "last_y"],
        [pltpu.VMEM((CZ - 2 * HALO, PY, LANES), f32)],
        us=4.0,
    )(table, waves, spectrum)
    return call(
        outer_kernel,
        (CZ, CY, CX),
        4,
        ["gains", "into_y", "out_x"],
        [pltpu.VMEM((2, HALO, PY, LANES), f32), pltpu.VMEM((2 * HALO, PY, LANES), f32)],
        us=3.0,
    )(table, waves, *z_ends, inner)


def solution(mesh):
    devices = mesh.devices.reshape(GX, GY, 2, 2)
    parts = jax.sharding.Mesh(devices, ("gx", "gy", "yh", "core"))
    placed = P(("yh", "core"), "gy", "gx")
    return jax.shard_map(body, mesh=parts, in_specs=(placed,), out_specs=placed, check_vma=False)
```

```python
import math

import jax
import jax.numpy as jnp
import ml_dtypes
import numpy as np
from jax import lax
from jax.experimental import pallas as pl
from jax.experimental.pallas import tpu as pltpu
from jax.sharding import PartitionSpec as P

HALO = 8
COARSEN = 4
SCREEN = 6.0
SOFTEN = 0.25

NZ, NY, NX = 128, 512, 1024
GZ, GY, GX = 4, 16, 8
CZ, CY, CX = NZ // GZ, NY // GY, NX // GX
MZ, MY, MX = NZ // COARSEN, NY // COARSEN, NX // COARSEN
BZ, BY, BX = MZ // GZ, MY // GY, MX // GX
PZ, PY, PX = CZ + 2 * HALO, CY + 2 * HALO, CX + 2 * HALO
LANES = 256
GROUP = 3 * PY
BORDER = BY + 2
SHARE = 2 * GX
KX = MX // SHARE
VMEM_MIB = 44
TABLE_ROWS = 24 * 2048

f32 = jnp.float32
bf16 = jnp.bfloat16
HIGHEST = lax.Precision.HIGHEST


def cas(a, b, points):
    angles = 2.0 * np.pi / points * (np.outer(a, b) % points)
    return np.cos(angles) + np.sin(angles)


def split(table):
    high = table.astype(np.float32).astype(ml_dtypes.bfloat16)
    low = (table - high.astype(np.float64)).astype(np.float32).astype(ml_dtypes.bfloat16)
    return high, low


def near_tables():
    reach = np.arange(HALO + 1)
    both = np.arange(-HALO, HALO + 1)
    squared = (
        reach[:, None, None] ** 2 + both[None, :, None] ** 2 + both[None, None, :] ** 2
    ).astype(np.float64)
    erfc = np.vectorize(math.erfc)
    kernel = erfc(np.sqrt(squared) / SCREEN) / (4.0 * math.pi * np.sqrt(squared + SOFTEN))
    cos_y = np.cos(2.0 * np.pi / PY * np.outer(np.arange(PY), both))
    cos_x = np.cos(2.0 * np.pi / PX * np.outer(np.arange(PX), both))
    spectral = np.einsum("dab,ka,lb->dkl", kernel, cos_y, cos_x) / (PY * PX)
    gains = np.zeros(((HALO + 1) * PY, LANES))
    gains[:, :PX] = spectral.reshape(-1, PX)

    every_x, every_y = np.arange(PX), np.arange(PY)
    forward_x = np.zeros((PX, LANES))
    forward_x[:, :PX] = cas(every_x, every_x, PX)
    high, low = split(forward_x)
    own = slice(HALO, HALO + CX)
    ends = np.r_[0:HALO, HALO + CX : PX]
    into_x = np.zeros((512, LANES))
    into_x[0:128], into_x[128:256], into_x[256:384] = high[own], low[own], high[own]
    into_x[384:400], into_x[400:416], into_x[416:432] = high[ends], low[ends], high[ends]

    high, low = split(cas(every_y, every_y, PY))
    into_y = np.zeros((PY, LANES))
    into_y[:, : 3 * PY] = np.concatenate([high, low, high], axis=1)

    back_x = np.zeros((LANES, CX))
    back_x[:PX] = cas(every_x, every_x[own], PX)
    high, low = split(back_x)
    out_x = np.concatenate([high, low, high], axis=0)
    return {"gains": gains, "into_x": into_x, "into_y": into_y, "out_x": out_x}


def far_tables():
    full_x = cas(np.arange(MX), np.arange(MX), MX)
    full_y = cas(np.arange(MY), np.arange(MY), MY)
    full_z = cas(np.arange(MZ), np.arange(MZ), MZ)

    first_x = np.tile(full_x.reshape(MX, SHARE, KX).transpose(1, 0, 2), (1, 1, 8))
    into_z = np.kron(full_z, np.eye(8))

    def waves(points):
        index = np.arange(points)
        signed = (index + points // 2) % points - points // 2
        laplace = 2.0 - 2.0 * np.cos(2.0 * np.pi / points * index)
        return laplace, (2.0 * np.pi / (points * COARSEN) * signed) ** 2

    (lap_z, wave_z), (lap_y, wave_y), (lap_x, wave_x) = waves(MZ), waves(MY), waves(MX)
    laplace = lap_z[:, None, None] + lap_y[None, :, None] + lap_x[None, None, :]
    wave = wave_z[:, None, None] + wave_y[None, :, None] + wave_x[None, None, :]
    laplace[0, 0, 0] = 1.0
    gain = np.exp(-(SCREEN * SCREEN / 4.0) * wave) / (COARSEN * laplace)
    gain[0, 0, 0] = 0.0
    gain = gain / (MZ * MY * MX)
    gain = gain.reshape(MZ, MY, SHARE, 2, 8).transpose(2, 0, 4, 3, 1).reshape(SHARE, MZ * 8, 2 * MY)

    out_z = np.zeros((2, 2 * BORDER * 8, MZ * 8))
    for g in range(2):
        z = np.concatenate([(2 * g + c) * BZ - 1 + np.arange(BORDER) for c in range(2)]) % MZ
        out_z[g] = np.kron(full_z[z], np.eye(8))

    out_y = np.zeros((GY, MY, 128))
    for g in range(GY):
        out_y[g, :, :BORDER] = full_y[:, (g * BY - 1 + np.arange(BORDER)) % MY]

    def refine(coarse):
        matrix = np.zeros((COARSEN * coarse, coarse + 2))
        for fine in range(COARSEN * coarse):
            below, t = fine // COARSEN, (fine % COARSEN + 0.5) / COARSEN - 0.5
            matrix[fine, below + 1] = 1.0 - abs(t)
            matrix[fine, below if t < 0 else below + 2] = abs(t)
        return matrix

    last_x = np.zeros((GX, MX, CX))
    for g in range(GX):
        last_x[g] = full_x[:, (g * BX - 1 + np.arange(BX + 2)) % MX] @ refine(BX).T
    last_y = np.zeros((BORDER * CY, 128))
    last_y[:, : BORDER * BORDER] = np.kron(np.eye(BORDER), refine(BY))
    return {
        "first_x": first_x,
        "full_y": full_y,
        "into_z": into_z,
        "gain": gain,
        "out_z": out_z,
        "out_y": out_y,
        "last_x": last_x,
        "last_y": last_y,
    }


class Tables:
    def __init__(self):
        self.place, rows, pieces = {}, 0, []
        for name, table in (near_tables() | far_tables()).items():
            count, lanes = table.shape[-2:]
            halves = lanes // 128
            flat = table.reshape(-1, count, halves, 128).swapaxes(1, 2).reshape(-1, 128)
            self.place[name] = rows, count, halves
            rows += flat.shape[0]
            pieces.append(flat)
        self.array = np.zeros((TABLE_ROWS, 128), np.float32)
        self.array[:rows] = np.concatenate(pieces)

    def shape(self, name):
        _, count, halves = self.place[name]
        return pltpu.VMEM((halves, count, 128), f32)

    def copies(self, ref, held, sems, index):
        made = []
        for i, (name, target) in enumerate(held.items()):
            first, count, halves = self.place[name]
            rows = halves * count
            start = first + index.get(name, 0) * rows
            if name in index:
                start = pl.multiple_of(start, 8)
            for half in range(halves):
                source = ref.at[pl.ds(start + half * count, count)]
                made.append(pltpu.make_async_copy(source, target.at[half], sems.at[i]))
        for copy in made:
            copy.start()
        pairs, at = {}, 0
        for name in held:
            halves = self.place[name][2]
            pairs[name] = made[at : at + halves]
            at += halves

        def wait(name):
            for copy in pairs[name]:
                copy.wait()
            target = held[name]
            if len(pairs[name]) == 1:
                return target[0]
            return jnp.concatenate([target[0], target[1]], axis=1)

        return wait


TABLES = Tables()


def dot(a, b):
    return jnp.dot(a, b, preferred_element_type=f32)


def exact_dot(a, b):
    return jnp.dot(a, b, preferred_element_type=f32, precision=HIGHEST)


def halves(x):
    high = x.astype(bf16)
    return high, (x - high.astype(f32)).astype(bf16)


def lane(shape):
    return lax.broadcasted_iota(jnp.int32, shape, len(shape) - 1)


def transposed_dot(a, b):
    return lax.dot_general(a, b, (((0,), (0,)), ((), ())), preferred_element_type=f32, precision=HIGHEST)


def share():
    return lax.axis_index("gx") * 2 + lax.axis_index("core")


def is_even(axis):
    return lax.rem(lax.axis_index(axis), 2) == 0


def charge_kernel(density, out, even, odd):
    parts = []
    for high in range(2):
        planes = []
        for low in range(4):
            z = (high * 4 + low) * COARSEN
            planes.append((density[z] + density[z + 1]) + (density[z + 2] + density[z + 3]))
        parts.append(jnp.concatenate(planes, axis=1))
    rows = jnp.concatenate(parts, axis=0)

    def pool(shape, fine, coarse):
        a = lax.broadcasted_iota(jnp.int32, shape, fine)
        b = lax.broadcasted_iota(jnp.int32, shape, coarse)
        return (a // COARSEN == b).astype(f32)

    rows = exact_dot(rows, pool((4 * CX, 128), 0, 1))
    rows = exact_dot(pool((2 * BY, 2 * CY), 1, 0), rows)
    for peer in range(SHARE):
        out[peer] = rows
    start = jnp.where(is_even("core"), CZ - HALO, 0)
    even[...] = density[pl.ds(start, HALO)]
    odd[...] = density[pl.ds(CZ - HALO - start, HALO)]


def first_kernel(table, charges, out, held, sems):
    wait = TABLES.copies(table, {"first_x": held}, sems, {"first_x": share()})
    peers = charges[...].reshape(GX, 32, 128)
    place = lane((32, 128)) // BX
    blocks = []
    for low in range(4):
        sides = []
        for side in range(2):
            total = None
            for q in range(4):
                shift = (q - low) * BX % 128
                peer = peers[side * 4 + q]
                moved = pltpu.roll(peer, shift, 1) if shift else peer
                total = moved if q == 0 else jnp.where(place == q, moved, total)
            sides.append(total)
        blocks.append(jnp.concatenate(sides, axis=1))
    rows = jnp.concatenate(blocks, axis=0)
    rows = exact_dot(rows, wait("first_x"))
    place = lane((BY, 128)) // KX
    for core in range(2):
        total = None
        for z in range(BZ):
            start = (z % 4) * 32 + core * 16 + (z // 4) * 8
            piece = rows[start : start + 8]
            total = piece if z == 0 else jnp.where(place == z, piece, total)
        for peer in range(2 * GY):
            out[peer, core] = total


def filter_kernel(table, spectrum, out, held_y, held_z, held_g, held_iz, held_iy, sems):
    held = {"full_y": held_y, "into_z": held_z, "gain": held_g, "out_z": held_iz, "out_y": held_iy}
    index = {"gain": share(), "out_z": lax.axis_index("yh"), "out_y": lax.axis_index("gy")}
    wait = TABLES.copies(table, held, sems, index)
    blocks = spectrum[...].reshape(GY, 4, BY, 128)
    full_y = wait("full_y")
    waves = [transposed_dot(blocks[:, b].reshape(MY, 128), full_y) for b in range(4)]
    rows = jnp.concatenate(waves, axis=0).reshape(MZ, 2, 8, MY)
    rows = jnp.concatenate([rows[:, half].reshape(MZ * 8, MY) for half in range(2)], axis=1)
    rows = exact_dot(wait("into_z"), rows)
    rows = rows * wait("gain")
    rows = exact_dot(wait("out_z"), rows)
    rows = jnp.concatenate([rows[:, :MY], rows[:, MY:]], axis=0)
    rows = exact_dot(rows, wait("out_y"))
    for core in range(2):
        sides = []
        for half in range(2):
            total = None
            for z in range(BORDER):
                start = ((half * 2 + core) * BORDER + z) * 8
                piece = rows[start : start + 8]
                total = piece if z == 0 else total + pltpu.roll(piece, z * BORDER, 1)
            sides.append(total)
        message = jnp.concatenate(sides, axis=0)
        for peer in range(GX):
            out[peer * 2 + core] = message


def far_kernel(table, spectrum, out, held_x, held_y, sems):
    held = {"last_x": held_x, "last_y": held_y}
    wait = TABLES.copies(table, held, sems, {"last_x": lax.axis_index("gx")})
    rows = spectrum[...].reshape(MX, 128)
    field = transposed_dot(rows, wait("last_x"))
    field = exact_dot(wait("last_y"), field)

    def plane(z):
        return field[z * CY : (z + 1) * CY]

    for block in range(BZ):
        before, here, after = plane(block), plane(block + 1), plane(block + 2)
        for residue in range(COARSEN):
            t = (residue + 0.5) / COARSEN - 0.5
            value = (1.0 - abs(t)) * here + abs(t) * (before if t < 0 else after)
            z = block * COARSEN + residue
            out[z] = value


def edge_y_kernel(density, z_even, z_odd, even, odd):
    lower = is_even("core")
    start = jnp.where(is_even("gy"), CY - HALO, 0)
    for target, first in ((even, start), (odd, CY - HALO - start)):
        rows = pl.ds(pl.multiple_of(first, 8), HALO)
        one, two = z_even[:, rows], z_odd[:, rows]
        target[0:HALO] = jnp.where(lower, two, one)
        target[HALO : HALO + CZ] = density[:, rows]
        target[HALO + CZ : PZ] = jnp.where(lower, one, two)


def edge_x_kernel(table, density, z_even, z_odd, y_even, y_odd, waves, even, odd, padded, held, sems):
    wait = TABLES.copies(table, {"into_y": held}, sems, {})
    lower = is_even("core")
    one, two = z_even[...], z_odd[...]
    middle = slice(HALO, HALO + CY)
    padded[0:HALO, middle] = jnp.where(lower, two, one)
    padded[HALO : HALO + CZ, middle] = density[...]
    padded[HALO + CZ : PZ, middle] = jnp.where(lower, one, two)
    lower = is_even("gy")
    one, two = y_even[...], y_odd[...]
    padded[:, 0:HALO] = jnp.where(lower, two, one)
    padded[:, HALO + CY : PY] = jnp.where(lower, one, two)

    into_y = wait("into_y")[:, : 3 * PY].astype(bf16)
    place = lane((GROUP, 128)) // HALO
    left = right = jnp.zeros((GROUP, 128), f32)
    for j in range(8):
        rows = []
        for pair in range(3):
            z = 6 * j + 2 * pair
            high, low = halves(jnp.concatenate([padded[z], padded[z + 1]], axis=1))
            wave = dot(into_y, jnp.concatenate([high, high, low], axis=0))
            waves[z], waves[z + 1] = wave[:, :128], wave[:, 128:]
            rows += [wave[:, :128], wave[:, 128:]]
        for i in range(2):
            group = jnp.concatenate(rows[3 * i : 3 * i + 3], axis=0)
            shift = (2 * j + i) * HALO
            left = jnp.where(place == 2 * j + i, pltpu.roll(group, shift, 1) if shift else group, left)
            shift = (shift - (CX - HALO)) % 128
            right = jnp.where(place == 2 * j + i, pltpu.roll(group, shift, 1) if shift else group, right)
    lower = is_even("gx")
    even[...] = jnp.where(lower, right, left)
    odd[...] = jnp.where(lower, left, right)


def near_kernel(
    table, waves, x_even, x_odd, far, out, wave_x, wave_z, held_g, held_ix, held_y, held_ox, sems
):
    held = {"into_x": held_ix, "gains": held_g, "into_y": held_y, "out_x": held_ox}
    wait = TABLES.copies(table, held, sems, {})
    lanes = lane((GROUP, 128))
    lower = is_even("gx")
    one, two = x_even[...], x_odd[...]
    left, right = jnp.where(lower, two, one), jnp.where(lower, one, two)
    into_x = wait("into_x").astype(bf16)
    for j in range(16):
        rows = waves[3 * j : 3 * j + 3].reshape(GROUP, 128)
        to_left, to_right = (-HALO * j) % 128, (HALO - HALO * j) % 128
        ends = jnp.where(
            lanes < HALO,
            pltpu.roll(left, to_left, 1) if to_left else left,
            pltpu.roll(right, to_right, 1) if to_right else right,
        )
        ends = jnp.where(lanes < 2 * HALO, ends, 0.0)
        high = ends.astype(bf16).astype(f32)
        low = ends - high
        ends = (high + pltpu.roll(high, 2 * HALO, 1) + pltpu.roll(low, 4 * HALO, 1)).astype(bf16)
        high, low = halves(rows)
        wave = dot(jnp.concatenate([high, high, low, ends], axis=1), into_x)
        for i in range(3):
            wave_x[3 * j + i] = wave[i * PY : (i + 1) * PY]

    wait("gains")

    @pl.loop(0, PY // 8)
    def _(c):
        for side in range(LANES // 128):
            gain = [
                held_g[side, pl.ds(pl.multiple_of(d * PY + c * 8, 8), 8)] for d in range(HALO + 1)
            ]
            row, column = pl.ds(pl.multiple_of(c * 8, 8), 8), pl.ds(side * 128, 128)
            window = [wave_x[z, row, column] for z in range(2 * HALO)]
            for z in range(CZ):
                window.append(wave_x[z + 2 * HALO, row, column])
                total = gain[0] * window[HALO]
                for d in range(1, HALO + 1):
                    total = total + gain[d] * (window[HALO - d] + window[HALO + d])
                wave_z[z, row, column] = total
                window.pop(0)

    out_y = wait("into_y")[HALO : HALO + CY, : 3 * PY].astype(bf16)
    out_x = wait("out_x").astype(bf16)

    for step in range(CZ // 4):
        rows = []
        for i in range(4):
            high, low = halves(wave_z[step * 4 + i])
            rows.append(dot(out_y, jnp.concatenate([high, high, low], axis=0)))
        high, low = halves(jnp.concatenate(rows, axis=0))
        field = dot(jnp.concatenate([high, high, low], axis=1), out_x)
        for i in range(4):
            out[step * 4 + i] = far[step * 4 + i] + field[i * CY : (i + 1) * CY]


def call(kernel, outs, arrays=0, tables=(), scratch=(), us=1.0):
    vmem = pl.BlockSpec(memory_space=pltpu.VMEM)
    many = isinstance(outs, list)
    specs = [vmem] * arrays
    scratch = list(scratch)
    if tables:
        specs = [pl.BlockSpec(memory_space=pltpu.HBM)] + specs
        scratch += [TABLES.shape(name) for name in tables]
        scratch.append(pltpu.SemaphoreType.DMA((len(tables),)))
    return pl.pallas_call(
        kernel,
        out_shape=[jax.ShapeDtypeStruct(s, f32) for s in outs] if many else jax.ShapeDtypeStruct(outs, f32),
        in_specs=specs,
        out_specs=[vmem] * len(outs) if many else vmem,
        scratch_shapes=scratch,
        compiler_params=pltpu.CompilerParams(vmem_limit_bytes=VMEM_MIB * 1024 * 1024),
        cost_estimate=pl.CostEstimate(flops=int(us * 1e9), bytes_accessed=int(us * 3e6), transcendentals=0),
        name=kernel.__name__,
    )


def exchange(even, odd, axis):
    peers = lax.axis_size(axis)
    low_first = [(i, i + 1 if i % 2 == 0 else i - 1) for i in range(peers)]
    high_first = [(i, (i + 1 if i % 2 else i - 1) % peers) for i in range(peers)]
    odd = lax.ppermute(odd, axis, high_first)
    return lax.ppermute(even, axis, low_first), odd


def body(density):
    table = jnp.asarray(TABLES.array)
    charges, *z_ends = call(
        charge_kernel, [(SHARE, 16, 128), (HALO, CY, CX), (HALO, CY, CX)], 1, us=1.0
    )(density)
    charges = lax.all_to_all(charges, ("gx", "core"), 0, 0, tiled=True)
    z_ends = exchange(*z_ends, ("yh", "core"))
    spectrum = call(first_kernel, (2 * GY, 2, 8, 128), 1, ["first_x"], us=1.3)(table, charges)
    spectrum = lax.all_to_all(spectrum, ("gy", "yh"), 0, 0, tiled=True)

    y_ends = call(edge_y_kernel, [(PZ, HALO, CX)] * 2, 3, us=10.0)(density, *z_ends)
    spectrum, _ = lax.optimization_barrier((spectrum, y_ends))
    y_ends = exchange(*y_ends, "gy")
    spectrum = call(filter_kernel, (SHARE, KX, 128), 1, ["full_y", "into_z", "gain", "out_z", "out_y"], us=3.0)(
        table, spectrum
    )
    y_ends, _ = lax.optimization_barrier((y_ends, spectrum))
    spectrum = lax.all_to_all(spectrum, ("gx", "core"), 0, 0, tiled=True)
    waves, even, odd = call(
        edge_x_kernel,
        [(PZ, PY, CX), (GROUP, 128), (GROUP, 128)],
        5,
        ["into_y"],
        [pltpu.VMEM((PZ, PY, CX), f32)],
        us=10.0,
    )(table, density, *z_ends, *y_ends)
    x_ends = exchange(even, odd, "gx")
    far = call(far_kernel, (CZ, CY, CX), 1, ["last_x", "last_y"], us=5.0)(table, spectrum)
    return call(
        near_kernel,
        (CZ, CY, CX),
        4,
        ["gains", "into_x", "into_y", "out_x"],
        [pltpu.VMEM((PZ, PY, LANES), f32), pltpu.VMEM((CZ, PY, LANES), f32)],
        us=0.1,
    )(table, waves, *x_ends, far)


def solution(mesh):
    devices = mesh.devices.reshape(GX, GY, 2, 2)
    parts = jax.sharding.Mesh(devices, ("gx", "gy", "yh", "core"))
    placed = P(("yh", "core"), "gy", "gx")
    return jax.shard_map(body, mesh=parts, in_specs=(placed,), out_specs=placed, check_vma=False)
```

```python
import math

import jax
import jax.numpy as jnp
import ml_dtypes
import numpy as np
from jax import lax
from jax.experimental import pallas as pl
from jax.experimental.pallas import tpu as pltpu
from jax.sharding import PartitionSpec as P

HALO = 8
COARSEN = 4
SCREEN = 6.0
SOFTEN = 0.25

NZ, NY, NX = 128, 512, 1024
GZ, GY, GX = 4, 16, 8
CZ, CY, CX = NZ // GZ, NY // GY, NX // GX
MZ, MY, MX = NZ // COARSEN, NY // COARSEN, NX // COARSEN
BZ, BY, BX = MZ // GZ, MY // GY, MX // GX
PZ, PY, PX = CZ + 2 * HALO, CY + 2 * HALO, CX + 2 * HALO
LANES = 256
BORDER = BY + 2
SHARE = 2 * GX
KX = MX // SHARE
VMEM_MIB = 44
TABLE_ROWS = 24 * 2048

f32 = jnp.float32
bf16 = jnp.bfloat16
HIGHEST = lax.Precision.HIGHEST


def cas(a, b, points):
    angles = 2.0 * np.pi / points * (np.outer(a, b) % points)
    return np.cos(angles) + np.sin(angles)


def split(table):
    high = table.astype(np.float32).astype(ml_dtypes.bfloat16)
    low = (table - high.astype(np.float64)).astype(np.float32).astype(ml_dtypes.bfloat16)
    return high, low


def near_tables():
    reach = np.arange(HALO + 1)
    both = np.arange(-HALO, HALO + 1)
    squared = (
        reach[:, None, None] ** 2 + both[None, :, None] ** 2 + both[None, None, :] ** 2
    ).astype(np.float64)
    erfc = np.vectorize(math.erfc)
    kernel = erfc(np.sqrt(squared) / SCREEN) / (4.0 * math.pi * np.sqrt(squared + SOFTEN))
    cos_y = np.cos(2.0 * np.pi / PY * np.outer(np.arange(PY), both))
    cos_x = np.cos(2.0 * np.pi / PX * np.outer(np.arange(PX), both))
    spectral = np.einsum("dab,ka,lb->dkl", kernel, cos_y, cos_x) / (PY * PX)
    gains = np.zeros(((HALO + 1) * PY, LANES))
    gains[:, :PX] = spectral.reshape(-1, PX)

    every_x, every_y = np.arange(PX), np.arange(PY)
    forward_x = np.zeros((PX, LANES))
    forward_x[:, :PX] = cas(every_x, every_x, PX)
    high, low = split(forward_x)
    own = slice(HALO, HALO + CX)
    ends = np.r_[0:HALO, HALO + CX : PX]
    into_x = np.zeros((512, LANES))
    into_x[0:128], into_x[128:256], into_x[256:384] = high[own], low[own], high[own]
    into_x[384:400], into_x[400:416], into_x[416:432] = high[ends], low[ends], high[ends]

    high, low = split(cas(every_y, every_y, PY))
    into_y = np.zeros((PY, LANES))
    into_y[:, : 3 * PY] = np.concatenate([high, low, high], axis=1)

    back_x = np.zeros((LANES, CX))
    back_x[:PX] = cas(every_x, every_x[own], PX)
    high, low = split(back_x)
    out_x = np.concatenate([high, low, high], axis=0)
    return {"gains": gains, "into_x": into_x, "into_y": into_y, "out_x": out_x}


def far_tables():
    full_x = cas(np.arange(MX), np.arange(MX), MX)
    full_y = cas(np.arange(MY), np.arange(MY), MY)
    full_z = cas(np.arange(MZ), np.arange(MZ), MZ)

    first_x = np.tile(full_x.reshape(MX, SHARE, KX).transpose(1, 0, 2), (1, 1, 8))
    into_z = np.kron(full_z, np.eye(8))

    def waves(points):
        index = np.arange(points)
        signed = (index + points // 2) % points - points // 2
        laplace = 2.0 - 2.0 * np.cos(2.0 * np.pi / points * index)
        return laplace, (2.0 * np.pi / (points * COARSEN) * signed) ** 2

    (lap_z, wave_z), (lap_y, wave_y), (lap_x, wave_x) = waves(MZ), waves(MY), waves(MX)
    laplace = lap_z[:, None, None] + lap_y[None, :, None] + lap_x[None, None, :]
    wave = wave_z[:, None, None] + wave_y[None, :, None] + wave_x[None, None, :]
    laplace[0, 0, 0] = 1.0
    gain = np.exp(-(SCREEN * SCREEN / 4.0) * wave) / (COARSEN * laplace)
    gain[0, 0, 0] = 0.0
    gain = gain / (MZ * MY * MX)
    gain = gain.reshape(MZ, MY, SHARE, 2, 8).transpose(2, 0, 4, 3, 1).reshape(SHARE, MZ * 8, 2 * MY)

    out_z = np.zeros((2, 2 * BORDER * 8, MZ * 8))
    for g in range(2):
        z = np.concatenate([(2 * g + c) * BZ - 1 + np.arange(BORDER) for c in range(2)]) % MZ
        out_z[g] = np.kron(full_z[z], np.eye(8))

    out_y = np.zeros((GY, MY, 128))
    for g in range(GY):
        out_y[g, :, :BORDER] = full_y[:, (g * BY - 1 + np.arange(BORDER)) % MY]

    def refine(coarse):
        matrix = np.zeros((COARSEN * coarse, coarse + 2))
        for fine in range(COARSEN * coarse):
            below, t = fine // COARSEN, (fine % COARSEN + 0.5) / COARSEN - 0.5
            matrix[fine, below + 1] = 1.0 - abs(t)
            matrix[fine, below if t < 0 else below + 2] = abs(t)
        return matrix

    last_x = np.zeros((GX, MX, CX))
    for g in range(GX):
        last_x[g] = full_x[:, (g * BX - 1 + np.arange(BX + 2)) % MX] @ refine(BX).T
    last_y = np.zeros((BORDER * CY, 128))
    last_y[:, : BORDER * BORDER] = np.kron(np.eye(BORDER), refine(BY))
    return {
        "first_x": first_x,
        "full_y": full_y,
        "into_z": into_z,
        "gain": gain,
        "out_z": out_z,
        "out_y": out_y,
        "last_x": last_x,
        "last_y": last_y,
    }


class Tables:
    def __init__(self):
        self.place, rows, pieces = {}, 0, []
        for name, table in (near_tables() | far_tables()).items():
            count, lanes = table.shape[-2:]
            halves = lanes // 128
            flat = table.reshape(-1, count, halves, 128).swapaxes(1, 2).reshape(-1, 128)
            self.place[name] = rows, count, halves
            rows += flat.shape[0]
            pieces.append(flat)
        self.array = np.zeros((TABLE_ROWS, 128), np.float32)
        self.array[:rows] = np.concatenate(pieces)

    def shape(self, name):
        _, count, halves = self.place[name]
        return pltpu.VMEM((halves, count, 128), f32)

    def copies(self, ref, held, sems, index):
        made = []
        for i, (name, target) in enumerate(held.items()):
            first, count, halves = self.place[name]
            rows = halves * count
            start = first + index.get(name, 0) * rows
            if name in index:
                start = pl.multiple_of(start, 8)
            for half in range(halves):
                source = ref.at[pl.ds(start + half * count, count)]
                made.append(pltpu.make_async_copy(source, target.at[half], sems.at[i]))
        for copy in made:
            copy.start()
        pairs, at = {}, 0
        for name in held:
            halves = self.place[name][2]
            pairs[name] = made[at : at + halves]
            at += halves

        def wait(name):
            for copy in pairs[name]:
                copy.wait()
            target = held[name]
            if len(pairs[name]) == 1:
                return target[0]
            return jnp.concatenate([target[0], target[1]], axis=1)

        return wait


TABLES = Tables()


def dot(a, b):
    return jnp.dot(a, b, preferred_element_type=f32)


def exact_dot(a, b):
    return jnp.dot(a, b, preferred_element_type=f32, precision=HIGHEST)


def halves(x):
    high = x.astype(bf16)
    return high, (x - high.astype(f32)).astype(bf16)


def close_dot(a, b):
    (a, a_low), (b, b_low) = halves(a), halves(b)
    return dot(a, b) + (dot(a, b_low) + dot(a_low, b))


def lane(shape):
    return lax.broadcasted_iota(jnp.int32, shape, len(shape) - 1)


def transposed_dot(a, b):
    return lax.dot_general(a, b, (((0,), (0,)), ((), ())), preferred_element_type=f32, precision=HIGHEST)


def share():
    return lax.axis_index("gx") * 2 + lax.axis_index("core")


def is_even(axis):
    return lax.rem(lax.axis_index(axis), 2) == 0


def charge_kernel(density, out, even, odd):
    parts = []
    for high in range(2):
        planes = []
        for low in range(4):
            z = (high * 4 + low) * COARSEN
            planes.append((density[z] + density[z + 1]) + (density[z + 2] + density[z + 3]))
        parts.append(jnp.concatenate(planes, axis=1))
    rows = jnp.concatenate(parts, axis=0)

    def pool(shape, fine, coarse):
        a = lax.broadcasted_iota(jnp.int32, shape, fine)
        b = lax.broadcasted_iota(jnp.int32, shape, coarse)
        return (a // COARSEN == b).astype(f32)

    rows = exact_dot(rows, pool((4 * CX, 128), 0, 1))
    rows = exact_dot(pool((2 * BY, 2 * CY), 1, 0), rows)
    for peer in range(SHARE):
        out[peer] = rows
    start = jnp.where(is_even("core"), CZ - HALO, 0)
    even[...] = density[pl.ds(start, HALO)]
    odd[...] = density[pl.ds(CZ - HALO - start, HALO)]


def first_kernel(table, charges, out, held, sems):
    wait = TABLES.copies(table, {"first_x": held}, sems, {"first_x": share()})
    peers = charges[...].reshape(GX, 32, 128)
    place = lane((32, 128)) // BX
    blocks = []
    for low in range(4):
        sides = []
        for side in range(2):
            total = None
            for q in range(4):
                shift = (q - low) * BX % 128
                peer = peers[side * 4 + q]
                moved = pltpu.roll(peer, shift, 1) if shift else peer
                total = moved if q == 0 else jnp.where(place == q, moved, total)
            sides.append(total)
        blocks.append(jnp.concatenate(sides, axis=1))
    rows = jnp.concatenate(blocks, axis=0)
    rows = exact_dot(rows, wait("first_x"))
    place = lane((BY, 128)) // KX
    for core in range(2):
        total = None
        for z in range(BZ):
            start = (z % 4) * 32 + core * 16 + (z // 4) * 8
            piece = rows[start : start + 8]
            total = piece if z == 0 else jnp.where(place == z, piece, total)
        for peer in range(2 * GY):
            out[peer, core] = total


def filter_kernel(table, spectrum, out, held_y, held_z, held_g, held_iz, held_iy, sems):
    held = {"full_y": held_y, "into_z": held_z, "gain": held_g, "out_z": held_iz, "out_y": held_iy}
    index = {"gain": share(), "out_z": lax.axis_index("yh"), "out_y": lax.axis_index("gy")}
    wait = TABLES.copies(table, held, sems, index)
    blocks = spectrum[...].reshape(GY, 4, BY, 128)
    full_y = wait("full_y")
    waves = [transposed_dot(blocks[:, b].reshape(MY, 128), full_y) for b in range(4)]
    rows = jnp.concatenate(waves, axis=0).reshape(MZ, 2, 8, MY)
    rows = jnp.concatenate([rows[:, half].reshape(MZ * 8, MY) for half in range(2)], axis=1)
    rows = exact_dot(wait("into_z"), rows)
    rows = rows * wait("gain")
    rows = close_dot(wait("out_z"), rows)
    rows = jnp.concatenate([rows[:, :MY], rows[:, MY:]], axis=0)
    rows = close_dot(rows, wait("out_y"))
    for core in range(2):
        sides = []
        for half in range(2):
            total = None
            for z in range(BORDER):
                start = ((half * 2 + core) * BORDER + z) * 8
                piece = rows[start : start + 8]
                total = piece if z == 0 else total + pltpu.roll(piece, z * BORDER, 1)
            sides.append(total)
        message = jnp.concatenate(sides, axis=0)
        for peer in range(GX):
            out[peer * 2 + core] = message


def far_kernel(table, spectrum, out, held_x, held_y, sems):
    held = {"last_x": held_x, "last_y": held_y}
    wait = TABLES.copies(table, held, sems, {"last_x": lax.axis_index("gx")})
    rows = spectrum[...].reshape(MX, 128)
    field = close_dot(rows.T, wait("last_x"))
    high, low = halves(field)
    refine = wait("last_y").astype(bf16)
    field = dot(refine, high) + dot(refine, low)

    def plane(z):
        return field[z * CY : (z + 1) * CY]

    for block in range(BZ):
        before, here, after = plane(block), plane(block + 1), plane(block + 2)
        for residue in range(COARSEN):
            t = (residue + 0.5) / COARSEN - 0.5
            value = (1.0 - abs(t)) * here + abs(t) * (before if t < 0 else after)
            z = block * COARSEN + residue
            out[z] = value


def edge_y_kernel(density, z_even, z_odd, even, odd):
    lower = is_even("core")
    start = jnp.where(is_even("gy"), CY - HALO, 0)
    for target, first in ((even, start), (odd, CY - HALO - start)):
        rows = pl.ds(pl.multiple_of(first, 8), HALO)
        one, two = z_even[:, rows], z_odd[:, rows]
        target[0:HALO] = jnp.where(lower, two, one)
        target[HALO : HALO + CZ] = density[:, rows]
        target[HALO + CZ : PZ] = jnp.where(lower, one, two)


def edge_x_kernel(table, density, z_even, z_odd, y_even, y_odd, waves, even, odd, padded, held, sems):
    wait = TABLES.copies(table, {"into_y": held}, sems, {})
    lower = is_even("core")
    one, two = z_even[...], z_odd[...]
    middle = slice(HALO, HALO + CY)
    padded[0:HALO, middle] = jnp.where(lower, two, one)
    padded[HALO : HALO + CZ, middle] = density[...]
    padded[HALO + CZ : PZ, middle] = jnp.where(lower, one, two)
    lower = is_even("gy")
    one, two = y_even[...], y_odd[...]
    padded[:, 0:HALO] = jnp.where(lower, two, one)
    padded[:, HALO + CY : PY] = jnp.where(lower, one, two)

    into_y = wait("into_y")[:, : 3 * PY].astype(bf16)
    for z in range(0, PZ, 2):
        high, low = halves(jnp.concatenate([padded[z], padded[z + 1]], axis=1))
        wave = dot(into_y, jnp.concatenate([high, high, low], axis=0))
        waves[z], waves[z + 1] = wave[:, :128], wave[:, 128:]
    flat = waves.reshape(PZ * PY, 128)
    left, right = [], []
    for j in range(PZ * PY // 128):
        turned = flat[j * 128 : (j + 1) * 128].T
        left.append(turned[:HALO])
        right.append(turned[128 - HALO :])
    left, right = jnp.concatenate(left, axis=1), jnp.concatenate(right, axis=1)
    lower = is_even("gx")
    even[...] = jnp.where(lower, right, left)
    odd[...] = jnp.where(lower, left, right)


def near_kernel(
    table, waves, x_even, x_odd, far, out, wave_x, wave_z, held_g, held_ix, held_y, held_ox, sems
):
    held = {"into_x": held_ix, "gains": held_g, "into_y": held_y, "out_x": held_ox}
    wait = TABLES.copies(table, held, sems, {})
    lower = is_even("gx")
    one, two = x_even[...], x_odd[...]
    ends = jnp.concatenate([jnp.where(lower, two, one), jnp.where(lower, one, two)], axis=0)
    high = ends.astype(bf16).astype(f32)
    ends = jnp.concatenate([high, high, ends - high], axis=0)
    into_x = wait("into_x")[:432].astype(bf16)
    flat = waves.reshape(PZ * PY, 128)
    flat_x = wave_x.reshape(PZ * PY, LANES)
    for j in range(18):
        part = slice(j * 128, (j + 1) * 128)
        high, low = halves(flat[part])
        flat_x[part] = dot(jnp.concatenate([high, high, low, ends[:, part].T.astype(bf16)], axis=1), into_x)

    wait("gains")

    @pl.loop(0, PY // 8)
    def _(c):
        for side in range(LANES // 128):
            gain = [
                held_g[side, pl.ds(pl.multiple_of(d * PY + c * 8, 8), 8)] for d in range(HALO + 1)
            ]
            row, column = pl.ds(pl.multiple_of(c * 8, 8), 8), pl.ds(side * 128, 128)
            window = [wave_x[z, row, column] for z in range(2 * HALO)]
            for z in range(CZ):
                window.append(wave_x[z + 2 * HALO, row, column])
                total = gain[0] * window[HALO]
                for d in range(1, HALO + 1):
                    total = total + gain[d] * (window[HALO - d] + window[HALO + d])
                wave_z[z, row, column] = total
                window.pop(0)

    out_y = wait("into_y")[HALO : HALO + CY, : 3 * PY].astype(bf16)
    out_x = wait("out_x").astype(bf16)
    high, low = halves(wave_z[...].reshape(CZ * PY, LANES))
    both = dot(high, jnp.concatenate([out_x[:256], out_x[256:512]], axis=1))
    rows = both[:, :128] + both[:, 128:] + dot(low, out_x[:256])
    for z in range(0, CZ, 2):
        pair = jnp.concatenate([rows[z * PY : (z + 1) * PY], rows[(z + 1) * PY : (z + 2) * PY]], axis=1)
        high, low = halves(pair)
        field = dot(out_y, jnp.concatenate([high, high, low], axis=0))
        out[z] = far[z] + field[:, :128]
        out[z + 1] = far[z + 1] + field[:, 128:]


def call(kernel, outs, arrays=0, tables=(), scratch=(), us=1.0):
    vmem = pl.BlockSpec(memory_space=pltpu.VMEM)
    many = isinstance(outs, list)
    specs = [vmem] * arrays
    scratch = list(scratch)
    if tables:
        specs = [pl.BlockSpec(memory_space=pltpu.HBM)] + specs
        scratch += [TABLES.shape(name) for name in tables]
        scratch.append(pltpu.SemaphoreType.DMA((len(tables),)))
    return pl.pallas_call(
        kernel,
        out_shape=[jax.ShapeDtypeStruct(s, f32) for s in outs] if many else jax.ShapeDtypeStruct(outs, f32),
        in_specs=specs,
        out_specs=[vmem] * len(outs) if many else vmem,
        scratch_shapes=scratch,
        compiler_params=pltpu.CompilerParams(vmem_limit_bytes=VMEM_MIB * 1024 * 1024),
        cost_estimate=pl.CostEstimate(flops=int(us * 1e9), bytes_accessed=int(us * 3e6), transcendentals=0),
        name=kernel.__name__,
    )


def exchange(even, odd, axis):
    peers = lax.axis_size(axis)
    low_first = [(i, i + 1 if i % 2 == 0 else i - 1) for i in range(peers)]
    high_first = [(i, (i + 1 if i % 2 else i - 1) % peers) for i in range(peers)]
    odd = lax.ppermute(odd, axis, high_first)
    return lax.ppermute(even, axis, low_first), odd


def body(density):
    table = jnp.asarray(TABLES.array)
    charges, *z_ends = call(
        charge_kernel, [(SHARE, 16, 128), (HALO, CY, CX), (HALO, CY, CX)], 1, us=1.0
    )(density)
    charges = lax.all_to_all(charges, ("gx", "core"), 0, 0, tiled=True)
    z_ends = exchange(*z_ends, ("yh", "core"))
    spectrum = call(first_kernel, (2 * GY, 2, 8, 128), 1, ["first_x"], us=1.3)(table, charges)
    spectrum = lax.all_to_all(spectrum, ("gy", "yh"), 0, 0, tiled=True)

    y_ends = call(edge_y_kernel, [(PZ, HALO, CX)] * 2, 3, us=10.0)(density, *z_ends)
    spectrum, _ = lax.optimization_barrier((spectrum, y_ends))
    y_ends = exchange(*y_ends, "gy")
    spectrum = call(filter_kernel, (SHARE, KX, 128), 1, ["full_y", "into_z", "gain", "out_z", "out_y"], us=3.0)(
        table, spectrum
    )
    y_ends, _ = lax.optimization_barrier((y_ends, spectrum))
    spectrum = lax.all_to_all(spectrum, ("gx", "core"), 0, 0, tiled=True)
    waves, even, odd = call(
        edge_x_kernel,
        [(PZ, PY, CX), (HALO, PZ * PY), (HALO, PZ * PY)],
        5,
        ["into_y"],
        [pltpu.VMEM((PZ, PY, CX), f32)],
        us=10.0,
    )(table, density, *z_ends, *y_ends)
    x_ends = exchange(even, odd, "gx")
    far = call(far_kernel, (CZ, CY, CX), 1, ["last_x", "last_y"], us=5.0)(table, spectrum)
    return call(
        near_kernel,
        (CZ, CY, CX),
        4,
        ["gains", "into_x", "into_y", "out_x"],
        [pltpu.VMEM((PZ, PY, LANES), f32), pltpu.VMEM((CZ, PY, LANES), f32)],
        us=0.1,
    )(table, waves, *x_ends, far)


def solution(mesh):
    devices = mesh.devices.reshape(GX, GY, 2, 2)
    parts = jax.sharding.Mesh(devices, ("gx", "gy", "yh", "core"))
    placed = P(("yh", "core"), "gy", "gx")
    return jax.shard_map(body, mesh=parts, in_specs=(placed,), out_specs=placed, check_vma=False)
```

```python
import math

import jax
import jax.numpy as jnp
import ml_dtypes
import numpy as np
from jax import lax
from jax.experimental import pallas as pl
from jax.experimental.pallas import tpu as pltpu
from jax.sharding import PartitionSpec as P

HALO = 8
COARSEN = 4
SCREEN = 6.0
SOFTEN = 0.25

NZ, NY, NX = 128, 512, 1024
GZ, GY, GX = 4, 16, 8
CZ, CY, CX = NZ // GZ, NY // GY, NX // GX
MZ, MY, MX = NZ // COARSEN, NY // COARSEN, NX // COARSEN
BZ, BY, BX = MZ // GZ, MY // GY, MX // GX
PZ, PY, PX = CZ + 2 * HALO, CY + 2 * HALO, CX + 2 * HALO
LANES = 256
OWN_US = 1.0
BORDER = BY + 2
SHARE = 2 * GX
KX = MX // SHARE
TAIL = PX - CX
VMEM_MIB = 44
TABLE_ROWS = 24 * 2048

f32 = jnp.float32
bf16 = jnp.bfloat16
HIGHEST = lax.Precision.HIGHEST


def cas(a, b, points):
    angles = 2.0 * np.pi / points * (np.outer(a, b) % points)
    return np.cos(angles) + np.sin(angles)


def split(table):
    high = table.astype(np.float32).astype(ml_dtypes.bfloat16)
    low = (table - high.astype(np.float64)).astype(np.float32).astype(ml_dtypes.bfloat16)
    return high, low


def near_tables():
    reach = np.arange(HALO + 1)
    both = np.arange(-HALO, HALO + 1)
    squared = (
        reach[:, None, None] ** 2 + both[None, :, None] ** 2 + both[None, None, :] ** 2
    ).astype(np.float64)
    erfc = np.vectorize(math.erfc)
    kernel = erfc(np.sqrt(squared) / SCREEN) / (4.0 * math.pi * np.sqrt(squared + SOFTEN))
    cos_y = np.cos(2.0 * np.pi / PY * np.outer(np.arange(PY), both))
    cos_x = np.cos(2.0 * np.pi / PX * np.outer(np.arange(PX), both))
    spectral = np.einsum("dab,ka,lb->dkl", kernel, cos_y, cos_x) / (PY * PX)
    gains = spectral[:, :, :CX].reshape(-1, CX)
    tail_gains = np.zeros((HALO + 1, 8, 128))
    tails = spectral[:, :, CX:].reshape(HALO + 1, PY // 8, 8, TAIL).swapaxes(1, 2)
    tail_gains[:, :, : PY // 8 * TAIL] = tails.reshape(HALO + 1, 8, PY // 8 * TAIL)
    tail_gains = tail_gains.reshape(-1, 128)

    every_x, every_y = np.arange(PX), np.arange(PY)
    spread = np.r_[0:CX, np.tile(np.arange(CX, PX), 8)]
    high, low = split(cas(every_x, spread, PX))
    own = slice(HALO, HALO + CX)
    ends = np.r_[0:HALO, HALO + CX : PX]
    into_x = np.zeros((512, LANES))
    into_x[0:128], into_x[128:256], into_x[256:384] = high[own], low[own], high[own]
    into_x[384:400], into_x[400:416], into_x[416:432] = high[ends], low[ends], high[ends]

    high, low = split(cas(every_y, every_y, PY))
    inner = slice(HALO, HALO + CY)
    into_y = np.zeros((PY, LANES))
    into_y[:, : 3 * PY] = np.concatenate([high, low, high], axis=1)

    high, low = split(cas(spread, every_x[own], PX))
    back_x = np.concatenate([high, low], axis=1)
    return {
        "gains": gains,
        "tail_gains": tail_gains,
        "into_x": into_x,
        "into_y": into_y,
        "back_y": into_y[inner],
        "back_x": back_x,
    }


def far_tables():
    full_x = cas(np.arange(MX), np.arange(MX), MX)
    full_y = cas(np.arange(MY), np.arange(MY), MY)
    full_z = cas(np.arange(MZ), np.arange(MZ), MZ)

    first_x = np.tile(full_x.reshape(MX, SHARE, KX).transpose(1, 0, 2), (1, 1, 8))
    into_z = np.kron(full_z, np.eye(8))

    def waves(points):
        index = np.arange(points)
        signed = (index + points // 2) % points - points // 2
        laplace = 2.0 - 2.0 * np.cos(2.0 * np.pi / points * index)
        return laplace, (2.0 * np.pi / (points * COARSEN) * signed) ** 2

    (lap_z, wave_z), (lap_y, wave_y), (lap_x, wave_x) = waves(MZ), waves(MY), waves(MX)
    laplace = lap_z[:, None, None] + lap_y[None, :, None] + lap_x[None, None, :]
    wave = wave_z[:, None, None] + wave_y[None, :, None] + wave_x[None, None, :]
    laplace[0, 0, 0] = 1.0
    gain = np.exp(-(SCREEN * SCREEN / 4.0) * wave) / (COARSEN * laplace)
    gain[0, 0, 0] = 0.0
    gain = gain / (MZ * MY * MX)
    gain = gain.reshape(MZ, MY, SHARE, 2, 8).transpose(2, 0, 4, 3, 1).reshape(SHARE, MZ * 8, 2 * MY)

    out_z = np.zeros((2, 2 * BORDER * 8, MZ * 8))
    for g in range(2):
        z = np.concatenate([(2 * g + c) * BZ - 1 + np.arange(BORDER) for c in range(2)]) % MZ
        out_z[g] = np.kron(full_z[z], np.eye(8))

    out_y = np.zeros((GY, MY, 128))
    for g in range(GY):
        out_y[g, :, :BORDER] = full_y[:, (g * BY - 1 + np.arange(BORDER)) % MY]

    def refine(coarse):
        matrix = np.zeros((COARSEN * coarse, coarse + 2))
        for fine in range(COARSEN * coarse):
            below, t = fine // COARSEN, (fine % COARSEN + 0.5) / COARSEN - 0.5
            matrix[fine, below + 1] = 1.0 - abs(t)
            matrix[fine, below if t < 0 else below + 2] = abs(t)
        return matrix

    last_x = np.zeros((GX, MX, CX))
    for g in range(GX):
        last_x[g] = full_x[:, (g * BX - 1 + np.arange(BX + 2)) % MX] @ refine(BX).T
    last_y = np.zeros((BORDER * CY, 128))
    last_y[:, : BORDER * BORDER] = np.kron(np.eye(BORDER), refine(BY))
    return {
        "first_x": first_x,
        "full_y": full_y,
        "into_z": into_z,
        "gain": gain,
        "out_z": out_z,
        "out_y": out_y,
        "last_x": last_x,
        "last_y": last_y,
    }


class Tables:
    def __init__(self):
        self.place, rows, pieces = {}, 0, []
        for name, table in (near_tables() | far_tables()).items():
            count, lanes = table.shape[-2:]
            halves = lanes // 128
            flat = table.reshape(-1, count, halves, 128).swapaxes(1, 2).reshape(-1, 128)
            self.place[name] = rows, count, halves
            rows += flat.shape[0]
            pieces.append(flat)
        self.array = np.zeros((TABLE_ROWS, 128), np.float32)
        self.array[:rows] = np.concatenate(pieces)

    def shape(self, name):
        _, count, halves = self.place[name]
        return halves * count, 128

    def copy(self, ref, name, held, sem, part=None):
        first, count, halves = self.place[name]
        rows = halves * count
        start = first if part is None else pl.multiple_of(first + part * rows, 8)
        return pltpu.make_async_copy(ref.at[pl.ds(start, rows)], held, sem)

    def height(self, names):
        return sum(self.shape(name)[0] for name in names)

    def rows(self, held, names, name):
        return held.at[pl.ds(self.height(names[: names.index(name)]), self.shape(name)[0])]

    def reader(self, held, names):
        def get(name):
            _, count, halves = self.place[name]
            rows = self.rows(held, names, name)
            if halves == 1:
                return rows[...]
            return jnp.concatenate([rows[0:count], rows[count : 2 * count]], axis=1)

        return get

    def fetch(self, ref, held, names, sems, part={}):
        copies = {
            name: self.copy(ref, name, self.rows(held, names, name), sems.at[i], part.get(name))
            for i, name in enumerate(names)
        }
        for copy in copies.values():
            copy.start()
        get = self.reader(held, names)

        def wait(name):
            copies[name].wait()
            return get(name)

        return wait


FILTER = ["full_y", "into_z", "gain", "out_z", "out_y"]
NEAR = ["gains", "tail_gains", "into_x", "back_y", "back_x"]
TABLES = Tables()


def dot(a, b):
    return jnp.dot(a, b, preferred_element_type=f32)


def exact_dot(a, b):
    return jnp.dot(a, b, preferred_element_type=f32, precision=HIGHEST)


def halves(x):
    high = x.astype(bf16)
    return high, (x - high.astype(f32)).astype(bf16)


def close_dot(a, b):
    (a, a_low), (b, b_low) = halves(a), halves(b)
    return dot(a, b) + (dot(a, b_low) + dot(a_low, b))


def lane(shape):
    return lax.broadcasted_iota(jnp.int32, shape, len(shape) - 1)


def transposed_dot(a, b):
    return lax.dot_general(a, b, (((0,), (0,)), ((), ())), preferred_element_type=f32, precision=HIGHEST)


def share():
    return lax.axis_index("gx") * 2 + lax.axis_index("core")


def is_even(axis):
    return lax.rem(lax.axis_index(axis), 2) == 0


def send(held, out, sems):
    count = held.shape[0]
    copies = [
        pltpu.make_async_copy(held, out.at[pl.ds(i * count, count)], sems.at[i])
        for i in range(out.shape[0] // count)
    ]
    for copy in copies:
        copy.start()

    def wait():
        for copy in copies:
            copy.wait()

    return wait


def charge_kernel(density, out, even, odd, message, sems):
    parts = []
    for high in range(2):
        planes = []
        for low in range(4):
            z = (high * 4 + low) * COARSEN
            planes.append((density[z] + density[z + 1]) + (density[z + 2] + density[z + 3]))
        parts.append(jnp.concatenate(planes, axis=1))
    rows = jnp.concatenate(parts, axis=0)

    def pool(shape, fine, coarse):
        a = lax.broadcasted_iota(jnp.int32, shape, fine)
        b = lax.broadcasted_iota(jnp.int32, shape, coarse)
        return (a // COARSEN == b).astype(f32)

    rows = exact_dot(rows, pool((4 * CX, 128), 0, 1))
    rows = exact_dot(pool((2 * BY, 2 * CY), 1, 0), rows)
    for copy in range(4):
        message[copy] = rows
    wait = send(message, out, sems)
    start = jnp.where(is_even("core"), CZ - HALO, 0)
    even[...] = density[pl.ds(start, HALO)]
    odd[...] = density[pl.ds(CZ - HALO - start, HALO)]
    wait()


def first_kernel(table, charges, out, held, message, sem, sems):
    copy = TABLES.copy(table, "first_x", held, sem, share())
    copy.start()
    peers = charges[...].reshape(GX, 32, 128)
    place = lane((32, 128)) // BX
    blocks = []
    for low in range(4):
        sides = []
        for side in range(2):
            total = None
            for q in range(4):
                shift = (q - low) * BX % 128
                peer = peers[side * 4 + q]
                moved = pltpu.roll(peer, shift, 1) if shift else peer
                total = moved if q == 0 else jnp.where(place == q, moved, total)
            sides.append(total)
        blocks.append(jnp.concatenate(sides, axis=1))
    rows = jnp.concatenate(blocks, axis=0)
    copy.wait()
    rows = exact_dot(rows, held[...])
    place = lane((BY, 128)) // KX
    for core in range(2):
        total = None
        for z in range(BZ):
            start = (z % 4) * 32 + core * 16 + (z // 4) * 8
            piece = rows[start : start + 8]
            total = piece if z == 0 else jnp.where(place == z, piece, total)
        for copy in range(8):
            message[copy, core] = total
    send(message, out, sems)()


def filter_kernel(held, spectrum, out, message, sems):
    blocks = spectrum[...].reshape(GY, 4, BY, 128)
    get = TABLES.reader(held, FILTER)
    full_y = get("full_y")
    waves = [transposed_dot(blocks[:, b].reshape(MY, 128), full_y) for b in range(4)]
    rows = jnp.concatenate(waves, axis=0).reshape(MZ, 2, 8, MY)
    rows = jnp.concatenate([rows[:, half].reshape(MZ * 8, MY) for half in range(2)], axis=1)
    rows = exact_dot(get("into_z"), rows)
    rows = rows * get("gain")
    rows = close_dot(get("out_z"), rows)
    rows = jnp.concatenate([rows[:, :MY], rows[:, MY:]], axis=0)
    rows = close_dot(rows, get("out_y"))
    for core in range(2):
        sides = []
        for half in range(2):
            total = None
            for z in range(BORDER):
                start = ((half * 2 + core) * BORDER + z) * 8
                piece = rows[start : start + 8]
                total = piece if z == 0 else total + pltpu.roll(piece, z * BORDER, 1)
            sides.append(total)
        rows_out = jnp.concatenate(sides, axis=0)
        for copy in range(2):
            message[copy * 2 + core] = rows_out
    send(message, out, sems)()


def far_kernel(table, spectrum, out, for_near, held, sems, more):
    wait = TABLES.fetch(table, held, ["last_x", "last_y"], sems, {"last_x": lax.axis_index("gx")})
    wait_near = TABLES.fetch(table, for_near, NEAR, more)
    rows = spectrum[...].reshape(MX, 128)
    field = close_dot(rows.T, wait("last_x"))
    high, low = halves(field)
    refine = wait("last_y").astype(bf16)
    field = dot(refine, high) + dot(refine, low)

    def plane(z):
        return field[z * CY : (z + 1) * CY]

    for block in range(BZ):
        before, here, after = plane(block), plane(block + 1), plane(block + 2)
        for residue in range(COARSEN):
            t = (residue + 0.5) / COARSEN - 0.5
            value = (1.0 - abs(t)) * here + abs(t) * (before if t < 0 else after)
            z = block * COARSEN + residue
            out[z] = value
    for name in NEAR:
        wait_near(name)


def edge_y_kernel(table, density, z_even, z_odd, even, odd, planes, for_filter, sems):
    part = {"gain": share(), "out_z": lax.axis_index("yh"), "out_y": lax.axis_index("gy")}
    wait = TABLES.fetch(table, for_filter, FILTER, sems, part)
    lower = is_even("core")
    one, two = z_even[...], z_odd[...]
    planes[0:HALO] = jnp.where(lower, two, one)
    planes[HALO : HALO + CZ] = density[...]
    planes[HALO + CZ : PZ] = jnp.where(lower, one, two)
    start = jnp.where(is_even("gy"), CY - HALO, 0)
    even[...] = planes[:, pl.ds(pl.multiple_of(start, 8), HALO)]
    odd[...] = planes[:, pl.ds(pl.multiple_of(CY - HALO - start, 8), HALO)]
    for name in FILTER:
        wait(name)


def edge_x_kernel(table, planes, y_even, y_odd, waves, even, odd, padded, held, sems):
    wait = TABLES.fetch(table, held, ["into_y"], sems)
    padded[:, HALO : HALO + CY] = planes[...]
    lower = is_even("gy")
    one, two = y_even[...], y_odd[...]
    padded[:, 0:HALO] = jnp.where(lower, two, one)
    padded[:, HALO + CY : PY] = jnp.where(lower, one, two)

    into_y = wait("into_y")[:, : 3 * PY].astype(bf16)
    for z in range(0, PZ, 2):
        high, low = halves(jnp.concatenate([padded[z], padded[z + 1]], axis=1))
        wave = dot(into_y, jnp.concatenate([high, high, low], axis=0))
        waves[z], waves[z + 1] = wave[:, :128], wave[:, 128:]
    flat = waves.reshape(PZ * PY, 128)
    left, right = [], []
    for j in range(PZ * PY // 128):
        turned = flat[j * 128 : (j + 1) * 128].T
        left.append(turned[:HALO])
        right.append(turned[128 - HALO :])
    left, right = jnp.concatenate(left, axis=1), jnp.concatenate(right, axis=1)
    lower = is_even("gx")
    even[...] = jnp.where(lower, right, left)
    odd[...] = jnp.where(lower, left, right)


def sum_planes(gain, load, store):
    window = [load(z) for z in range(2 * HALO)]
    for z in range(CZ):
        window.append(load(z + 2 * HALO))
        total = gain[0] * window[HALO]
        for d in range(1, HALO + 1):
            total = total + gain[d] * (window[HALO - d] + window[HALO + d])
        store(z, total)
        window.pop(0)


def near_kernel(
    held, waves, x_even, x_odd, far, out, wave_x, tails, sums, tail_sums, field, sems
):
    get = TABLES.reader(held, NEAR)
    lower = is_even("gx")
    one, two = x_even[...], x_odd[...]
    ends = jnp.concatenate([jnp.where(lower, two, one), jnp.where(lower, one, two)], axis=0)
    high = ends.astype(bf16).astype(f32)
    ends = jnp.concatenate([high, high, ends - high], axis=0)
    weights = get("into_x")[:432].astype(bf16)
    flat, flat_x = waves.reshape(PZ * PY, 128), wave_x.reshape(PZ * PY, 128)
    tile = lane((8, 128)) // TAIL
    planes = {}
    for j in range(18):
        part = slice(j * 128, (j + 1) * 128)
        high, low = halves(flat[part])
        wave = dot(jnp.concatenate([high, high, low, ends[:, part].T.astype(bf16)], axis=1), weights)
        flat_x[part] = wave[:, :128]
        for i in range(16):
            z, t = divmod(16 * j + i, PY // 8)
            piece = wave[8 * i : 8 * i + 8, 128:]
            planes[z] = piece if t == 0 else jnp.where(tile == t, piece, planes[z])
            if t == PY // 8 - 1:
                tails[z] = planes.pop(z)

    def store_tail(z, value):
        tail_sums[z] = value

    gains, tail_gains = (TABLES.rows(held, NEAR, name) for name in ("gains", "tail_gains"))
    sum_planes([tail_gains[d * 8 : d * 8 + 8] for d in range(HALO + 1)], lambda z: tails[z], store_tail)

    @pl.loop(0, PY // 8)
    def _(c):
        row = pl.ds(pl.multiple_of(c * 8, 8), 8)

        def store(z, value):
            sums[z, row] = value

        sum_planes(
            [gains[pl.ds(pl.multiple_of(d * PY + c * 8, 8), 8)] for d in range(HALO + 1)],
            lambda z: wave_x[z, row],
            store,
        )

    to_y = get("back_y")[:, : 3 * PY].astype(bf16)
    to_x = get("back_x").astype(bf16)
    rows = []
    for z in range(CZ):
        tail = tail_sums[z]
        tail = jnp.concatenate([jnp.where(tile == t, tail, 0.0) for t in range(PY // 8)], axis=0)
        rows.append(jnp.concatenate([sums[z], tail], axis=1))
    high, low = halves(jnp.concatenate(rows, axis=0))
    both = dot(high, to_x)
    rows = both[:, :128] + both[:, 128:] + dot(low, to_x[:, :128])
    copies = []
    for z in range(0, CZ, 2):
        pair = jnp.concatenate([rows[z * PY : (z + 1) * PY], rows[(z + 1) * PY : (z + 2) * PY]], axis=1)
        high, low = halves(pair)
        cells = dot(to_y, jnp.concatenate([high, high, low], axis=0))
        field[z] = far[z] + cells[:, :128]
        field[z + 1] = far[z + 1] + cells[:, 128:]
        if z % 8 == 6:
            part = pl.ds(z - 6, 8)
            copies.append(pltpu.make_async_copy(field.at[part], out.at[part], sems.at[z // 8]))
            copies[-1].start()
    for copy in copies:
        copy.wait()


def call(kernel, outs, arrays=0, table=False, sent=0, scratch=(), us=1.0):
    vmem, hbm = pl.BlockSpec(memory_space=pltpu.VMEM), pl.BlockSpec(memory_space=pltpu.HBM)
    many = isinstance(outs, list)
    specs = [hbm] * table + [vmem] * arrays
    return pl.pallas_call(
        kernel,
        out_shape=[jax.ShapeDtypeStruct(s, f32) for s in outs] if many else jax.ShapeDtypeStruct(outs, f32),
        in_specs=specs,
        out_specs=[hbm] * sent + [vmem] * (len(outs) - sent) if many else hbm if sent else vmem,
        scratch_shapes=list(scratch),
        compiler_params=pltpu.CompilerParams(vmem_limit_bytes=VMEM_MIB * 1024 * 1024),
        cost_estimate=pl.CostEstimate(flops=int(us * 1e9), bytes_accessed=int(us * 3e6), transcendentals=0),
        name=kernel.__name__,
    )


def exchange(even, odd, axis):
    peers = lax.axis_size(axis)
    low_first = [(i, i + 1 if i % 2 == 0 else i - 1) for i in range(peers)]
    high_first = [(i, (i + 1 if i % 2 else i - 1) % peers) for i in range(peers)]
    odd = lax.ppermute(odd, axis, high_first)
    return lax.ppermute(even, axis, low_first), odd


def body(density):
    dma, vmem = pltpu.SemaphoreType.DMA, pltpu.VMEM
    table = jnp.asarray(TABLES.array)
    charges, *z_ends = call(
        charge_kernel,
        [(SHARE, 16, 128), (HALO, CY, CX), (HALO, CY, CX)],
        1,
        sent=1,
        scratch=[vmem((4, 16, 128), f32), dma((4,))],
    )(density)
    charges = lax.all_to_all(charges, ("gx", "core"), 0, 0, tiled=True)
    z_ends = exchange(*z_ends, ("yh", "core"))
    spectrum = call(
        first_kernel,
        (2 * GY, 2, 8, 128),
        1,
        table=True,
        sent=1,
        scratch=[vmem((MX, 128), f32), vmem((8, 2, 8, 128), f32), dma, dma((4,))],
        us=1.3,
    )(table, charges)
    spectrum = lax.all_to_all(spectrum, ("gy", "yh"), 0, 0, tiled=True)

    *y_ends, planes, for_filter = call(
        edge_y_kernel,
        [(PZ, HALO, CX), (PZ, HALO, CX), (PZ, CY, CX), (TABLES.height(FILTER), 128)],
        3,
        table=True,
        scratch=[dma((len(FILTER),))],
        us=10.0,
    )(table, density, *z_ends)
    spectrum, _ = lax.optimization_barrier((spectrum, y_ends))
    y_ends = exchange(*y_ends, "gy")
    spectrum = call(
        filter_kernel, (SHARE, KX, 128), 2, sent=1, scratch=[vmem((4, KX, 128), f32), dma((4,))], us=3.0
    )(for_filter, spectrum)
    y_ends, _ = lax.optimization_barrier((y_ends, spectrum))
    spectrum = lax.all_to_all(spectrum, ("gx", "core"), 0, 0, tiled=True)
    waves, even, odd = call(
        edge_x_kernel,
        [(PZ, PY, CX), (HALO, PZ * PY), (HALO, PZ * PY)],
        3,
        table=True,
        scratch=[vmem((PZ, PY, CX), f32), vmem(TABLES.shape("into_y"), f32), dma((1,))],
        us=10.0,
    )(table, planes, *y_ends)
    x_ends = exchange(even, odd, "gx")
    far, for_near = call(
        far_kernel,
        [(CZ, CY, CX), (TABLES.height(NEAR), 128)],
        1,
        table=True,
        scratch=[vmem((TABLES.height(["last_x", "last_y"]), 128), f32), dma((2,)), dma((len(NEAR),))],
        us=5.0,
    )(table, spectrum)
    return call(
        near_kernel,
        (CZ, CY, CX),
        5,
        sent=1,
        scratch=[
            vmem((PZ, PY, 128), f32),
            vmem((PZ, 8, 128), f32),
            vmem((CZ, PY, 128), f32),
            vmem((CZ, 8, 128), f32),
            vmem((CZ, CY, CX), f32),
            dma((4,)),
        ],
        us=0.1,
    )(for_near, waves, *x_ends, far)


def solution(mesh):
    devices = mesh.devices.reshape(GX, GY, 2, 2)
    parts = jax.sharding.Mesh(devices, ("gx", "gy", "yh", "core"))
    placed = P(("yh", "core"), "gy", "gx")
    return jax.shard_map(body, mesh=parts, in_specs=(placed,), out_specs=placed, check_vma=False)
```

```python
import math

import jax
import jax.numpy as jnp
import ml_dtypes
import numpy as np
from jax import lax
from jax.experimental import pallas as pl
from jax.experimental.pallas import tpu as pltpu
from jax.sharding import PartitionSpec as P

HALO = 8
COARSEN = 4
SCREEN = 6.0
SOFTEN = 0.25

NZ, NY, NX = 128, 512, 1024
GZ, GY, GX = 4, 16, 8
CZ, CY, CX = NZ // GZ, NY // GY, NX // GX
MZ, MY, MX = NZ // COARSEN, NY // COARSEN, NX // COARSEN
BZ, BY, BX = MZ // GZ, MY // GY, MX // GX
PZ, PY, PX = CZ + 2 * HALO, CY + 2 * HALO, CX + 2 * HALO
LANES = 256
OWN_US = 1.0
BORDER = BY + 2
SHARE = 2 * GX
KX = MX // SHARE
TAIL = PX - CX
VMEM_MIB = 44
TABLE_ROWS = 24 * 2048

f32 = jnp.float32
bf16 = jnp.bfloat16
HIGHEST = lax.Precision.HIGHEST


def cas(a, b, points):
    angles = 2.0 * np.pi / points * (np.outer(a, b) % points)
    return np.cos(angles) + np.sin(angles)


def split(table):
    high = table.astype(np.float32).astype(ml_dtypes.bfloat16)
    low = (table - high.astype(np.float64)).astype(np.float32).astype(ml_dtypes.bfloat16)
    return high, low


def near_tables():
    reach = np.arange(HALO + 1)
    both = np.arange(-HALO, HALO + 1)
    squared = (
        reach[:, None, None] ** 2 + both[None, :, None] ** 2 + both[None, None, :] ** 2
    ).astype(np.float64)
    erfc = np.vectorize(math.erfc)
    kernel = erfc(np.sqrt(squared) / SCREEN) / (4.0 * math.pi * np.sqrt(squared + SOFTEN))
    cos_y = np.cos(2.0 * np.pi / PY * np.outer(np.arange(PY), both))
    cos_x = np.cos(2.0 * np.pi / PX * np.outer(np.arange(PX), both))
    spectral = np.einsum("dab,ka,lb->dkl", kernel, cos_y, cos_x) / (PY * PX)
    gains = spectral[:, :, :CX].reshape(-1, CX)
    tail_gains = np.zeros((HALO + 1, 8, 128))
    tails = spectral[:, :, CX:].reshape(HALO + 1, PY // 8, 8, TAIL).swapaxes(1, 2)
    tail_gains[:, :, : PY // 8 * TAIL] = tails.reshape(HALO + 1, 8, PY // 8 * TAIL)
    tail_gains = tail_gains.reshape(-1, 128)

    every_x, every_y = np.arange(PX), np.arange(PY)
    spread = np.r_[0:CX, np.tile(np.arange(CX, PX), 8)]
    high, low = split(cas(every_x, spread, PX))
    own = slice(HALO, HALO + CX)
    ends = np.r_[0:HALO, HALO + CX : PX]
    into_x = np.zeros((512, LANES))
    into_x[0:128], into_x[128:256], into_x[256:384] = high[own], low[own], high[own]
    into_x[384:400], into_x[400:416], into_x[416:432] = high[ends], low[ends], high[ends]

    high, low = split(cas(every_y, every_y, PY))
    inner = slice(HALO, HALO + CY)
    into_y = np.zeros((PY, LANES))
    into_y[:, : 3 * PY] = np.concatenate([high, low, high], axis=1)

    high, low = split(cas(spread, every_x[own], PX))
    back_x = np.concatenate([high, low], axis=1)
    return {
        "gains": gains,
        "tail_gains": tail_gains,
        "into_x": into_x,
        "into_y": into_y,
        "back_y": into_y[inner],
        "back_x": back_x,
    }


def far_tables():
    full_x = cas(np.arange(MX), np.arange(MX), MX)
    full_y = cas(np.arange(MY), np.arange(MY), MY)
    full_z = cas(np.arange(MZ), np.arange(MZ), MZ)

    first_x = np.tile(full_x.reshape(MX, SHARE, KX).transpose(1, 0, 2), (1, 1, 8))
    into_z = np.kron(full_z, np.eye(8))

    def waves(points):
        index = np.arange(points)
        signed = (index + points // 2) % points - points // 2
        laplace = 2.0 - 2.0 * np.cos(2.0 * np.pi / points * index)
        return laplace, (2.0 * np.pi / (points * COARSEN) * signed) ** 2

    (lap_z, wave_z), (lap_y, wave_y), (lap_x, wave_x) = waves(MZ), waves(MY), waves(MX)
    laplace = lap_z[:, None, None] + lap_y[None, :, None] + lap_x[None, None, :]
    wave = wave_z[:, None, None] + wave_y[None, :, None] + wave_x[None, None, :]
    laplace[0, 0, 0] = 1.0
    gain = np.exp(-(SCREEN * SCREEN / 4.0) * wave) / (COARSEN * laplace)
    gain[0, 0, 0] = 0.0
    gain = gain / (MZ * MY * MX)
    gain = gain.reshape(MZ, MY, SHARE, 2, 8).transpose(2, 0, 4, 3, 1).reshape(SHARE, MZ * 8, 2 * MY)

    out_z = np.zeros((2, 2 * BORDER * 8, MZ * 8))
    for g in range(2):
        z = np.concatenate([(2 * g + c) * BZ - 1 + np.arange(BORDER) for c in range(2)]) % MZ
        out_z[g] = np.kron(full_z[z], np.eye(8))

    out_y = np.zeros((GY, MY, 128))
    for g in range(GY):
        out_y[g, :, :BORDER] = full_y[:, (g * BY - 1 + np.arange(BORDER)) % MY]

    def refine(coarse):
        matrix = np.zeros((COARSEN * coarse, coarse + 2))
        for fine in range(COARSEN * coarse):
            below, t = fine // COARSEN, (fine % COARSEN + 0.5) / COARSEN - 0.5
            matrix[fine, below + 1] = 1.0 - abs(t)
            matrix[fine, below if t < 0 else below + 2] = abs(t)
        return matrix

    last_x = np.zeros((GX, MX, CX))
    for g in range(GX):
        last_x[g] = full_x[:, (g * BX - 1 + np.arange(BX + 2)) % MX] @ refine(BX).T
    last_y = np.zeros((BORDER * CY, 128))
    last_y[:, : BORDER * BORDER] = np.kron(np.eye(BORDER), refine(BY))
    return {
        "first_x": first_x,
        "full_y": full_y,
        "into_z": into_z,
        "gain": gain,
        "out_z": out_z,
        "out_y": out_y,
        "last_x": last_x,
        "last_y": last_y,
    }


class Tables:
    def __init__(self):
        self.place, rows, pieces = {}, 0, []
        for name, table in (near_tables() | far_tables()).items():
            count, lanes = table.shape[-2:]
            halves = lanes // 128
            flat = table.reshape(-1, count, halves, 128).swapaxes(1, 2).reshape(-1, 128)
            self.place[name] = rows, count, halves
            rows += flat.shape[0]
            pieces.append(flat)
        self.array = np.zeros((TABLE_ROWS, 128), np.float32)
        self.array[:rows] = np.concatenate(pieces)

    def shape(self, name):
        _, count, halves = self.place[name]
        return halves * count, 128

    def copy(self, ref, name, held, sem, part=None):
        first, count, halves = self.place[name]
        rows = halves * count
        start = first if part is None else pl.multiple_of(first + part * rows, 8)
        return pltpu.make_async_copy(ref.at[pl.ds(start, rows)], held, sem)

    def height(self, names):
        return sum(self.shape(name)[0] for name in names)

    def rows(self, held, names, name):
        return held.at[pl.ds(self.height(names[: names.index(name)]), self.shape(name)[0])]

    def reader(self, held, names):
        def get(name):
            _, count, halves = self.place[name]
            rows = self.rows(held, names, name)
            if halves == 1:
                return rows[...]
            return jnp.concatenate([rows[0:count], rows[count : 2 * count]], axis=1)

        return get

    def fetch(self, ref, held, names, sems, part={}):
        copies = {
            name: self.copy(ref, name, self.rows(held, names, name), sems.at[i], part.get(name))
            for i, name in enumerate(names)
        }
        for copy in copies.values():
            copy.start()
        get = self.reader(held, names)

        def wait(name):
            copies[name].wait()
            return get(name)

        return wait


FILTER = ["full_y", "into_z", "gain", "out_z", "out_y"]
NEAR = ["gains", "tail_gains", "into_x", "back_y", "back_x"]
TABLES = Tables()


def dot(a, b):
    return jnp.dot(a, b, preferred_element_type=f32)


def exact_dot(a, b):
    return jnp.dot(a, b, preferred_element_type=f32, precision=HIGHEST)


def halves(x):
    high = x.astype(bf16)
    return high, (x - high.astype(f32)).astype(bf16)


def close_dot(a, b):
    (a, a_low), (b, b_low) = halves(a), halves(b)
    return dot(a, b) + (dot(a, b_low) + dot(a_low, b))


def lane(shape):
    return lax.broadcasted_iota(jnp.int32, shape, len(shape) - 1)


def transposed_dot(a, b):
    return lax.dot_general(a, b, (((0,), (0,)), ((), ())), preferred_element_type=f32, precision=HIGHEST)


def share():
    return lax.axis_index("gx") * 2 + lax.axis_index("core")


def is_even(axis):
    return lax.rem(lax.axis_index(axis), 2) == 0


def send(held, out, sems):
    count = held.shape[0]
    copies = [
        pltpu.make_async_copy(held, out.at[pl.ds(i * count, count)], sems.at[i])
        for i in range(out.shape[0] // count)
    ]
    for copy in copies:
        copy.start()

    def wait():
        for copy in copies:
            copy.wait()

    return wait


def charge_kernel(table, density, out, even, odd, first_x, message, sems, more):
    wait_first = TABLES.fetch(table, first_x, ["first_x"], more, {"first_x": share()})
    parts = []
    for high in range(2):
        planes = []
        for low in range(4):
            z = (high * 4 + low) * COARSEN
            planes.append((density[z] + density[z + 1]) + (density[z + 2] + density[z + 3]))
        parts.append(jnp.concatenate(planes, axis=1))
    rows = jnp.concatenate(parts, axis=0)

    def pool(shape, fine, coarse):
        a = lax.broadcasted_iota(jnp.int32, shape, fine)
        b = lax.broadcasted_iota(jnp.int32, shape, coarse)
        return (a // COARSEN == b).astype(f32)

    rows = exact_dot(rows, pool((4 * CX, 128), 0, 1))
    rows = exact_dot(pool((2 * BY, 2 * CY), 1, 0), rows)
    for copy in range(4):
        message[copy] = rows
    wait = send(message, out, sems)
    start = jnp.where(is_even("core"), CZ - HALO, 0)
    even[...] = density[pl.ds(start, HALO)]
    odd[...] = density[pl.ds(CZ - HALO - start, HALO)]
    wait_first("first_x")
    wait()


def first_kernel(first_x, charges, out, message, sems):
    peers = charges[...].reshape(GX, 32, 128)
    place = lane((32, 128)) // BX
    blocks = []
    for low in range(4):
        sides = []
        for side in range(2):
            total = None
            for q in range(4):
                shift = (q - low) * BX % 128
                peer = peers[side * 4 + q]
                moved = pltpu.roll(peer, shift, 1) if shift else peer
                total = moved if q == 0 else jnp.where(place == q, moved, total)
            sides.append(total)
        blocks.append(jnp.concatenate(sides, axis=1))
    rows = jnp.concatenate(blocks, axis=0)
    rows = exact_dot(rows, first_x[...])
    place = lane((BY, 128)) // KX
    for core in range(2):
        total = None
        for z in range(BZ):
            start = (z % 4) * 32 + core * 16 + (z // 4) * 8
            piece = rows[start : start + 8]
            total = piece if z == 0 else jnp.where(place == z, piece, total)
        for copy in range(8):
            message[copy, core] = total
    send(message, out, sems)()


def filter_kernel(held, spectrum, out, message, sems):
    blocks = spectrum[...].reshape(GY, 4, BY, 128)
    get = TABLES.reader(held, FILTER)
    full_y = get("full_y")
    waves = [transposed_dot(blocks[:, b].reshape(MY, 128), full_y) for b in range(4)]
    rows = jnp.concatenate(waves, axis=0).reshape(MZ, 2, 8, MY)
    rows = jnp.concatenate([rows[:, half].reshape(MZ * 8, MY) for half in range(2)], axis=1)
    rows = exact_dot(get("into_z"), rows)
    rows = rows * get("gain")
    rows = close_dot(get("out_z"), rows)
    rows = jnp.concatenate([rows[:, :MY], rows[:, MY:]], axis=0)
    rows = close_dot(rows, get("out_y"))
    for core in range(2):
        sides = []
        for half in range(2):
            total = None
            for z in range(BORDER):
                start = ((half * 2 + core) * BORDER + z) * 8
                piece = rows[start : start + 8]
                total = piece if z == 0 else total + pltpu.roll(piece, z * BORDER, 1)
            sides.append(total)
        rows_out = jnp.concatenate(sides, axis=0)
        for copy in range(2):
            message[copy * 2 + core] = rows_out
    send(message, out, sems)()


def far_kernel(table, spectrum, out, for_near, held, sems, more):
    wait = TABLES.fetch(table, held, ["last_x", "last_y"], sems, {"last_x": lax.axis_index("gx")})
    wait_near = TABLES.fetch(table, for_near, NEAR, more)
    rows = spectrum[...].reshape(MX, 128)
    field = close_dot(rows.T, wait("last_x"))
    high, low = halves(field)
    refine = wait("last_y").astype(bf16)
    field = dot(refine, high) + dot(refine, low)

    def plane(z):
        return field[z * CY : (z + 1) * CY]

    for block in range(BZ):
        before, here, after = plane(block), plane(block + 1), plane(block + 2)
        for residue in range(COARSEN):
            t = (residue + 0.5) / COARSEN - 0.5
            value = (1.0 - abs(t)) * here + abs(t) * (before if t < 0 else after)
            z = block * COARSEN + residue
            out[z] = value
    for name in NEAR:
        wait_near(name)


def edge_y_kernel(table, density, z_even, z_odd, even, odd, planes, for_filter, sems):
    part = {"gain": share(), "out_z": lax.axis_index("yh"), "out_y": lax.axis_index("gy")}
    wait = TABLES.fetch(table, for_filter, FILTER, sems, part)
    lower = is_even("core")
    one, two = z_even[...], z_odd[...]
    planes[0:HALO] = jnp.where(lower, two, one)
    planes[HALO : HALO + CZ] = density[...]
    planes[HALO + CZ : PZ] = jnp.where(lower, one, two)
    start = jnp.where(is_even("gy"), CY - HALO, 0)
    even[...] = planes[:, pl.ds(pl.multiple_of(start, 8), HALO)]
    odd[...] = planes[:, pl.ds(pl.multiple_of(CY - HALO - start, 8), HALO)]
    for name in FILTER:
        wait(name)


def edge_x_kernel(table, planes, y_even, y_odd, waves, even, odd, padded, held, sems):
    wait = TABLES.fetch(table, held, ["into_y"], sems)
    padded[:, HALO : HALO + CY] = planes[...]
    lower = is_even("gy")
    one, two = y_even[...], y_odd[...]
    padded[:, 0:HALO] = jnp.where(lower, two, one)
    padded[:, HALO + CY : PY] = jnp.where(lower, one, two)

    into_y = wait("into_y")[:, : 3 * PY].astype(bf16)
    for z in range(0, PZ, 2):
        high, low = halves(jnp.concatenate([padded[z], padded[z + 1]], axis=1))
        wave = dot(into_y, jnp.concatenate([high, high, low], axis=0))
        waves[z], waves[z + 1] = wave[:, :128], wave[:, 128:]
    flat = waves.reshape(PZ * PY, 128)
    left, right = [], []
    for j in range(PZ * PY // 128):
        turned = flat[j * 128 : (j + 1) * 128].T
        left.append(turned[:HALO])
        right.append(turned[128 - HALO :])
    left, right = jnp.concatenate(left, axis=1), jnp.concatenate(right, axis=1)
    lower = is_even("gx")
    even[...] = jnp.where(lower, right, left)
    odd[...] = jnp.where(lower, left, right)


def sum_planes(gain, load, store):
    window = [load(z) for z in range(2 * HALO)]
    for z in range(CZ):
        window.append(load(z + 2 * HALO))
        total = gain[0] * window[HALO]
        for d in range(1, HALO + 1):
            total = total + gain[d] * (window[HALO - d] + window[HALO + d])
        store(z, total)
        window.pop(0)


def near_kernel(
    held, waves, x_even, x_odd, far, out, wave_x, tails, sums, tail_sums, field, sems
):
    get = TABLES.reader(held, NEAR)
    lower = is_even("gx")
    one, two = x_even[...], x_odd[...]
    ends = jnp.concatenate([jnp.where(lower, two, one), jnp.where(lower, one, two)], axis=0)
    high = ends.astype(bf16).astype(f32)
    ends = jnp.concatenate([high, high, ends - high], axis=0)
    weights = get("into_x")[:432].astype(bf16)
    flat, flat_x = waves.reshape(PZ * PY, 128), wave_x.reshape(PZ * PY, 128)
    tile = lane((8, 128)) // TAIL
    planes = {}
    for j in range(18):
        part = slice(j * 128, (j + 1) * 128)
        high, low = halves(flat[part])
        wave = dot(jnp.concatenate([high, high, low, ends[:, part].T.astype(bf16)], axis=1), weights)
        flat_x[part] = wave[:, :128]
        for i in range(16):
            z, t = divmod(16 * j + i, PY // 8)
            piece = wave[8 * i : 8 * i + 8, 128:]
            planes[z] = piece if t == 0 else jnp.where(tile == t, piece, planes[z])
            if t == PY // 8 - 1:
                tails[z] = planes.pop(z)

    def store_tail(z, value):
        tail_sums[z] = value

    gains, tail_gains = (TABLES.rows(held, NEAR, name) for name in ("gains", "tail_gains"))
    sum_planes([tail_gains[d * 8 : d * 8 + 8] for d in range(HALO + 1)], lambda z: tails[z], store_tail)

    @pl.loop(0, PY // 8)
    def _(c):
        row = pl.ds(pl.multiple_of(c * 8, 8), 8)

        def store(z, value):
            sums[z, row] = value

        sum_planes(
            [gains[pl.ds(pl.multiple_of(d * PY + c * 8, 8), 8)] for d in range(HALO + 1)],
            lambda z: wave_x[z, row],
            store,
        )

    to_y = get("back_y")[:, : 3 * PY].astype(bf16)
    to_x = get("back_x").astype(bf16)
    rows = []
    for z in range(CZ):
        tail = tail_sums[z]
        tail = jnp.concatenate([jnp.where(tile == t, tail, 0.0) for t in range(PY // 8)], axis=0)
        rows.append(jnp.concatenate([sums[z], tail], axis=1))
    high, low = halves(jnp.concatenate(rows, axis=0))
    both = dot(high, to_x)
    rows = both[:, :128] + both[:, 128:] + dot(low, to_x[:, :128])
    copies = []
    for z in range(0, CZ, 2):
        pair = jnp.concatenate([rows[z * PY : (z + 1) * PY], rows[(z + 1) * PY : (z + 2) * PY]], axis=1)
        high, low = halves(pair)
        cells = dot(to_y, jnp.concatenate([high, high, low], axis=0))
        field[z] = far[z] + cells[:, :128]
        field[z + 1] = far[z + 1] + cells[:, 128:]
        if z % 8 == 6:
            part = pl.ds(z - 6, 8)
            copies.append(pltpu.make_async_copy(field.at[part], out.at[part], sems.at[z // 8]))
            copies[-1].start()
    for copy in copies:
        copy.wait()


def call(kernel, outs, arrays=0, table=False, sent=0, scratch=(), us=1.0):
    vmem, hbm = pl.BlockSpec(memory_space=pltpu.VMEM), pl.BlockSpec(memory_space=pltpu.HBM)
    many = isinstance(outs, list)
    specs = [hbm] * table + [vmem] * arrays
    return pl.pallas_call(
        kernel,
        out_shape=[jax.ShapeDtypeStruct(s, f32) for s in outs] if many else jax.ShapeDtypeStruct(outs, f32),
        in_specs=specs,
        out_specs=[hbm] * sent + [vmem] * (len(outs) - sent) if many else hbm if sent else vmem,
        scratch_shapes=list(scratch),
        compiler_params=pltpu.CompilerParams(vmem_limit_bytes=VMEM_MIB * 1024 * 1024),
        cost_estimate=pl.CostEstimate(flops=int(us * 1e9), bytes_accessed=int(us * 3e6), transcendentals=0),
        name=kernel.__name__,
    )


def exchange(even, odd, axis):
    peers = lax.axis_size(axis)
    low_first = [(i, i + 1 if i % 2 == 0 else i - 1) for i in range(peers)]
    high_first = [(i, (i + 1 if i % 2 else i - 1) % peers) for i in range(peers)]
    odd = lax.ppermute(odd, axis, high_first)
    return lax.ppermute(even, axis, low_first), odd


def body(density):
    dma, vmem = pltpu.SemaphoreType.DMA, pltpu.VMEM
    table = jnp.asarray(TABLES.array)
    charges, *z_ends, first_x = call(
        charge_kernel,
        [(SHARE, 16, 128), (HALO, CY, CX), (HALO, CY, CX), (MX, 128)],
        1,
        table=True,
        sent=1,
        scratch=[vmem((4, 16, 128), f32), dma((4,)), dma((1,))],
    )(table, density)
    charges = lax.all_to_all(charges, ("gx", "core"), 0, 0, tiled=True)
    z_ends = exchange(*z_ends, ("yh", "core"))
    spectrum = call(
        first_kernel, (2 * GY, 2, 8, 128), 2, sent=1, scratch=[vmem((8, 2, 8, 128), f32), dma((4,))], us=1.3
    )(first_x, charges)
    spectrum = lax.all_to_all(spectrum, ("gy", "yh"), 0, 0, tiled=True)

    *y_ends, planes, for_filter = call(
        edge_y_kernel,
        [(PZ, HALO, CX), (PZ, HALO, CX), (PZ, CY, CX), (TABLES.height(FILTER), 128)],
        3,
        table=True,
        scratch=[dma((len(FILTER),))],
        us=10.0,
    )(table, density, *z_ends)
    spectrum, _ = lax.optimization_barrier((spectrum, y_ends))
    y_ends = exchange(*y_ends, "gy")
    spectrum = call(
        filter_kernel, (SHARE, KX, 128), 2, sent=1, scratch=[vmem((4, KX, 128), f32), dma((4,))], us=3.0
    )(for_filter, spectrum)
    y_ends, _ = lax.optimization_barrier((y_ends, spectrum))
    spectrum = lax.all_to_all(spectrum, ("gx", "core"), 0, 0, tiled=True)
    waves, even, odd = call(
        edge_x_kernel,
        [(PZ, PY, CX), (HALO, PZ * PY), (HALO, PZ * PY)],
        3,
        table=True,
        scratch=[vmem((PZ, PY, CX), f32), vmem(TABLES.shape("into_y"), f32), dma((1,))],
        us=10.0,
    )(table, planes, *y_ends)
    x_ends = exchange(even, odd, "gx")
    far, for_near = call(
        far_kernel,
        [(CZ, CY, CX), (TABLES.height(NEAR), 128)],
        1,
        table=True,
        scratch=[vmem((TABLES.height(["last_x", "last_y"]), 128), f32), dma((2,)), dma((len(NEAR),))],
        us=5.0,
    )(table, spectrum)
    return call(
        near_kernel,
        (CZ, CY, CX),
        5,
        sent=1,
        scratch=[
            vmem((PZ, PY, 128), f32),
            vmem((PZ, 8, 128), f32),
            vmem((CZ, PY, 128), f32),
            vmem((CZ, 8, 128), f32),
            vmem((CZ, CY, CX), f32),
            dma((4,)),
        ],
        us=0.1,
    )(for_near, waves, *x_ends, far)


def solution(mesh):
    devices = mesh.devices.reshape(GX, GY, 2, 2)
    parts = jax.sharding.Mesh(devices, ("gx", "gy", "yh", "core"))
    placed = P(("yh", "core"), "gy", "gx")
    return jax.shard_map(body, mesh=parts, in_specs=(placed,), out_specs=placed, check_vma=False)
```

```python
import math

import jax
import jax.numpy as jnp
import ml_dtypes
import numpy as np
from jax import lax
from jax.experimental import pallas as pl
from jax.experimental.pallas import tpu as pltpu
from jax.sharding import PartitionSpec as P

HALO = 8
COARSEN = 4
SCREEN = 6.0
SOFTEN = 0.25

NZ, NY, NX = 128, 512, 1024
GZ, GY, GX = 4, 16, 8
CZ, CY, CX = NZ // GZ, NY // GY, NX // GX
MZ, MY, MX = NZ // COARSEN, NY // COARSEN, NX // COARSEN
BZ, BY, BX = MZ // GZ, MY // GY, MX // GX
PZ, PY, PX = CZ + 2 * HALO, CY + 2 * HALO, CX + 2 * HALO
LANES = 256
BORDER = BY + 2
SHARE = 2 * GX
KX = MX // SHARE
TAIL = PX - CX
VMEM_MIB = 44
TABLE_ROWS = 24 * 2048

f32 = jnp.float32
bf16 = jnp.bfloat16
HIGHEST = lax.Precision.HIGHEST


def cas(a, b, points):
    angles = 2.0 * np.pi / points * (np.outer(a, b) % points)
    return np.cos(angles) + np.sin(angles)


def split(table):
    high = table.astype(np.float32).astype(ml_dtypes.bfloat16)
    low = (table - high.astype(np.float64)).astype(np.float32).astype(ml_dtypes.bfloat16)
    return high, low


def near_tables():
    reach = np.arange(HALO + 1)
    both = np.arange(-HALO, HALO + 1)
    squared = (
        reach[:, None, None] ** 2 + both[None, :, None] ** 2 + both[None, None, :] ** 2
    ).astype(np.float64)
    erfc = np.vectorize(math.erfc)
    kernel = erfc(np.sqrt(squared) / SCREEN) / (4.0 * math.pi * np.sqrt(squared + SOFTEN))
    cos_y = np.cos(2.0 * np.pi / PY * np.outer(np.arange(PY), both))
    cos_x = np.cos(2.0 * np.pi / PX * np.outer(np.arange(PX), both))
    spectral = np.einsum("dab,ka,lb->dkl", kernel, cos_y, cos_x) / (PY * PX)
    gains = spectral[:, :, :CX].reshape(-1, CX)
    tail_gains = np.zeros((HALO + 1, 8, 128))
    tails = spectral[:, :, CX:].reshape(HALO + 1, PY // 8, 8, TAIL).swapaxes(1, 2)
    tail_gains[:, :, : PY // 8 * TAIL] = tails.reshape(HALO + 1, 8, PY // 8 * TAIL)
    tail_gains = tail_gains.reshape(-1, 128)

    every_x, every_y = np.arange(PX), np.arange(PY)
    spread = np.r_[0:CX, np.tile(np.arange(CX, PX), 8)]
    high, low = split(cas(every_x, spread, PX))
    own = slice(HALO, HALO + CX)
    ends = np.r_[0:HALO, HALO + CX : PX]
    into_x = np.zeros((512, LANES))
    into_x[0:128], into_x[128:256], into_x[256:384] = high[own], low[own], high[own]
    into_x[384:400], into_x[400:416], into_x[416:432] = high[ends], low[ends], high[ends]

    high, low = split(cas(every_y, every_y, PY))
    inner = slice(HALO, HALO + CY)
    into_y = np.zeros((PY, LANES))
    into_y[:, : 3 * PY] = np.concatenate([high, low, high], axis=1)

    high, low = split(cas(spread, every_x[own], PX))
    back_x = np.concatenate([high, low], axis=1)
    return {
        "gains": gains,
        "tail_gains": tail_gains,
        "into_x": into_x,
        "into_y": into_y,
        "back_y": into_y[inner],
        "back_x": back_x,
    }


def far_tables():
    full_x = cas(np.arange(MX), np.arange(MX), MX)
    full_y = cas(np.arange(MY), np.arange(MY), MY)
    full_z = cas(np.arange(MZ), np.arange(MZ), MZ)

    first_x = np.tile(full_x.reshape(MX, SHARE, KX).transpose(1, 0, 2), (1, 1, 8))
    into_z = np.kron(full_z, np.eye(8))

    def waves(points):
        index = np.arange(points)
        signed = (index + points // 2) % points - points // 2
        laplace = 2.0 - 2.0 * np.cos(2.0 * np.pi / points * index)
        return laplace, (2.0 * np.pi / (points * COARSEN) * signed) ** 2

    (lap_z, wave_z), (lap_y, wave_y), (lap_x, wave_x) = waves(MZ), waves(MY), waves(MX)
    laplace = lap_z[:, None, None] + lap_y[None, :, None] + lap_x[None, None, :]
    wave = wave_z[:, None, None] + wave_y[None, :, None] + wave_x[None, None, :]
    laplace[0, 0, 0] = 1.0
    gain = np.exp(-(SCREEN * SCREEN / 4.0) * wave) / (COARSEN * laplace)
    gain[0, 0, 0] = 0.0
    gain = gain / (MZ * MY * MX)
    gain = gain.reshape(MZ, MY, SHARE, 2, 8).transpose(2, 0, 4, 3, 1).reshape(SHARE, MZ * 8, 2 * MY)

    out_z = np.zeros((2, 2 * BORDER * 8, MZ * 8))
    for g in range(2):
        z = np.concatenate([(2 * g + c) * BZ - 1 + np.arange(BORDER) for c in range(2)]) % MZ
        out_z[g] = np.kron(full_z[z], np.eye(8))

    out_y = np.zeros((GY, MY, 128))
    for g in range(GY):
        out_y[g, :, :BORDER] = full_y[:, (g * BY - 1 + np.arange(BORDER)) % MY]

    def refine(coarse):
        matrix = np.zeros((COARSEN * coarse, coarse + 2))
        for fine in range(COARSEN * coarse):
            below, t = fine // COARSEN, (fine % COARSEN + 0.5) / COARSEN - 0.5
            matrix[fine, below + 1] = 1.0 - abs(t)
            matrix[fine, below if t < 0 else below + 2] = abs(t)
        return matrix

    last_x = np.zeros((GX, MX, CX))
    for g in range(GX):
        last_x[g] = full_x[:, (g * BX - 1 + np.arange(BX + 2)) % MX] @ refine(BX).T
    last_y = np.zeros((BORDER * CY, 128))
    last_y[:, : BORDER * BORDER] = np.kron(np.eye(BORDER), refine(BY))
    return {
        "first_x": first_x,
        "full_y": full_y,
        "into_z": into_z,
        "gain": gain,
        "out_z": out_z,
        "out_y": out_y,
        "last_x": last_x,
        "last_y": last_y,
    }


class Tables:
    def __init__(self):
        self.place, rows, pieces = {}, 0, []
        for name, table in (near_tables() | far_tables()).items():
            count, lanes = table.shape[-2:]
            halves = lanes // 128
            flat = table.reshape(-1, count, halves, 128).swapaxes(1, 2).reshape(-1, 128)
            self.place[name] = rows, count, halves
            rows += flat.shape[0]
            pieces.append(flat)
        self.array = np.zeros((TABLE_ROWS, 128), np.float32)
        self.array[:rows] = np.concatenate(pieces)

    def shape(self, name):
        _, count, halves = self.place[name]
        return halves * count, 128

    def copy(self, ref, name, held, sem, part=None):
        first, count, halves = self.place[name]
        rows = halves * count
        start = first if part is None else pl.multiple_of(first + part * rows, 8)
        return pltpu.make_async_copy(ref.at[pl.ds(start, rows)], held, sem)

    def height(self, names):
        return sum(self.shape(name)[0] for name in names)

    def rows(self, held, names, name):
        return held.at[pl.ds(self.height(names[: names.index(name)]), self.shape(name)[0])]

    def reader(self, held, names):
        def get(name):
            _, count, halves = self.place[name]
            rows = self.rows(held, names, name)
            if halves == 1:
                return rows[...]
            return jnp.concatenate([rows[0:count], rows[count : 2 * count]], axis=1)

        return get

    def fetch(self, ref, held, names, sems, part={}):
        copies = {
            name: self.copy(ref, name, self.rows(held, names, name), sems.at[i], part.get(name))
            for i, name in enumerate(names)
        }
        for copy in copies.values():
            copy.start()
        get = self.reader(held, names)

        def wait(name):
            copies[name].wait()
            return get(name)

        return wait


LAST = ["last_x", "last_y"]
FILTER = ["full_y", "into_z", "gain", "out_z", "out_y"]
NEAR = ["gains", "tail_gains", "into_x", "back_y", "back_x"]
TABLES = Tables()


def dot(a, b):
    return jnp.dot(a, b, preferred_element_type=f32)


def exact_dot(a, b):
    return jnp.dot(a, b, preferred_element_type=f32, precision=HIGHEST)


def halves(x):
    high = x.astype(bf16)
    return high, (x - high.astype(f32)).astype(bf16)


def close_dot(a, b):
    (a, a_low), (b, b_low) = halves(a), halves(b)
    return dot(a, b) + (dot(a, b_low) + dot(a_low, b))


def lane(shape):
    return lax.broadcasted_iota(jnp.int32, shape, len(shape) - 1)


def transposed_dot(a, b):
    return lax.dot_general(a, b, (((0,), (0,)), ((), ())), preferred_element_type=f32, precision=HIGHEST)


def share():
    return lax.axis_index("gx") * 2 + lax.axis_index("core")


def is_even(axis):
    return lax.rem(lax.axis_index(axis), 2) == 0


def send(held, out, sems):
    count = held.shape[0]
    copies = [
        pltpu.make_async_copy(held, out.at[pl.ds(i * count, count)], sems.at[i])
        for i in range(out.shape[0] // count)
    ]
    for copy in copies:
        copy.start()

    def wait():
        for copy in copies:
            copy.wait()

    return wait


def charge_kernel(table, density, out, even, odd, first_x, message, sems, more):
    wait_first = TABLES.fetch(table, first_x, ["first_x"], more, {"first_x": share()})
    parts = []
    for high in range(2):
        planes = []
        for low in range(4):
            z = (high * 4 + low) * COARSEN
            planes.append((density[z] + density[z + 1]) + (density[z + 2] + density[z + 3]))
        parts.append(jnp.concatenate(planes, axis=1))
    rows = jnp.concatenate(parts, axis=0)

    def pool(shape, fine, coarse):
        a = lax.broadcasted_iota(jnp.int32, shape, fine)
        b = lax.broadcasted_iota(jnp.int32, shape, coarse)
        return (a // COARSEN == b).astype(f32)

    rows = exact_dot(rows, pool((4 * CX, 128), 0, 1))
    rows = exact_dot(pool((2 * BY, 2 * CY), 1, 0), rows)
    for copy in range(4):
        message[copy] = rows
    wait = send(message, out, sems)
    start = jnp.where(is_even("core"), CZ - HALO, 0)
    even[...] = density[pl.ds(start, HALO)]
    odd[...] = density[pl.ds(CZ - HALO - start, HALO)]
    wait_first("first_x")
    wait()


def first_kernel(first_x, charges, out, message, sems):
    peers = charges[...].reshape(GX, 32, 128)
    place = lane((32, 128)) // BX
    blocks = []
    for low in range(4):
        sides = []
        for side in range(2):
            total = None
            for q in range(4):
                shift = (q - low) * BX % 128
                peer = peers[side * 4 + q]
                moved = pltpu.roll(peer, shift, 1) if shift else peer
                total = moved if q == 0 else jnp.where(place == q, moved, total)
            sides.append(total)
        blocks.append(jnp.concatenate(sides, axis=1))
    rows = jnp.concatenate(blocks, axis=0)
    rows = exact_dot(rows, first_x[...])
    place = lane((BY, 128)) // KX
    for core in range(2):
        total = None
        for z in range(BZ):
            start = (z % 4) * 32 + core * 16 + (z // 4) * 8
            piece = rows[start : start + 8]
            total = piece if z == 0 else jnp.where(place == z, piece, total)
        for copy in range(8):
            message[copy, core] = total
    send(message, out, sems)()


def filter_kernel(table, held, spectrum, out, for_far, message, sems, sems_far):
    wait_far = TABLES.fetch(table, for_far, LAST, sems_far, {"last_x": lax.axis_index("gx")})
    blocks = spectrum[...].reshape(GY, 4, BY, 128)
    get = TABLES.reader(held, FILTER)
    full_y = get("full_y")
    waves = [transposed_dot(blocks[:, b].reshape(MY, 128), full_y) for b in range(4)]
    rows = jnp.concatenate(waves, axis=0).reshape(MZ, 2, 8, MY)
    rows = jnp.concatenate([rows[:, half].reshape(MZ * 8, MY) for half in range(2)], axis=1)
    rows = exact_dot(get("into_z"), rows)
    rows = rows * get("gain")
    rows = close_dot(get("out_z"), rows)
    rows = jnp.concatenate([rows[:, :MY], rows[:, MY:]], axis=0)
    rows = close_dot(rows, get("out_y"))
    for core in range(2):
        sides = []
        for half in range(2):
            total = None
            for z in range(BORDER):
                start = ((half * 2 + core) * BORDER + z) * 8
                piece = rows[start : start + 8]
                total = piece if z == 0 else total + pltpu.roll(piece, z * BORDER, 1)
            sides.append(total)
        rows_out = jnp.concatenate(sides, axis=0)
        for copy in range(2):
            message[copy * 2 + core] = rows_out
    wait_out = send(message, out, sems)
    for name in LAST:
        wait_far(name)
    wait_out()


def far_kernel(table, held, spectrum, out, for_near, more):
    get = TABLES.reader(held, LAST)
    wait_near = TABLES.fetch(table, for_near, NEAR, more)
    rows = spectrum[...].reshape(MX, 128)
    field = close_dot(rows.T, get("last_x"))
    high, low = halves(field)
    refine = get("last_y").astype(bf16)
    field = dot(refine, high) + dot(refine, low)

    def plane(z):
        return field[z * CY : (z + 1) * CY]

    for block in range(BZ):
        before, here, after = plane(block), plane(block + 1), plane(block + 2)
        for residue in range(COARSEN):
            t = (residue + 0.5) / COARSEN - 0.5
            value = (1.0 - abs(t)) * here + abs(t) * (before if t < 0 else after)
            z = block * COARSEN + residue
            out[z] = value
    for name in NEAR:
        wait_near(name)


def edge_y_kernel(table, density, z_even, z_odd, even, odd, planes, for_filter, sems):
    part = {"gain": share(), "out_z": lax.axis_index("yh"), "out_y": lax.axis_index("gy")}
    wait = TABLES.fetch(table, for_filter, FILTER, sems, part)
    lower = is_even("core")
    one, two = z_even[...], z_odd[...]
    planes[0:HALO] = jnp.where(lower, two, one)
    planes[HALO : HALO + CZ] = density[...]
    planes[HALO + CZ : PZ] = jnp.where(lower, one, two)
    start = jnp.where(is_even("gy"), CY - HALO, 0)
    even[...] = planes[:, pl.ds(pl.multiple_of(start, 8), HALO)]
    odd[...] = planes[:, pl.ds(pl.multiple_of(CY - HALO - start, 8), HALO)]
    for name in FILTER:
        wait(name)


def edge_x_kernel(table, planes, y_even, y_odd, waves, even, odd, padded, held, sems):
    wait = TABLES.fetch(table, held, ["into_y"], sems)
    padded[:, HALO : HALO + CY] = planes[...]
    lower = is_even("gy")
    one, two = y_even[...], y_odd[...]
    padded[:, 0:HALO] = jnp.where(lower, two, one)
    padded[:, HALO + CY : PY] = jnp.where(lower, one, two)

    into_y = wait("into_y")[:, : 3 * PY].astype(bf16)
    for z in range(0, PZ, 2):
        high, low = halves(jnp.concatenate([padded[z], padded[z + 1]], axis=1))
        wave = dot(into_y, jnp.concatenate([high, high, low], axis=0))
        waves[z], waves[z + 1] = wave[:, :128], wave[:, 128:]
    flat = waves.reshape(PZ * PY, 128)
    left, right = [], []
    for j in range(PZ * PY // 128):
        turned = flat[j * 128 : (j + 1) * 128].T
        left.append(turned[:HALO])
        right.append(turned[128 - HALO :])
    left, right = jnp.concatenate(left, axis=1), jnp.concatenate(right, axis=1)
    lower = is_even("gx")
    even[...] = jnp.where(lower, right, left)
    odd[...] = jnp.where(lower, left, right)


def sum_planes(gain, load, store):
    window = [load(z) for z in range(2 * HALO)]
    for z in range(CZ):
        window.append(load(z + 2 * HALO))
        total = gain[0] * window[HALO]
        for d in range(1, HALO + 1):
            total = total + gain[d] * (window[HALO - d] + window[HALO + d])
        store(z, total)
        window.pop(0)


def near_kernel(
    held, waves, x_even, x_odd, far, out, wave_x, tails, sums, tail_sums, field, sems
):
    get = TABLES.reader(held, NEAR)
    lower = is_even("gx")
    one, two = x_even[...], x_odd[...]
    ends = jnp.concatenate([jnp.where(lower, two, one), jnp.where(lower, one, two)], axis=0)
    high = ends.astype(bf16).astype(f32)
    ends = jnp.concatenate([high, high, ends - high], axis=0)
    weights = get("into_x")[:432].astype(bf16)
    flat, flat_x = waves.reshape(PZ * PY, 128), wave_x.reshape(PZ * PY, 128)
    tile = lane((8, 128)) // TAIL
    planes = {}
    for j in range(18):
        part = slice(j * 128, (j + 1) * 128)
        high, low = halves(flat[part])
        wave = dot(jnp.concatenate([high, high, low, ends[:, part].T.astype(bf16)], axis=1), weights)
        flat_x[part] = wave[:, :128]
        for i in range(16):
            z, t = divmod(16 * j + i, PY // 8)
            piece = wave[8 * i : 8 * i + 8, 128:]
            planes[z] = piece if t == 0 else jnp.where(tile == t, piece, planes[z])
            if t == PY // 8 - 1:
                tails[z] = planes.pop(z)

    def store_tail(z, value):
        tail_sums[z] = value

    gains, tail_gains = (TABLES.rows(held, NEAR, name) for name in ("gains", "tail_gains"))
    sum_planes([tail_gains[d * 8 : d * 8 + 8] for d in range(HALO + 1)], lambda z: tails[z], store_tail)

    @pl.loop(0, PY // 8)
    def _(c):
        row = pl.ds(pl.multiple_of(c * 8, 8), 8)

        def store(z, value):
            sums[z, row] = value

        sum_planes(
            [gains[pl.ds(pl.multiple_of(d * PY + c * 8, 8), 8)] for d in range(HALO + 1)],
            lambda z: wave_x[z, row],
            store,
        )

    to_y = get("back_y")[:, : 3 * PY].astype(bf16)
    to_x = get("back_x").astype(bf16)
    rows = []
    for z in range(CZ):
        tail = tail_sums[z]
        tail = jnp.concatenate([jnp.where(tile == t, tail, 0.0) for t in range(PY // 8)], axis=0)
        rows.append(jnp.concatenate([sums[z], tail], axis=1))
    high, low = halves(jnp.concatenate(rows, axis=0))
    both = dot(high, to_x)
    rows = both[:, :128] + both[:, 128:] + dot(low, to_x[:, :128])
    copies = []
    for z in range(0, CZ, 2):
        pair = jnp.concatenate([rows[z * PY : (z + 1) * PY], rows[(z + 1) * PY : (z + 2) * PY]], axis=1)
        high, low = halves(pair)
        cells = dot(to_y, jnp.concatenate([high, high, low], axis=0))
        field[z] = far[z] + cells[:, :128]
        field[z + 1] = far[z + 1] + cells[:, 128:]
        if z % 8 == 6:
            part = pl.ds(z - 6, 8)
            copies.append(pltpu.make_async_copy(field.at[part], out.at[part], sems.at[z // 8]))
            copies[-1].start()
    for copy in copies:
        copy.wait()


def call(kernel, outs, arrays=0, table=False, sent=0, scratch=(), us=1.0):
    vmem, hbm = pl.BlockSpec(memory_space=pltpu.VMEM), pl.BlockSpec(memory_space=pltpu.HBM)
    many = isinstance(outs, list)
    specs = [hbm] * table + [vmem] * arrays
    return pl.pallas_call(
        kernel,
        out_shape=[jax.ShapeDtypeStruct(s, f32) for s in outs] if many else jax.ShapeDtypeStruct(outs, f32),
        in_specs=specs,
        out_specs=[hbm] * sent + [vmem] * (len(outs) - sent) if many else hbm if sent else vmem,
        scratch_shapes=list(scratch),
        compiler_params=pltpu.CompilerParams(vmem_limit_bytes=VMEM_MIB * 1024 * 1024),
        cost_estimate=pl.CostEstimate(flops=int(us * 1e9), bytes_accessed=int(us * 3e6), transcendentals=0),
        name=kernel.__name__,
    )


def exchange(even, odd, axis):
    peers = lax.axis_size(axis)
    low_first = [(i, i + 1 if i % 2 == 0 else i - 1) for i in range(peers)]
    high_first = [(i, (i + 1 if i % 2 else i - 1) % peers) for i in range(peers)]
    odd = lax.ppermute(odd, axis, high_first)
    return lax.ppermute(even, axis, low_first), odd


def body(density):
    dma, vmem = pltpu.SemaphoreType.DMA, pltpu.VMEM
    table = jnp.asarray(TABLES.array)
    charges, *z_ends, first_x = call(
        charge_kernel,
        [(SHARE, 16, 128), (HALO, CY, CX), (HALO, CY, CX), (MX, 128)],
        1,
        table=True,
        sent=1,
        scratch=[vmem((4, 16, 128), f32), dma((4,)), dma((1,))],
    )(table, density)
    charges = lax.all_to_all(charges, ("gx", "core"), 0, 0, tiled=True)
    z_ends = exchange(*z_ends, ("yh", "core"))
    spectrum = call(
        first_kernel, (2 * GY, 2, 8, 128), 2, sent=1, scratch=[vmem((8, 2, 8, 128), f32), dma((4,))], us=1.3
    )(first_x, charges)
    spectrum = lax.all_to_all(spectrum, ("gy", "yh"), 0, 0, tiled=True)

    *y_ends, planes, for_filter = call(
        edge_y_kernel,
        [(PZ, HALO, CX), (PZ, HALO, CX), (PZ, CY, CX), (TABLES.height(FILTER), 128)],
        3,
        table=True,
        scratch=[dma((len(FILTER),))],
        us=10.0,
    )(table, density, *z_ends)
    spectrum, _ = lax.optimization_barrier((spectrum, y_ends))
    y_ends = exchange(*y_ends, "gy")
    spectrum, for_far = call(
        filter_kernel,
        [(SHARE, KX, 128), (TABLES.height(LAST), 128)],
        2,
        table=True,
        sent=1,
        scratch=[vmem((4, KX, 128), f32), dma((4,)), dma((len(LAST),))],
        us=3.0,
    )(table, for_filter, spectrum)
    y_ends, _ = lax.optimization_barrier((y_ends, spectrum))
    spectrum = lax.all_to_all(spectrum, ("gx", "core"), 0, 0, tiled=True)
    waves, even, odd = call(
        edge_x_kernel,
        [(PZ, PY, CX), (HALO, PZ * PY), (HALO, PZ * PY)],
        3,
        table=True,
        scratch=[vmem((PZ, PY, CX), f32), vmem(TABLES.shape("into_y"), f32), dma((1,))],
        us=10.0,
    )(table, planes, *y_ends)
    x_ends = exchange(even, odd, "gx")
    far, for_near = call(
        far_kernel,
        [(CZ, CY, CX), (TABLES.height(NEAR), 128)],
        2,
        table=True,
        scratch=[dma((len(NEAR),))],
        us=5.0,
    )(table, for_far, spectrum)
    return call(
        near_kernel,
        (CZ, CY, CX),
        5,
        sent=1,
        scratch=[
            vmem((PZ, PY, 128), f32),
            vmem((PZ, 8, 128), f32),
            vmem((CZ, PY, 128), f32),
            vmem((CZ, 8, 128), f32),
            vmem((CZ, CY, CX), f32),
            dma((4,)),
        ],
        us=0.1,
    )(for_near, waves, *x_ends, far)


def solution(mesh):
    devices = mesh.devices.reshape(GX, GY, 2, 2)
    parts = jax.sharding.Mesh(devices, ("gx", "gy", "yh", "core"))
    placed = P(("yh", "core"), "gy", "gx")
    return jax.shard_map(body, mesh=parts, in_specs=(placed,), out_specs=placed, check_vma=False)
```
